32 devices in a mesh: dp: 8 (over y, x, core), mp: 4 (over z).
Axes of the slice: x: 2, y: 2, z: 4, core: 2. Of those that a mesh axis runs over, the one named last changes fastest.
Arguments:
- byte_in: float32 [32, 2048, 768], P('dp', 'mp'), may hold values from -6 to 6
- latents: float32 [32, 256, 1280], P('dp', 'mp'), may hold values from -6 to 6
- cotangent: float32 [32, 256, 1280], P('dp', 'mp'), may hold values from -6 to 6
- byte_gain: float32 [768], replicated, may hold values from 0.5 to 1.5
- latent_gain: float32 [1280], replicated, may hold values from 0.5 to 1.5
- mlp_gain: float32 [1280], replicated, may hold values from 0.5 to 1.5
- w_query: bfloat16 [1280, 1280], P(None, 'mp'), may hold values from -0.15625 to 0.15625
- w_key: bfloat16 [768, 1280], P(None, 'mp'), may hold values from -0.21875 to 0.21875
- w_value: bfloat16 [768, 1280], P(None, 'mp'), may hold values from -0.21875 to 0.21875
- w_out: bfloat16 [1280, 1280], P('mp'), may hold values from -4 to 4
- b_out: float32 [1280], replicated, may hold values from -3 to 3
- w_up: bfloat16 [1280, 1280], P(None, 'mp'), may hold values from -0.15625 to 0.15625
- b_up: float32 [1280], P('mp'), may hold values from -3 to 3
- w_down: bfloat16 [1280, 1280], P('mp'), may hold values from -0.15625 to 0.15625
- b_down: float32 [1280], replicated, may hold values from -3 to 3
- byte_seg: int32 [32, 2048], P('dp'), may hold values from 0 to 2, as said below
- byte_pad: int32 [32, 2048], P('dp'), may hold values from 0 to 1, as said below
- latent_seg: int32 [32, 256], P('dp'), may hold values from 0 to 2, as said below
Outputs:
- latents_out: float32 [32, 256, 1280], P('dp', 'mp')
- grad_bytes: float32 [32, 2048, 768], P('dp', 'mp')
- grad_latents: float32 [32, 256, 1280], P('dp', 'mp')
- grad_byte_gain: float32 [768], replicated
- grad_latent_gain: float32 [1280], replicated
- grad_mlp_gain: float32 [1280], replicated
- grad_w_query: float32 [1280, 1280], P(None, 'mp')
- grad_w_key: float32 [768, 1280], P(None, 'mp')
- grad_w_value: float32 [768, 1280], P(None, 'mp')
- grad_w_out: float32 [1280, 1280], P('mp')
- grad_b_out: float32 [1280], replicated
- grad_w_up: float32 [1280, 1280], P(None, 'mp')
- grad_b_up: float32 [1280], P('mp')
- grad_w_down: float32 [1280, 1280], P('mp')
- grad_b_down: float32 [1280], replicated
The draws below stay inside these ranges and needn't reach their ends.
Inputs may be any that keep to these rules, and one draw needn't show every extreme that they name: `byte_seg`: each packed row holds three documents in order, each with bytes and latents; one of them, drawn from the seed, covers all but fewer than 256 of the row's bytes. `byte_pad`: padding is a tail of each row, at least one byte long and shorter than the row's last document. `latent_seg`: latents follow the documents of their row in order, every document has one or more latents.
All inputs are finite; a program needn't handle non-finite values.
Results may differ from the reference program's by a relative error of at most 0.015.
Values may be sent and summed in bfloat16 or wider, within the bound.
No kernel may reach another device: no remote copies, remote signals or barrier semaphores. Data moves between devices by JAX's collectives and lax.ppermute only.
A program may use at most 192 MiB of HBM per device.

```python
import jax
import jax.numpy as jnp
from jax import lax

D_BYTE = 768
D_LAT = 1280
HEADS = 8
MLP = 1280
LAT = 256
BYTES = 2048
HEAD_DIM = 160
ROWS = 32


def document_counts(key_long, key_short, total, short_top):
    doc_slots = jnp.arange(3)[None, :]
    long_doc = jax.random.randint(key_long, (ROWS, 1), 0, 3)
    short_sizes = jax.random.randint(key_short, (ROWS, 3), 2, short_top)
    short_sizes = jnp.where(doc_slots == long_doc, 0, short_sizes)
    return jnp.where(doc_slots == long_doc, total - jnp.sum(short_sizes, 1, keepdims=True), short_sizes)


def ids_from_counts(counts, total):
    doc_ends = jnp.cumsum(counts, 1)
    positions = jnp.arange(total)[None, :, None]
    return jnp.sum((positions >= doc_ends[:, None, :2]).astype(jnp.int32), -1)


def document_layout(key):
    key_long, key_short, key_tail, key_latent = jax.random.split(key, 4)
    byte_counts = document_counts(key_long, key_short, BYTES, BYTES // 16)
    byte_ids = ids_from_counts(byte_counts, BYTES)
    tail_limit = jnp.minimum(byte_counts[:, 2], BYTES // 32 + 1)
    tail_pads = jax.random.randint(key_tail, (ROWS,), 1, tail_limit)
    pad_flags = (jnp.arange(BYTES)[None, :] < BYTES - tail_pads[:, None]).astype(jnp.int32)
    lat_counts = document_counts(key_long, key_latent, LAT, LAT // 4 + 1)
    lat_ids = ids_from_counts(lat_counts, LAT)
    return (byte_ids, pad_flags, lat_ids)


def draw_byte_seg(key, part):
    shared = document_layout(key)
    return shared[0]


def draw_byte_pad(key, part):
    shared = document_layout(key)
    return shared[1]


def draw_latent_seg(key, part):
    shared = document_layout(key)
    return shared[2]


def block_scale(stream_key, shape, cuts, least, top_value):
    factor_of = 1.0
    for dim, parts in cuts:
        heights = jax.random.uniform(jax.random.fold_in(jax.random.fold_in(stream_key, 6), dim), (parts,), jnp.float32, least / len(cuts), top_value / len(cuts))
        factor_of = factor_of * jnp.repeat(jnp.exp(heights), shape[dim] // parts).reshape((-1,) + (1,) * (len(shape) - 1 - dim))
    return factor_of


def scatter_about(rng, shape, spread, bound, shards=(), kind=jnp.bfloat16):
    loudness = block_scale(rng, shape, shards, -0.22, 0.18) if shards else 1.0
    values = jax.random.normal(rng, shape, jnp.float32) * spread * loudness
    return jnp.minimum(jnp.maximum(values, -bound), bound).astype(kind)


def setup_inputs(seed: int = 0) -> dict:
    key_list = jax.random.split(jax.random.key(seed), 19)
    return {
        "byte_in": scatter_about(key_list[0], (ROWS, BYTES, D_BYTE), 1.0, 6.0, ((0, 8), (1, 4)), jnp.float32),
        "latents": scatter_about(key_list[1], (ROWS, LAT, D_LAT), 1.0, 6.0, ((0, 8), (1, 4)), jnp.float32),
        "cotangent": scatter_about(key_list[2], (ROWS, LAT, D_LAT), 1.0, 6.0, ((0, 8), (1, 4)), jnp.float32),
        "byte_gain": jnp.clip(1.0 + 0.1 * jax.random.normal(key_list[3], (D_BYTE,), jnp.float32), 0.5, 1.5),
        "latent_gain": jnp.clip(1.0 + 0.1 * jax.random.normal(key_list[4], (D_LAT,), jnp.float32), 0.5, 1.5),
        "mlp_gain": jnp.clip(1.0 + 0.1 * jax.random.normal(key_list[5], (D_LAT,), jnp.float32), 0.5, 1.5),
        "w_query": scatter_about(key_list[6], (D_LAT, D_LAT), D_LAT ** -0.5, 0.15625, ((1, 4),)),
        "w_key": scatter_about(key_list[7], (D_BYTE, D_LAT), D_BYTE ** -0.5, 0.21875, ((1, 4),)),
        "w_value": scatter_about(key_list[8], (D_BYTE, D_LAT), D_BYTE ** -0.5, 0.21875, ((1, 4),)),
        "w_out": scatter_about(key_list[9], (D_LAT, D_LAT), (max(1, D_LAT * 4 // BYTES)) ** -0.5, 4.0, ((0, 4),)),
        "b_out": scatter_about(key_list[10], (D_LAT,), 0.5, 3.0, (), jnp.float32),
        "w_up": scatter_about(key_list[11], (D_LAT, MLP), D_LAT ** -0.5, 0.15625, ((1, 4),)),
        "b_up": scatter_about(key_list[12], (MLP,), 0.5, 3.0, ((0, 4),), jnp.float32),
        "w_down": scatter_about(key_list[13], (MLP, D_LAT), MLP ** -0.5, 0.15625, ((0, 4),)),
        "b_down": scatter_about(key_list[14], (D_LAT,), 0.5, 3.0, (), jnp.float32),
        "byte_seg": draw_byte_seg(jax.random.fold_in(key_list[18], 71), 0),
        "byte_pad": draw_byte_pad(jax.random.fold_in(key_list[18], 71), 0),
        "latent_seg": draw_latent_seg(jax.random.fold_in(key_list[18], 71), 0),
    }


EPS = 1e-05

@jax.custom_vjp
def low(v):
    return lax.optimization_barrier(v.astype(jnp.bfloat16)).astype(jnp.float32)

@jax.custom_vjp
def low_back(v):
    return v

def low_keep(v):
    return (low(v), None)

def low_pass(kept, grad):
    return (grad,)

def back_keep(v):
    return (v, None)

def back_low(kept, grad):
    return (low(grad),)
low.defvjp(low_keep, low_pass)
low_back.defvjp(back_keep, back_low)

def normalize(field, scale_vec):
    average = lax.optimization_barrier(jnp.mean(field, -1, keepdims=True))
    centred = field - average
    return centred * lax.rsqrt(lax.optimization_barrier(jnp.mean(centred * centred, -1, keepdims=True)) + EPS) * scale_vec

def dense(operand, matrix):
    return jnp.dot(operand, matrix, precision=lax.Precision.HIGHEST, preferred_element_type=jnp.float32)

def encoder_row(byte_row, lat_row, byte_gain, latent_gain, mlp_gain, w_query, w_key, w_value, w_out, b_out, w_up, b_up, w_down, b_down, byte_ids, pad_flags, lat_ids):
    score_scale = HEAD_DIM ** (-0.5)
    byte_norm = low(normalize(byte_row, byte_gain))
    lat_norm = low(normalize(lat_row, latent_gain))
    queries = low_back(low(dense(lat_norm, w_query) * score_scale)).reshape(LAT, HEADS, HEAD_DIM)
    key_proj = low_back(low(dense(byte_norm, w_key))).reshape(BYTES, HEADS, HEAD_DIM)
    value_proj = low_back(low(dense(byte_norm, w_value))).reshape(BYTES, HEADS, HEAD_DIM)
    raw_scores = low_back(jnp.einsum('lhd,shd->hls', queries, key_proj, precision=lax.Precision.HIGHEST))
    allowed = (lat_ids[:, None] == byte_ids[None, :]) & (pad_flags[None, :] == 1)
    scores = jnp.where(allowed[None], raw_scores, -1e+30)
    row_peak = lax.optimization_barrier(jnp.max(scores, -1, keepdims=True))
    exp_scores = jnp.exp(scores - row_peak)
    attn_probs = exp_scores / lax.optimization_barrier(jnp.sum(exp_scores, -1, keepdims=True))
    attended = jnp.einsum('hls,shd->lhd', low(attn_probs), value_proj, precision=lax.Precision.HIGHEST)
    attended = low_back(low(attended)).reshape(LAT, D_LAT)
    hidden = lat_row + low_back(dense(attended, w_out)) + b_out
    mid_norm = low(normalize(hidden, mlp_gain))
    pre_act = low_back(dense(mid_norm, w_up) + b_up)
    activated = low(jax.nn.gelu(pre_act, approximate=False))
    return hidden + low_back(dense(activated, w_down)) + b_down

def reference(byte_in, latents, cotangent, byte_gain, latent_gain, mlp_gain, w_query, w_key, w_value, w_out, b_out, w_up, b_up, w_down, b_down, byte_seg, byte_pad, latent_seg):
    params = tuple((item.astype(jnp.float32) for item in (byte_gain, latent_gain, mlp_gain, w_query, w_key, w_value, w_out, b_out, w_up, b_up, w_down, b_down)))

    def step(totals, row_data):
        byte_row, lat_row, grad_row, byte_ids, pad_flags, lat_ids = row_data

        def row_fn(byte_arg, lat_arg, *weights):
            return encoder_row(byte_arg, lat_arg, *weights, byte_ids, pad_flags, lat_ids)
        output, pullback = jax.vjp(row_fn, byte_row, lat_row, *params)
        grads = pullback(grad_row)
        totals = tuple((total + grad for total, grad in zip(totals, grads[2:])))
        return (totals, (output, grads[0], grads[1]))
    start = tuple((jnp.zeros_like(item) for item in params))
    totals, (result, grad_bytes, grad_latents) = lax.scan(step, start, (byte_in, latents, cotangent, byte_seg, byte_pad, latent_seg))
    return (result, grad_bytes, grad_latents, totals[0], totals[1], totals[2], totals[3], totals[4], totals[5], totals[6], totals[7], totals[8], totals[9], totals[10], totals[11])
```

```python
import functools

import jax
import jax.numpy as jnp
from jax import lax
from jax.experimental import pallas as pl
from jax.experimental.pallas import tpu as pltpu
from jax.sharding import PartitionSpec as P

HEAD_DIM = 160
EPS = 1e-05
NEG = -1e30
LANES = 128
F32 = jnp.float32
BF16 = jnp.bfloat16
NN = (((1,), (0,)), ((), ()))
NT = (((1,), (1,)), ((), ()))
TN = (((0,), (0,)), ((), ()))


def dot(a, b, dims=NN):
    return lax.dot_general(a, b, dims, preferred_element_type=F32)


def normalize(field):
    average = jnp.mean(field, -1, keepdims=True)
    centred = field - average
    inv_scale = lax.rsqrt(jnp.mean(centred * centred, -1, keepdims=True) + EPS)
    return (centred * inv_scale, inv_scale)


def norm_back(grad_out, normed, inv_scale, scale_vec):
    weighted = grad_out * scale_vec
    centred_grad = (
        weighted
        - jnp.mean(weighted, -1, keepdims=True)
        - normed * jnp.mean(weighted * normed, -1, keepdims=True)
    )
    return (inv_scale * centred_grad, jnp.sum(grad_out * normed, axis=0))


def gelu_exact(field):
    return jax.nn.gelu(field, approximate=False)


def windows(columns):
    out = []
    for head in range(columns // HEAD_DIM):
        start = head * HEAD_DIM
        base = start // LANES * LANES
        assert start + HEAD_DIM <= base + 2 * LANES
        out.append((base, start - base, start - base + HEAD_DIM))
    return out


def own_columns(shape, low, high):
    lane = lax.broadcasted_iota(jnp.int32, shape, 1)
    return (lane >= low) & (lane < high)


def lse_kernel(query_ref, key_ref, lat_seg_ref, byte_seg_ref, lse_ref):
    allowed = byte_seg_ref[0] == lat_seg_ref[0]
    for head, (base, low, high) in enumerate(windows(query_ref.shape[2])):
        query = query_ref[0, :, base : base + 2 * LANES]
        query = jnp.where(own_columns(query.shape, low, high), query, 0)
        key = key_ref[0, :, base : base + 2 * LANES]
        scores = jnp.where(allowed, dot(key, query, NT), NEG)
        peak = jnp.max(scores, 0, keepdims=True)
        total = jnp.sum(jnp.exp(scores - peak), 0, keepdims=True)
        lse_ref[0, head : head + 1, :] = peak + jnp.log(total)


class Tiles:
    def __init__(self, ref):
        self.ref = ref
        self.held = {}

    def add(self, base, window):
        for part in range(2):
            tile = base + part * LANES
            piece = window[:, part * LANES : (part + 1) * LANES]
            self.held[tile] = self.held[tile] + piece if tile in self.held else piece
        for tile in [t for t in self.held if t < base]:
            self.store(tile)

    def store(self, tile):
        self.ref[0, :, tile : tile + LANES] = self.held.pop(tile).astype(self.ref.dtype)

    def finish(self):
        for tile in list(self.held):
            self.store(tile)


def attend_kernel(query_ref, key_ref, value_ref, lat_seg_ref, byte_seg_ref, lse_ref, out_ref):
    allowed = lat_seg_ref[0] == byte_seg_ref[0]
    tiles = Tiles(out_ref)
    for head, (base, low, high) in enumerate(windows(query_ref.shape[2])):
        query = query_ref[0, :, base : base + 2 * LANES]
        mine = own_columns(query.shape, low, high)
        query = jnp.where(mine, query, 0)
        key = key_ref[0, :, base : base + 2 * LANES]
        value = value_ref[0, :, base : base + 2 * LANES]
        scores = jnp.where(allowed, dot(query, key, NT), NEG)
        probs = jnp.exp(scores - lse_ref[0, :, head : head + 1]).astype(BF16)
        tiles.add(base, jnp.where(mine, dot(probs, value), 0.0))
    tiles.finish()


def attend_back_kernel(
    query_ref,
    key_ref,
    value_ref,
    grad_ref,
    lat_seg_ref,
    byte_seg_ref,
    lse_ref,
    delta_ref,
    grad_query_ref,
    grad_key_ref,
    grad_value_ref,
):
    allowed = byte_seg_ref[0] == lat_seg_ref[0]
    query_tiles, key_tiles, value_tiles = (
        Tiles(grad_query_ref),
        Tiles(grad_key_ref),
        Tiles(grad_value_ref),
    )
    for head, (base, low, high) in enumerate(windows(query_ref.shape[2])):
        query = query_ref[0, :, base : base + 2 * LANES]
        mine = own_columns(query.shape, low, high)
        query = jnp.where(mine, query, 0)
        grad = jnp.where(mine, grad_ref[0, :, base : base + 2 * LANES], 0)
        key = key_ref[0, :, base : base + 2 * LANES]
        value = value_ref[0, :, base : base + 2 * LANES]
        scores = jnp.where(allowed, dot(key, query, NT), NEG)
        probs = jnp.exp(scores - lse_ref[0, head : head + 1, :])
        grad_probs = dot(value, grad, NT)
        grad_scores = (probs * (grad_probs - delta_ref[0, head : head + 1, :])).astype(BF16)
        value_tiles.add(base, dot(probs.astype(BF16), grad))
        key_tiles.add(base, dot(grad_scores, query))
        query_tiles.add(base, jnp.where(mine, dot(grad_scores, key, TN), 0.0))
    query_tiles.finish()
    key_tiles.finish()
    value_tiles.finish()


def row_call(kernel, name, args, outs, flops):
    def spec(shape):
        rest = len(shape) - 1
        return pl.BlockSpec((1,) + tuple(shape[1:]), lambda row: (row,) + (0,) * rest)

    moved = sum(a.size * a.dtype.itemsize for a in list(args) + list(outs))
    return pl.pallas_call(
        kernel,
        grid=(args[0].shape[0],),
        in_specs=[spec(a.shape) for a in args],
        out_specs=[spec(o.shape) for o in outs],
        out_shape=outs,
        name=name,
        cost_estimate=pl.CostEstimate(flops=flops, bytes_accessed=moved, transcendentals=0),
        compiler_params=pltpu.CompilerParams(vmem_limit_bytes=48 * 1024 * 1024),
    )(*args)


def shards(
    dp,
    mp,
    byte_in,
    latents,
    cotangent,
    byte_gain,
    latent_gain,
    mlp_gain,
    w_query,
    w_key,
    w_value,
    w_out,
    b_out,
    w_up,
    b_up,
    w_down,
    b_down,
    byte_seg,
    byte_pad,
    latent_seg,
):
    score_scale = HEAD_DIM ** (-0.5)
    rows, byte_len, byte_width = byte_in.shape
    own_lat, lat_width = latents.shape[1:]
    lat_len = own_lat * mp
    dp_index = lax.axis_index("dp")
    mp_index = lax.axis_index("mp")
    heads = w_query.shape[1] * mp // HEAD_DIM

    def whole(shard):
        part = shard.shape[0] // dp
        mine = lax.dynamic_slice_in_dim(shard, dp_index * part, part, 0)
        return lax.all_gather(mine, ("mp", "dp"), axis=0, tiled=True)

    key_t, value_t = whole(w_key.T), whole(w_value.T)
    query_t = whole(w_query.T)
    out_w = whole(w_out)
    up_t, down_w = whole(w_up.T), whole(w_down)
    b_up_all = lax.all_gather(b_up, "mp", axis=0, tiled=True)

    latents = latents.reshape(rows * own_lat, lat_width)
    cotangent = cotangent.reshape(rows * own_lat, lat_width)
    byte_in = byte_in.reshape(rows * byte_len, byte_width)
    lat_hat, lat_inv = normalize(latents)
    lat_norm = (lat_hat * latent_gain).astype(BF16)
    lat_all = lax.all_gather(
        lat_norm.reshape(rows, own_lat, lat_width), "mp", axis=1, tiled=True
    ).reshape(rows * lat_len, lat_width)
    byte_hat, byte_inv = normalize(byte_in)
    byte_norm = (byte_hat * byte_gain).astype(BF16)

    keys = dot(byte_norm, key_t, NT).astype(BF16).reshape(rows, byte_len, -1)
    values = dot(byte_norm, value_t, NT).astype(BF16).reshape(rows, byte_len, -1)
    queries = (dot(lat_all, query_t, NT) * score_scale).astype(BF16).reshape(rows, lat_len, -1)

    real_seg = jnp.where(byte_pad == 1, byte_seg, -1)
    real_seg = lax.dynamic_slice_in_dim(real_seg, mp_index * byte_len, byte_len, 1)
    byte_col, byte_row = real_seg[:, :, None], real_seg[:, None, :]
    lat_col, lat_row = latent_seg[:, :, None], latent_seg[:, None, :]
    unit = 2 * rows * lat_len * byte_len * heads * 2 * LANES

    (lse_part,) = row_call(
        lse_kernel,
        "lse",
        (queries, keys, lat_row, byte_col),
        [jax.ShapeDtypeStruct((rows, heads, lat_len), F32)],
        unit,
    )
    lse_parts = lax.all_gather(lse_part, "mp", axis=0)
    lse_peak = jnp.max(lse_parts, 0)
    lse = lse_peak + jnp.log(jnp.sum(jnp.exp(lse_parts - lse_peak), 0))
    (attended_part,) = row_call(
        attend_kernel,
        "attend",
        (queries, keys, values, lat_col, byte_row, lse.transpose(0, 2, 1)),
        [jax.ShapeDtypeStruct((rows, lat_len, lat_width), BF16)],
        2 * unit,
    )
    attended = lax.psum_scatter(attended_part, "mp", scatter_dimension=1, tiled=True)
    attended = attended.reshape(rows * own_lat, lat_width)

    hidden = latents + dot(attended, out_w) + b_out
    mid_hat, mid_inv = normalize(hidden)
    mid_norm = (mid_hat * mlp_gain).astype(BF16)
    pre_act = dot(mid_norm, up_t, NT) + b_up_all
    activated = gelu_exact(pre_act).astype(BF16)
    result = hidden + dot(activated, down_w) + b_down

    grad_down = cotangent.astype(BF16)
    grad_act = dot(grad_down, down_w, NT)
    _, gelu_pull = jax.vjp(gelu_exact, pre_act)
    grad_pre = gelu_pull(grad_act)[0].astype(BF16)
    grad_b_up = jnp.sum(grad_pre.astype(F32), axis=0)
    grad_mid = dot(grad_pre, up_t)
    grad_mid_back, grad_mlp_gain = norm_back(grad_mid, mid_hat, mid_inv, mlp_gain)
    grad_hidden = cotangent + grad_mid_back
    grad_attn = grad_hidden.astype(BF16)
    grad_att = dot(grad_attn, out_w, NT).astype(BF16)
    delta = jnp.sum(
        (attended.astype(F32) * grad_att.astype(F32)).reshape(rows, own_lat, heads, HEAD_DIM), -1
    )
    grad_att_all = lax.all_gather(
        grad_att.reshape(rows, own_lat, lat_width), "mp", axis=1, tiled=True
    )
    delta_all = lax.all_gather(delta.transpose(0, 2, 1), "mp", axis=2, tiled=True)

    def summed(partial):
        piece = lax.psum_scatter(
            partial.astype(BF16), ("mp", "dp"), scatter_dimension=0, tiled=True
        )
        return lax.all_gather(piece, "dp", axis=0, tiled=True).astype(F32)

    grad_w_down = summed(dot(activated, grad_down, TN))
    grad_w_up = summed(dot(grad_pre, mid_norm, TN)).T
    grad_w_out = summed(dot(attended, grad_attn, TN))

    grad_queries, grad_keys, grad_values = row_call(
        attend_back_kernel,
        "attend_back",
        (queries, keys, values, grad_att_all, lat_row, byte_col, lse, delta_all),
        [
            jax.ShapeDtypeStruct((rows, lat_len, lat_width), BF16),
            jax.ShapeDtypeStruct((rows, byte_len, lat_width), BF16),
            jax.ShapeDtypeStruct((rows, byte_len, lat_width), BF16),
        ],
        5 * unit,
    )
    grad_queries_own = lax.psum_scatter(grad_queries, "mp", scatter_dimension=1, tiled=True)
    grad_queries_own = grad_queries_own.reshape(rows * own_lat, lat_width)
    grad_queries = grad_queries.reshape(rows * lat_len, lat_width)
    grad_keys = grad_keys.reshape(rows * byte_len, lat_width)
    grad_values = grad_values.reshape(rows * byte_len, lat_width)
    grad_w_value = summed(dot(grad_values, byte_norm, TN)).T
    grad_w_key = summed(dot(grad_keys, byte_norm, TN)).T
    grad_w_query = summed(dot(grad_queries, lat_all, TN) * score_scale).T
    grad_byte_norm = dot(grad_keys, key_t) + dot(grad_values, value_t)
    grad_bytes, grad_byte_gain = norm_back(grad_byte_norm, byte_hat, byte_inv, byte_gain)
    grad_lat_norm = dot(grad_queries_own, query_t) * score_scale
    grad_lat_back, grad_latent_gain = norm_back(grad_lat_norm, lat_hat, lat_inv, latent_gain)
    grad_latents = grad_hidden + grad_lat_back
    grad_b_out = jnp.sum(grad_hidden, axis=0)
    grad_b_down = jnp.sum(cotangent, axis=0)
    small = lax.psum(
        (grad_byte_gain, grad_latent_gain, grad_mlp_gain, grad_b_out, grad_b_down, grad_b_up),
        ("dp", "mp"),
    )
    own_units = b_up.shape[0]
    return (
        result.reshape(rows, own_lat, lat_width),
        grad_bytes.reshape(rows, byte_len, byte_width),
        grad_latents.reshape(rows, own_lat, lat_width),
        small[0],
        small[1],
        small[2],
        grad_w_query,
        grad_w_key,
        grad_w_value,
        grad_w_out,
        small[3],
        grad_w_up,
        lax.dynamic_slice_in_dim(small[5], mp_index * own_units, own_units, 0),
        grad_w_down,
        small[4],
    )


def solution(mesh):
    by_row = P("dp", "mp", None)
    columns, lines = P(None, "mp"), P("mp", None)
    return jax.shard_map(
        functools.partial(shards, mesh.shape["dp"], mesh.shape["mp"]),
        mesh=mesh,
        in_specs=(
            by_row,
            by_row,
            by_row,
            P(),
            P(),
            P(),
            columns,
            columns,
            columns,
            lines,
            P(),
            columns,
            P("mp"),
            lines,
            P(),
            P("dp", None),
            P("dp", None),
            P("dp", None),
        ),
        out_specs=(
            by_row,
            by_row,
            by_row,
            P(),
            P(),
            P(),
            columns,
            columns,
            columns,
            lines,
            P(),
            columns,
            P("mp"),
            lines,
            P(),
        ),
        check_vma=False,
    )
```

```python
import functools

import jax
import jax.numpy as jnp
from jax import lax
from jax.experimental import pallas as pl
from jax.experimental.pallas import tpu as pltpu
from jax.sharding import PartitionSpec as P

HEAD_DIM = 160
EPS = 1e-05
NEG = -1e30
LANES = 128
F32 = jnp.float32
BF16 = jnp.bfloat16
NN = (((1,), (0,)), ((), ()))
NT = (((1,), (1,)), ((), ()))
TN = (((0,), (0,)), ((), ()))


def dot(a, b, dims=NN):
    return lax.dot_general(a, b, dims, preferred_element_type=F32)


def normalize(field):
    average = jnp.mean(field, -1, keepdims=True)
    centred = field - average
    inv_scale = lax.rsqrt(jnp.mean(centred * centred, -1, keepdims=True) + EPS)
    return (centred * inv_scale, inv_scale)


def norm_back(grad_out, normed, inv_scale, scale_vec):
    weighted = grad_out * scale_vec
    centred_grad = (
        weighted
        - jnp.mean(weighted, -1, keepdims=True)
        - normed * jnp.mean(weighted * normed, -1, keepdims=True)
    )
    return (inv_scale * centred_grad, jnp.sum(grad_out * normed, axis=0))


def gelu_exact(field):
    return jax.nn.gelu(field, approximate=False)


def windows(columns):
    out = []
    for head in range(columns // HEAD_DIM):
        start = head * HEAD_DIM
        base = start // LANES * LANES
        assert start + HEAD_DIM <= base + 2 * LANES
        out.append((base, start - base, start - base + HEAD_DIM))
    return out


def own_columns(shape, low, high):
    lane = lax.broadcasted_iota(jnp.int32, shape, 1)
    return (lane >= low) & (lane < high)


def lse_kernel(query_ref, key_ref, lat_seg_ref, byte_seg_ref, lse_ref):
    allowed = byte_seg_ref[0] == lat_seg_ref[0]
    for head, (base, low, high) in enumerate(windows(query_ref.shape[2])):
        query = query_ref[0, :, base : base + 2 * LANES]
        query = jnp.where(own_columns(query.shape, low, high), query, 0)
        key = key_ref[0, :, base : base + 2 * LANES]
        scores = jnp.where(allowed, dot(key, query, NT), NEG)
        peak = jnp.max(scores, 0, keepdims=True)
        total = jnp.sum(jnp.exp(scores - peak), 0, keepdims=True)
        lse_ref[0, head : head + 1, :] = peak + jnp.log(total)


class Tiles:
    def __init__(self, ref):
        self.ref = ref
        self.held = {}

    def add(self, base, window):
        for part in range(2):
            tile = base + part * LANES
            piece = window[:, part * LANES : (part + 1) * LANES]
            self.held[tile] = self.held[tile] + piece if tile in self.held else piece
        for tile in [t for t in self.held if t < base]:
            self.store(tile)

    def store(self, tile):
        self.ref[0, :, tile : tile + LANES] = self.held.pop(tile).astype(self.ref.dtype)

    def finish(self):
        for tile in list(self.held):
            self.store(tile)


def attend_kernel(query_ref, key_ref, value_ref, lat_seg_ref, byte_seg_ref, lse_ref, out_ref):
    allowed = lat_seg_ref[0] == byte_seg_ref[0]
    tiles = Tiles(out_ref)
    for head, (base, low, high) in enumerate(windows(query_ref.shape[2])):
        query = query_ref[0, :, base : base + 2 * LANES]
        mine = own_columns(query.shape, low, high)
        query = jnp.where(mine, query, 0)
        key = key_ref[0, :, base : base + 2 * LANES]
        value = value_ref[0, :, base : base + 2 * LANES]
        scores = jnp.where(allowed, dot(query, key, NT), NEG)
        probs = jnp.exp(scores - lse_ref[0, :, head : head + 1]).astype(BF16)
        tiles.add(base, jnp.where(mine, dot(probs, value), 0.0))
    tiles.finish()


def attend_back_kernel(
    query_ref,
    key_ref,
    value_ref,
    grad_ref,
    lat_seg_ref,
    byte_seg_ref,
    lse_ref,
    delta_ref,
    grad_query_ref,
    grad_key_ref,
    grad_value_ref,
):
    allowed = byte_seg_ref[0] == lat_seg_ref[0]
    query_tiles, key_tiles, value_tiles = (
        Tiles(grad_query_ref),
        Tiles(grad_key_ref),
        Tiles(grad_value_ref),
    )
    for head, (base, low, high) in enumerate(windows(query_ref.shape[2])):
        query = query_ref[0, :, base : base + 2 * LANES]
        mine = own_columns(query.shape, low, high)
        query = jnp.where(mine, query, 0)
        grad = jnp.where(mine, grad_ref[0, :, base : base + 2 * LANES], 0)
        key = key_ref[0, :, base : base + 2 * LANES]
        value = value_ref[0, :, base : base + 2 * LANES]
        scores = jnp.where(allowed, dot(key, query, NT), NEG)
        probs = jnp.exp(scores - lse_ref[0, head : head + 1, :])
        grad_probs = dot(value, grad, NT)
        grad_scores = (probs * (grad_probs - delta_ref[0, head : head + 1, :])).astype(BF16)
        value_tiles.add(base, dot(probs.astype(BF16), grad))
        key_tiles.add(base, dot(grad_scores, query))
        query_tiles.add(base, jnp.where(mine, dot(grad_scores, key, TN), 0.0))
    query_tiles.finish()
    key_tiles.finish()
    value_tiles.finish()


def row_call(kernel, name, args, outs, flops):
    def spec(shape):
        rest = len(shape) - 1
        return pl.BlockSpec((1,) + tuple(shape[1:]), lambda row: (row,) + (0,) * rest)

    moved = sum(a.size * a.dtype.itemsize for a in list(args) + list(outs))
    return pl.pallas_call(
        kernel,
        grid=(args[0].shape[0],),
        in_specs=[spec(a.shape) for a in args],
        out_specs=[spec(o.shape) for o in outs],
        out_shape=outs,
        name=name,
        cost_estimate=pl.CostEstimate(flops=flops, bytes_accessed=moved, transcendentals=0),
        compiler_params=pltpu.CompilerParams(vmem_limit_bytes=48 * 1024 * 1024),
    )(*args)


def ring(size, step=1):
    return [(i, (i + step) % size) for i in range(size)]


def add(a, b):
    return (a.astype(F32) + b.astype(F32)).astype(a.dtype)


class Mesh:
    def __init__(self, dp, mp):
        self.dp, self.mp = dp, mp
        self.dp_index = lax.axis_index("dp")
        self.mp_index = lax.axis_index("mp")
        self.links = [1 << k for k in range(1, dp.bit_length() - 1)]

    def order(self, turn):
        turn %= len(self.links)
        return [1] + self.links[turn:] + self.links[:turn]

    def swap(self, x, bit):
        return lax.ppermute(x, "dp", [(i, i ^ bit) for i in range(self.dp)])

    def bit(self, bit):
        return (self.dp_index // bit) % 2

    def ring_gather(self, x):
        blocks = [x]
        for _ in range(self.mp - 1):
            blocks.append(lax.ppermute(blocks[-1], "mp", ring(self.mp)))
        return blocks

    def ring_scatter(self, parts):
        total = parts[1] if self.mp > 1 else parts[0]
        for step in range(2, self.mp + 1):
            total = add(lax.ppermute(total, "mp", ring(self.mp)), parts[step % self.mp])
        return total

    def keep_half(self, x, bit):
        half = x.shape[1] // 2
        mine = self.bit(bit)
        sent = lax.dynamic_slice_in_dim(x, (1 - mine) * half, half, 1)
        kept = lax.dynamic_slice_in_dim(x, mine * half, half, 1)
        return add(self.swap(sent, bit), kept)

    def double(self, x, bit):
        other = self.swap(x, bit)
        low = self.bit(bit) == 0
        return jnp.concatenate([jnp.where(low, x, other), jnp.where(low, other, x)], 1)

    def whole(self, shard, turn):
        order = self.order(turn)
        lines = shard.shape[0]
        place, part = 0, lines
        for bit in order:
            part //= 2
            place = place + self.bit(bit) * part
        mine = lax.dynamic_slice_in_dim(shard, place, part, 0)
        others = jnp.stack(self.ring_gather(mine)[1:])
        for bit in reversed(order):
            others = self.double(others, bit)
        blocks = jnp.concatenate([shard[None], others])
        back = (self.mp_index - jnp.arange(self.mp)) % self.mp
        return jnp.take(blocks, back, axis=0).reshape(self.mp * lines, -1)

    def summed(self, partial, turn):
        order = self.order(turn)
        blocks = partial.astype(BF16).reshape(self.mp, -1, partial.shape[1])
        for bit in order:
            blocks = self.keep_half(blocks, bit)
        parts = [
            lax.dynamic_index_in_dim(blocks, (self.mp_index - r) % self.mp, 0, False)
            for r in range(self.mp)
        ]
        total = self.ring_scatter(parts)[None]
        for bit in reversed(order):
            total = self.double(total, bit)
        return total[0].astype(F32)

    def total(self, x):
        for bit in self.order(0):
            x = x + self.swap(x, bit)
        return sum(
            (lax.ppermute(x, "mp", ring(self.mp, step)) for step in range(1, self.mp)), x
        )

    def turned(self, x, axis, back):
        blocks = x.reshape(x.shape[:axis] + (self.mp, -1) + x.shape[axis + 1 :])
        index = (self.mp_index - jnp.arange(self.mp)) % self.mp
        return jnp.take(blocks, index, axis=axis).reshape(x.shape)


def shards(
    dp,
    mp,
    byte_in,
    latents,
    cotangent,
    byte_gain,
    latent_gain,
    mlp_gain,
    w_query,
    w_key,
    w_value,
    w_out,
    b_out,
    w_up,
    b_up,
    w_down,
    b_down,
    byte_seg,
    byte_pad,
    latent_seg,
):
    score_scale = HEAD_DIM ** (-0.5)
    rows, byte_len, byte_width = byte_in.shape
    own_lat, lat_width = latents.shape[1:]
    lat_len = own_lat * mp
    heads = w_query.shape[1] * mp // HEAD_DIM
    net = Mesh(dp, mp)
    mp_index = net.mp_index

    latents = latents.reshape(rows * own_lat, lat_width)
    cotangent = cotangent.reshape(rows * own_lat, lat_width)
    byte_in = byte_in.reshape(rows * byte_len, byte_width)
    lat_hat, lat_inv = normalize(latents)
    lat_norm = (lat_hat * latent_gain).astype(BF16)

    def gather_latents(x):
        blocks = net.ring_gather(x.reshape(rows, own_lat, lat_width))
        return jnp.concatenate(blocks, 1)

    def scatter_latents(x):
        blocks = x.reshape(rows, mp, own_lat, lat_width)
        return net.ring_scatter([blocks[:, r] for r in range(mp)]).reshape(-1, lat_width)

    key_t, value_t = net.whole(w_key.T, 0), net.whole(w_value.T, 1)
    query_t = net.whole(w_query.T, 0)
    lat_all = gather_latents(lat_norm).reshape(rows * lat_len, lat_width)
    out_w = net.whole(w_out, 1)
    up_t, down_w = net.whole(w_up.T, 0), net.whole(w_down, 1)
    b_up_all = net.turned(jnp.concatenate(net.ring_gather(b_up)), 0, True)

    byte_hat, byte_inv = normalize(byte_in)
    byte_norm = (byte_hat * byte_gain).astype(BF16)
    keys = dot(byte_norm, key_t, NT).astype(BF16).reshape(rows, byte_len, -1)
    values = dot(byte_norm, value_t, NT).astype(BF16).reshape(rows, byte_len, -1)
    queries = (dot(lat_all, query_t, NT) * score_scale).astype(BF16).reshape(rows, lat_len, -1)

    real_seg = jnp.where(byte_pad == 1, byte_seg, -1)
    real_seg = lax.dynamic_slice_in_dim(real_seg, mp_index * byte_len, byte_len, 1)
    latent_seg = net.turned(latent_seg, 1, False)
    byte_col, byte_row = real_seg[:, :, None], real_seg[:, None, :]
    lat_col, lat_row = latent_seg[:, :, None], latent_seg[:, None, :]
    unit = 2 * rows * lat_len * byte_len * heads * 2 * LANES

    (lse_part,) = row_call(
        lse_kernel,
        "lse",
        (queries, keys, lat_row, byte_col),
        [jax.ShapeDtypeStruct((rows, heads, lat_len), F32)],
        unit,
    )
    lse_part = net.turned(lse_part, 2, True)
    lse_parts = jnp.stack(
        [lse_part] + [lax.ppermute(lse_part, "mp", ring(mp, step)) for step in range(1, mp)]
    )
    lse_peak = jnp.max(lse_parts, 0)
    lse = lse_peak + jnp.log(jnp.sum(jnp.exp(lse_parts - lse_peak), 0))
    lse = net.turned(lse, 2, False)
    (attended_part,) = row_call(
        attend_kernel,
        "attend",
        (queries, keys, values, lat_col, byte_row, lse.transpose(0, 2, 1)),
        [jax.ShapeDtypeStruct((rows, lat_len, lat_width), BF16)],
        2 * unit,
    )
    attended = scatter_latents(attended_part)

    hidden = latents + dot(attended, out_w) + b_out
    mid_hat, mid_inv = normalize(hidden)
    mid_norm = (mid_hat * mlp_gain).astype(BF16)
    pre_act = dot(mid_norm, up_t, NT) + b_up_all
    activated = gelu_exact(pre_act).astype(BF16)
    result = hidden + dot(activated, down_w) + b_down

    grad_down = cotangent.astype(BF16)
    grad_act = dot(grad_down, down_w, NT)
    _, gelu_pull = jax.vjp(gelu_exact, pre_act)
    grad_pre = gelu_pull(grad_act)[0].astype(BF16)
    grad_b_up = jnp.sum(grad_pre.astype(F32), axis=0)
    grad_mid = dot(grad_pre, up_t)
    grad_mid_back, grad_mlp_gain = norm_back(grad_mid, mid_hat, mid_inv, mlp_gain)
    grad_hidden = cotangent + grad_mid_back
    grad_attn = grad_hidden.astype(BF16)
    grad_att = dot(grad_attn, out_w, NT).astype(BF16)
    delta = jnp.sum(
        (attended.astype(F32) * grad_att.astype(F32)).reshape(rows, own_lat, heads, HEAD_DIM), -1
    )
    grad_att_all = gather_latents(grad_att)
    delta_all = jnp.concatenate(net.ring_gather(delta.transpose(0, 2, 1)), 2)

    grad_w_down = net.summed(dot(activated, grad_down, TN), 0)
    grad_w_up = net.summed(dot(grad_pre, mid_norm, TN), 1).T
    grad_w_out = net.summed(dot(attended, grad_attn, TN), 0)

    grad_queries, grad_keys, grad_values = row_call(
        attend_back_kernel,
        "attend_back",
        (queries, keys, values, grad_att_all, lat_row, byte_col, lse, delta_all),
        [
            jax.ShapeDtypeStruct((rows, lat_len, lat_width), BF16),
            jax.ShapeDtypeStruct((rows, byte_len, lat_width), BF16),
            jax.ShapeDtypeStruct((rows, byte_len, lat_width), BF16),
        ],
        5 * unit,
    )
    grad_queries_own = scatter_latents(grad_queries)
    grad_queries = grad_queries.reshape(rows * lat_len, lat_width)
    grad_keys = grad_keys.reshape(rows * byte_len, lat_width)
    grad_values = grad_values.reshape(rows * byte_len, lat_width)
    grad_w_query = net.summed(dot(grad_queries, lat_all, TN) * score_scale, 0).T
    grad_w_value = net.summed(dot(grad_values, byte_norm, TN), 1).T
    grad_w_key = net.summed(dot(grad_keys, byte_norm, TN), 1).T
    grad_byte_norm = dot(grad_keys, key_t) + dot(grad_values, value_t)
    grad_bytes, grad_byte_gain = norm_back(grad_byte_norm, byte_hat, byte_inv, byte_gain)
    grad_lat_norm = dot(grad_queries_own, query_t) * score_scale
    grad_lat_back, grad_latent_gain = norm_back(grad_lat_norm, lat_hat, lat_inv, latent_gain)
    grad_latents = grad_hidden + grad_lat_back
    grad_b_out = jnp.sum(grad_hidden, axis=0)
    grad_b_down = jnp.sum(cotangent, axis=0)

    def small_sums(*vectors):
        sums = net.total(jnp.concatenate(vectors))
        return jnp.split(sums, [sum(v.size for v in vectors[:k]) for k in range(1, len(vectors))])

    sum_mlp_gain, sum_b_out, sum_b_down, sum_b_up = small_sums(
        grad_mlp_gain, grad_b_out, grad_b_down, grad_b_up
    )
    sum_byte_gain, sum_latent_gain = small_sums(grad_byte_gain, grad_latent_gain)
    own_units = b_up.shape[0]
    return (
        result.reshape(rows, own_lat, lat_width),
        grad_bytes.reshape(rows, byte_len, byte_width),
        grad_latents.reshape(rows, own_lat, lat_width),
        sum_byte_gain,
        sum_latent_gain,
        sum_mlp_gain,
        grad_w_query,
        grad_w_key,
        grad_w_value,
        grad_w_out,
        sum_b_out,
        grad_w_up,
        lax.dynamic_slice_in_dim(sum_b_up, mp_index * own_units, own_units, 0),
        grad_w_down,
        sum_b_down,
    )


def solution(mesh):
    by_row = P("dp", "mp", None)
    columns, lines = P(None, "mp"), P("mp", None)
    return jax.shard_map(
        functools.partial(shards, mesh.shape["dp"], mesh.shape["mp"]),
        mesh=mesh,
        in_specs=(
            by_row,
            by_row,
            by_row,
            P(),
            P(),
            P(),
            columns,
            columns,
            columns,
            lines,
            P(),
            columns,
            P("mp"),
            lines,
            P(),
            P("dp", None),
            P("dp", None),
            P("dp", None),
        ),
        out_specs=(
            by_row,
            by_row,
            by_row,
            P(),
            P(),
            P(),
            columns,
            columns,
            columns,
            lines,
            P(),
            columns,
            P("mp"),
            lines,
            P(),
        ),
        check_vma=False,
    )
```

```python
import functools

import jax
import jax.numpy as jnp
from jax import lax
from jax.experimental import pallas as pl
from jax.experimental.pallas import tpu as pltpu
from jax.sharding import PartitionSpec as P

HEAD_DIM = 160
EPS = 1e-05
NEG = -1e30
LANES = 128
F32 = jnp.float32
BF16 = jnp.bfloat16
NN = (((1,), (0,)), ((), ()))
NT = (((1,), (1,)), ((), ()))
TN = (((0,), (0,)), ((), ()))


def dot(a, b, dims=NN):
    return lax.dot_general(a, b, dims, preferred_element_type=F32)


def normalize(field):
    average = jnp.mean(field, -1, keepdims=True)
    centred = field - average
    inv_scale = lax.rsqrt(jnp.mean(centred * centred, -1, keepdims=True) + EPS)
    return (centred * inv_scale, inv_scale)


def norm_back(grad_out, normed, inv_scale, scale_vec):
    weighted = grad_out * scale_vec
    centred_grad = (
        weighted
        - jnp.mean(weighted, -1, keepdims=True)
        - normed * jnp.mean(weighted * normed, -1, keepdims=True)
    )
    return (inv_scale * centred_grad, jnp.sum(grad_out * normed, axis=0))


def gelu_exact(field):
    return jax.nn.gelu(field, approximate=False)


def windows(columns):
    out = []
    for head in range(columns // HEAD_DIM):
        start = head * HEAD_DIM
        base = start // LANES * LANES
        assert start + HEAD_DIM <= base + 2 * LANES
        out.append((base, start - base, start - base + HEAD_DIM))
    return out


def lines_of(ref, base):
    return ref[:, 0, :, base : base + 2 * LANES].reshape(-1, 2 * LANES)


def own_columns(shape, low, high):
    lane = lax.broadcasted_iota(jnp.int32, shape, 1)
    return (lane >= low) & (lane < high)


def byte_norm_kernel(byte_ref, gain_ref, out_ref):
    out_ref[...] = (normalize(byte_ref[...])[0] * gain_ref[...]).astype(BF16)


def byte_back_kernel(
    halves, byte_ref, gain_ref, key_ref, value_ref, *refs
):
    grad_keys, grad_values = refs[:halves], refs[halves : 2 * halves]
    grad_ref, gain_grad_ref = refs[2 * halves :]
    grad = 0.0
    for part in range(halves):
        size = grad_keys[part].shape[1]
        grad = grad + dot(grad_keys[part][...], key_ref[part * size : (part + 1) * size, :])
        grad = grad + dot(grad_values[part][...], value_ref[part * size : (part + 1) * size, :])
    normed, inv_scale = normalize(byte_ref[...])
    grad_ref[...], gain_grad = norm_back(grad, normed, inv_scale, gain_ref[...])

    @pl.when(pl.program_id(0) == 0)
    def _():
        gain_grad_ref[...] = jnp.zeros_like(gain_grad_ref)

    gain_grad_ref[...] += gain_grad


def feed_kernel(
    latents_ref,
    cotangent_ref,
    grad_act_ref,
    gain_ref,
    b_out_ref,
    b_up_ref,
    out_ref,
    up_ref,
    attended_a_ref,
    attended_b_ref,
    hidden_ref,
    mid_norm_ref,
    activated_ref,
    grad_pre_ref,
    grad_hidden_ref,
    grad_attn_ref,
    attended_ref,
    grad_a_ref,
    grad_b_ref,
    delta_ref,
    sums_ref,
):
    half = attended_a_ref.shape[1]
    attended_ref[:, :half] = attended_a_ref[...]
    attended_ref[:, half:] = attended_b_ref[...]
    hidden_ref[...] = latents_ref[...] + dot(attended_ref[...], out_ref[...]) + b_out_ref[...]
    mid_hat, mid_inv = normalize(hidden_ref[...])
    mid_norm_ref[...] = (mid_hat * gain_ref[...]).astype(BF16)
    pre_act = dot(mid_norm_ref[...], up_ref[...], NT) + b_up_ref[...]
    below = 0.5 * (1.0 + lax.erf(pre_act * 0.5**0.5))
    activated_ref[...] = (pre_act * below).astype(BF16)
    slope = below + pre_act * (jnp.exp(-0.5 * pre_act * pre_act) * (2.0 * jnp.pi) ** -0.5)
    grad_pre_ref[...] = (grad_act_ref[...] * slope).astype(BF16)
    sums_ref[1:2, :] = jnp.sum(grad_pre_ref[...].astype(F32), axis=0, keepdims=True)
    grad_mid = dot(grad_pre_ref[...], up_ref[...])
    mid_hat, mid_inv = normalize(hidden_ref[...])
    back, gain_grad = norm_back(grad_mid, mid_hat, mid_inv, gain_ref[...])
    sums_ref[0:1, :] = gain_grad[None]
    grad_hidden_ref[...] = cotangent_ref[...] + back
    sums_ref[2:3, :] = jnp.sum(grad_hidden_ref[...], axis=0, keepdims=True)
    sums_ref[3:4, :] = jnp.sum(cotangent_ref[...], axis=0, keepdims=True)
    grad_attn_ref[...] = grad_hidden_ref[...].astype(BF16)
    grad_a_ref[...] = dot(grad_attn_ref[...], out_ref[:half, :], NT).astype(BF16)
    grad_b_ref[...] = dot(grad_attn_ref[...], out_ref[half:, :], NT).astype(BF16)
    for head, (base, low, high) in enumerate(windows(2 * half)):
        grad_ref, start = (grad_a_ref, base) if base < half else (grad_b_ref, base - half)
        product = attended_ref[:, base : base + 2 * LANES].astype(F32) * grad_ref[
            :, start : start + 2 * LANES
        ].astype(F32)
        product = jnp.where(own_columns(product.shape, low, high), product, 0.0)
        delta_ref[:, head : head + 1] = jnp.sum(product, 1, keepdims=True)


def lse_kernel(query_ref, key_ref, lat_seg_ref, byte_seg_ref, lse_ref):
    allowed = byte_seg_ref[0] == lat_seg_ref[0]
    for head, (base, low, high) in enumerate(windows(query_ref.shape[3])):
        query = lines_of(query_ref, base)
        query = jnp.where(own_columns(query.shape, low, high), query, 0)
        key = key_ref[0, :, base : base + 2 * LANES]
        scores = jnp.where(allowed, dot(key, query, NT), NEG)
        peak = jnp.max(scores, 0, keepdims=True)
        total = jnp.sum(jnp.exp(scores - peak), 0, keepdims=True)
        lse_ref[0, head : head + 1, :] = peak + jnp.log(total)


class Tiles:
    def __init__(self, ref):
        self.ref = ref
        self.held = {}

    def add(self, base, window):
        for part in range(2):
            tile = base + part * LANES
            piece = window[:, part * LANES : (part + 1) * LANES]
            self.held[tile] = self.held[tile] + piece if tile in self.held else piece
        for tile in [t for t in self.held if t < base]:
            self.store(tile)

    def store(self, tile):
        done = self.held.pop(tile).astype(self.ref.dtype)
        if len(self.ref.shape) == 4:
            self.ref[:, 0, :, tile : tile + LANES] = done.reshape(
                self.ref.shape[0], self.ref.shape[2], LANES
            )
        else:
            self.ref[0, :, tile : tile + LANES] = done

    def finish(self):
        for tile in list(self.held):
            self.store(tile)


def attend_kernel(own_lat, first_head, query_ref, key_ref, value_ref, lat_seg_ref, byte_seg_ref, *refs):
    part_refs, (out_ref, lse_ref) = refs[:-2], refs[-2:]
    parts = [part_refs[0][0]]
    for step, ref in enumerate(part_refs[1:], 1):
        parts.append(pltpu.roll(ref[0], step * own_lat, 1))
    peak = functools.reduce(jnp.maximum, parts)
    lse_ref[0] = peak + jnp.log(sum(jnp.exp(part - peak) for part in parts))
    allowed = byte_seg_ref[0] == lat_seg_ref[0]
    tiles = Tiles(out_ref)
    for head, (base, low, high) in enumerate(windows(query_ref.shape[3])):
        query = lines_of(query_ref, base)
        mine = own_columns(query.shape, low, high)
        query = jnp.where(mine, query, 0)
        key = key_ref[0, :, base : base + 2 * LANES]
        value = value_ref[0, :, base : base + 2 * LANES]
        scores = jnp.where(allowed, dot(key, query, NT), NEG)
        own = first_head + head
        probs = jnp.exp(scores - lse_ref[0, own : own + 1, :]).astype(BF16)
        tiles.add(base, jnp.where(mine, dot(probs, value, TN), 0.0))
    tiles.finish()


def attend_back_kernel(
    first_head,
    place_ref,
    query_ref,
    key_ref,
    value_ref,
    lat_seg_ref,
    byte_seg_ref,
    lse_ref,
    delta_ref,
    grad_ref,
    grad_query_ref,
    grad_key_ref,
    grad_value_ref,
):
    blocks = grad_ref.shape[0]
    ring_order = [lax.rem(place_ref[0] + (blocks - r), blocks) for r in range(blocks)]
    allowed = byte_seg_ref[0] == lat_seg_ref[0]
    query_tiles, key_tiles, value_tiles = (
        Tiles(grad_query_ref),
        Tiles(grad_key_ref),
        Tiles(grad_value_ref),
    )
    for head, (base, low, high) in enumerate(windows(query_ref.shape[3])):
        query = lines_of(query_ref, base)
        mine = own_columns(query.shape, low, high)
        query = jnp.where(mine, query, 0)
        grad = jnp.concatenate([grad_ref[at, 0, :, base : base + 2 * LANES] for at in ring_order])
        grad = jnp.where(mine, grad, 0)
        key = key_ref[0, :, base : base + 2 * LANES]
        value = value_ref[0, :, base : base + 2 * LANES]
        scores = jnp.where(allowed, dot(key, query, NT), NEG)
        own = first_head + head
        probs = jnp.exp(scores - lse_ref[0, own : own + 1, :])
        grad_probs = dot(value, grad, NT)
        grad_scores = (probs * (grad_probs - delta_ref[0, own : own + 1, :])).astype(BF16)
        value_tiles.add(base, dot(probs.astype(BF16), grad))
        key_tiles.add(base, dot(grad_scores, query))
        query_tiles.add(base, jnp.where(mine, dot(grad_scores, key, TN), 0.0))
    query_tiles.finish()
    key_tiles.finish()
    value_tiles.finish()


def row_call(kernel, name, args, outs, flops, half=None):
    def spec(shape, halved=False):
        if len(shape) == 1:
            return pl.BlockSpec(memory_space=pltpu.SMEM)
        block = list(shape)
        block[1 if len(shape) == 4 else 0] = 1
        if halved:
            block[-1] //= 2
        at = half if halved else 0
        if len(shape) == 4:
            return pl.BlockSpec(tuple(block), lambda row: (0, row, 0, at))
        return pl.BlockSpec(tuple(block), lambda row: (row, 0, at))

    moved = sum(a.size * a.dtype.itemsize for a, _ in args)
    return pl.pallas_call(
        kernel,
        grid=(outs[-1].shape[0],),
        in_specs=[spec(a.shape, halved) for a, halved in args],
        out_specs=[spec(o.shape) for o in outs],
        out_shape=outs,
        name=name,
        cost_estimate=pl.CostEstimate(flops=flops, bytes_accessed=moved, transcendentals=0),
        compiler_params=pltpu.CompilerParams(vmem_limit_bytes=48 * 1024 * 1024),
    )(*[a for a, _ in args])


def block_call(kernel, name, lines, args, outs, flops):
    def spec(shape, cut):
        block = (lines if cut else shape[0], shape[1])
        return pl.BlockSpec(block, (lambda i: (i, 0)) if cut else (lambda i: (0, 0)))

    moved = sum(a.size * a.dtype.itemsize for a, _ in args)
    return pl.pallas_call(
        kernel,
        grid=(args[0][0].shape[0] // lines,),
        in_specs=[spec(a.shape, cut) for a, cut in args],
        out_specs=[spec(o.shape, cut) for o, cut in outs],
        out_shape=[o for o, _ in outs],
        name=name,
        cost_estimate=pl.CostEstimate(flops=flops, bytes_accessed=moved, transcendentals=0),
        compiler_params=pltpu.CompilerParams(vmem_limit_bytes=56 * 1024 * 1024),
    )(*[a for a, _ in args])


def ring(size, step=1):
    return [(i, (i + step) % size) for i in range(size)]


def add(first, *others):
    total = first.astype(F32)
    for other in others:
        total = total + other.astype(F32)
    return total.astype(first.dtype)


def panels(widths):
    return [(m, p) for m, width in enumerate(widths) for p in range(width // (2 * LANES))]


def join_kernel(widths, core_ref, mine_ref, other_ref, *out_refs):
    chips, part = mine_ref.shape[0], mine_ref.shape[3]

    def copy(sides):
        for number, (m, p) in enumerate(panels(widths)):
            for side, ref in enumerate(sides):
                at = side * widths[m] // 2 + p * LANES
                for chip in range(chips):
                    out_refs[m][chip * part : (chip + 1) * part, at : at + LANES] = ref[
                        chip, 0, number
                    ]

    @pl.when(core_ref[0] == 0)
    def _():
        copy((mine_ref, other_ref))

    @pl.when(core_ref[0] == 1)
    def _():
        copy((other_ref, mine_ref))


def split_kernel(widths, core_ref, *refs):
    in_refs, (kept_ref, sent_ref) = refs[:-2], refs[-2:]
    chips, part = kept_ref.shape[0], kept_ref.shape[3]

    def copy(sides):
        for number, (m, p) in enumerate(panels(widths)):
            for side, ref in enumerate(sides):
                at = side * widths[m] // 2 + p * LANES
                for chip in range(chips):
                    ref[chip, 0, number] = in_refs[m][
                        chip * part : (chip + 1) * part, at : at + LANES
                    ]

    @pl.when(core_ref[0] == 0)
    def _():
        copy((kept_ref, sent_ref))

    @pl.when(core_ref[0] == 1)
    def _():
        copy((sent_ref, kept_ref))


def packed_spec(shape):
    chips, _, count, part, lanes = shape
    return pl.BlockSpec((chips, 1, count, part, lanes), lambda z: (0, z, 0, 0, 0))


def matrix_spec(lines, width):
    return pl.BlockSpec((lines, width), lambda z: (z, 0))


def join(core, mine, other, widths):
    chips, blocks, _, part, _ = mine.shape
    lines = chips * part
    return pl.pallas_call(
        functools.partial(join_kernel, widths),
        grid=(blocks,),
        in_specs=[
            pl.BlockSpec(memory_space=pltpu.SMEM),
            packed_spec(mine.shape),
            packed_spec(mine.shape),
        ],
        out_specs=[matrix_spec(lines, width) for width in widths],
        out_shape=[jax.ShapeDtypeStruct((blocks * lines, width), mine.dtype) for width in widths],
        name="join",
        cost_estimate=pl.CostEstimate(
            flops=0, bytes_accessed=4 * mine.size * 2, transcendentals=0
        ),
        compiler_params=pltpu.CompilerParams(vmem_limit_bytes=48 * 1024 * 1024),
    )(core, mine, other)


def split(core, matrices, chips, blocks):
    widths = [m.shape[1] for m in matrices]
    lines = matrices[0].shape[0] // blocks
    shape = (chips, blocks, len(panels(widths)), lines // chips, LANES)
    packed = jax.ShapeDtypeStruct(shape, matrices[0].dtype)
    return pl.pallas_call(
        functools.partial(split_kernel, widths),
        grid=(blocks,),
        in_specs=[pl.BlockSpec(memory_space=pltpu.SMEM)]
        + [matrix_spec(lines, width) for width in widths],
        out_specs=[packed_spec(shape)] * 2,
        out_shape=[packed] * 2,
        name="split",
        cost_estimate=pl.CostEstimate(
            flops=0, bytes_accessed=8 * sum(m.size for m in matrices) // 2, transcendentals=0
        ),
        compiler_params=pltpu.CompilerParams(vmem_limit_bytes=48 * 1024 * 1024),
    )(core, *matrices)


def after(x, *earlier):
    return lax.optimization_barrier((x, *earlier))[0]


def three_parts(x, shape):
    parts = []
    for _ in range(3):
        part = lax.reduce_precision(x, 8, 7)
        parts.append(part.astype(BF16))
        x = x - part
    parts = jnp.concatenate(parts)
    size = shape[0] * shape[1]
    return jnp.pad(parts, (0, size - parts.size)).reshape(shape)


def from_three_parts(x, size):
    parts = x.reshape(x.shape[0], -1)[:, : 3 * size].astype(F32).reshape(-1, 3, size)
    return (parts[:, 0] + (parts[:, 1] + parts[:, 2])).reshape(-1)


class Mesh:
    def __init__(self, dp, mp):
        self.dp, self.mp = dp, mp
        self.dp_index = lax.axis_index("dp")
        self.mp_index = lax.axis_index("mp")
        self.core = self.dp_index % 2

    def cut(self, lines):
        chips = 1
        while 2 * chips <= self.dp // 2 and lines % (32 * chips) == 0:
            chips *= 2
        return chips, [2 * k for k in (1 << b for b in range(8)) if chips <= k < self.dp // 2]

    def swap(self, x, bit):
        return lax.ppermute(x, "dp", [(i, i ^ bit) for i in range(self.dp)])

    def shift(self, x, step):
        return lax.ppermute(x, "mp", ring(self.mp, step))

    def ring_gather(self, x):
        blocks = [x]
        for _ in range(self.mp - 1):
            blocks.append(self.shift(blocks[-1], 1))
        return blocks

    def ring_scatter(self, parts):
        total = parts[1] if self.mp > 1 else parts[0]
        for step in range(2, self.mp + 1):
            total = add(self.shift(total, 1), parts[step % self.mp])
        return total

    def chip_groups(self, chips):
        return [
            [2 * (chip + chips * rest) + core for chip in range(chips)]
            for rest in range(self.dp // 2 // chips)
            for core in range(2)
        ]

    def slice_of(self, shards):
        chips, _ = self.cut(shards[0].shape[0])
        part = shards[0].shape[0] // chips
        chip = self.dp_index // 2 % chips
        return jnp.concatenate(
            [
                lax.dynamic_slice(
                    shard,
                    (chip * part, self.core * (shard.shape[1] // 2)),
                    (part, shard.shape[1] // 2),
                )
                .reshape(part, -1, LANES)
                .transpose(1, 0, 2)
                for shard in shards
            ]
        )

    def in_order(self, parts):
        blocks = jnp.stack(parts)
        back = (self.mp_index - jnp.arange(self.mp)) % self.mp
        return jnp.take(blocks, back, axis=0)

    def gather_chips(self, x, lines):
        chips, _ = self.cut(lines)
        return lax.all_gather(x, "dp", axis=0, axis_index_groups=self.chip_groups(chips))

    def both_cores(self, mine, widths):
        return join(self.core[None], mine, self.swap(mine, 1), widths)

    def split_core(self, partials, lines):
        chips, _ = self.cut(lines)
        blocks = partials[0].shape[0] // lines
        return split(self.core[None], partials, chips, blocks)

    def scatter_chips(self, total, lines):
        chips, _ = self.cut(lines)
        return lax.psum_scatter(
            total, "dp", scatter_dimension=0, axis_index_groups=self.chip_groups(chips)
        )

    def link_pieces(self, total, lines):
        chips, _ = self.cut(lines)
        bits = [1 << b for b in range(chips.bit_length() - 1)]
        middle = (total.shape[2] + 1) // 2
        return [
            (piece.reshape((2,) * len(bits) + piece.shape[1:]), order, sorted(bits, reverse=True))
            for order, piece in ((bits, total[:, :, :middle]), (bits[::-1], total[:, :, middle:]))
        ]

    def link_step(self, pieces, *earlier):
        out = []
        for piece, order, left in pieces:
            mine = self.dp_index // (2 * order[0]) % 2
            axis = left.index(order[0])
            if earlier:
                piece = after(piece, *earlier)
            sent = lax.dynamic_index_in_dim(piece, 1 - mine, axis, False)
            kept = lax.dynamic_index_in_dim(piece, mine, axis, False)
            piece = add(kept, self.swap(sent, 2 * order[0]))
            out.append((piece, order[1:], [bit for bit in left if bit != order[0]]))
        return out

    def finish_sum(self, total, lines, widths, small=None):
        chips, rest = self.cut(lines)
        for bit in rest:
            total = add(total, self.swap(total, bit))
        blocks = [
            lax.dynamic_index_in_dim(total, (self.mp_index + step) % self.mp, 0, False)
            for step in range(self.mp)
        ]
        if small is not None:
            panel = small.astype(BF16)
            panel = jnp.pad(panel, (0, total[0, 0].size - panel.size)).reshape(1, -1, LANES)
            blocks = [jnp.concatenate([block, panel]) for block in blocks]
        total = add(blocks[0], *[self.shift(blocks[step], step) for step in range(1, self.mp)])
        slices = [total] + [self.swap(total, 2 * k) for k in range(1, chips)]
        if small is not None:
            panel = add(*[piece[-1] for piece in slices])
            for bit in rest:
                panel = add(panel, self.swap(panel, bit))
            slices = [jnp.concatenate([piece[:-1], panel[None]]) for piece in slices]
        chip = self.dp_index // 2 % chips
        mine = jnp.take(jnp.stack(slices), chip ^ jnp.arange(chips), axis=0)[:, None]
        other = self.swap(mine, 1)
        out = join(self.core[None], mine, other, widths)
        if small is None:
            return out
        panel = mine[0, 0, -1].astype(F32) + other[0, 0, -1].astype(F32)
        return out, panel.reshape(-1)[: small.size]

    def turned(self, x, axis):
        blocks = x.reshape(x.shape[:axis] + (self.mp, -1) + x.shape[axis + 1 :])
        index = (self.mp_index - jnp.arange(self.mp)) % self.mp
        return jnp.take(blocks, index, axis=axis).reshape(x.shape)


def shards(
    dp,
    mp,
    byte_in,
    latents,
    cotangent,
    byte_gain,
    latent_gain,
    mlp_gain,
    w_query,
    w_key,
    w_value,
    w_out,
    b_out,
    w_up,
    b_up,
    w_down,
    b_down,
    byte_seg,
    byte_pad,
    latent_seg,
):
    score_scale = HEAD_DIM ** (-0.5)
    rows, byte_len, byte_width = byte_in.shape
    own_lat, lat_width = latents.shape[1:]
    lat_len = own_lat * mp
    own_lines, half_width = rows * own_lat, lat_width // 2
    heads = w_query.shape[1] * mp // HEAD_DIM
    half_heads = heads // 2
    net = Mesh(dp, mp)
    mp_index = net.mp_index
    shape = jax.ShapeDtypeStruct

    lines = w_query.shape[1]
    head_widths = [lat_width, byte_width, byte_width]
    feed_widths = [lat_width] * 3
    feed_slice = net.slice_of([w_out, w_up.T, w_down])
    feed_slice = jnp.concatenate([feed_slice, three_parts(b_up, feed_slice.shape[1:])[None]])
    head_slice = net.slice_of([w_query.T, w_key.T, w_value.T])
    head_parts = [head_slice] + [net.shift(head_slice, step) for step in range(1, mp)]

    latents = latents.reshape(own_lines, lat_width)
    cotangent = cotangent.reshape(own_lines, lat_width)
    byte_in = byte_in.reshape(rows * byte_len, byte_width)
    lat_hat, lat_inv = normalize(latents)
    lat_norm = (lat_hat * latent_gain).astype(BF16).reshape(rows, own_lat, lat_width)
    (byte_norm,) = block_call(
        byte_norm_kernel,
        "byte_norm",
        byte_len,
        [(byte_in, True), (byte_gain[None], False)],
        [(shape(byte_in.shape, BF16), True)],
        10 * byte_in.size,
    )
    lat_blocks = [lat_norm, net.shift(lat_norm, 1)]
    head_parts, lat_blocks, byte_norm = lax.optimization_barrier(
        (head_parts, lat_blocks, byte_norm)
    )
    head_slices = net.in_order(head_parts)
    for step in range(2, mp):
        block = lat_blocks[-1]
        if step == 3:
            block = after(block, head_slices)
        lat_blocks.append(net.shift(block, 1))
    feed_slices = lax.all_gather(after(feed_slice, lat_blocks[mp - 2]), "mp", axis=0)
    lat_all = jnp.stack(lat_blocks)
    lat_flat = lat_all.reshape(rows * lat_len, lat_width)
    head_slices = after(net.gather_chips(head_slices, lines), lat_blocks[-1])
    query_t, key_t, value_t = net.both_cores(head_slices, head_widths)

    real_seg = jnp.where(byte_pad == 1, byte_seg, -1)
    real_seg = lax.dynamic_slice_in_dim(real_seg, mp_index * byte_len, byte_len, 1)
    byte_col = real_seg[:, :, None]
    lat_row = net.turned(latent_seg, 1)[:, None, :]
    unit = 2 * rows * lat_len * byte_len * half_heads * 2 * LANES

    keys = dot(byte_norm, key_t, NT).astype(BF16).reshape(rows, byte_len, lat_width)
    queries = (dot(lat_flat, query_t, NT) * score_scale).astype(BF16)
    queries = queries.reshape(lat_all.shape)
    (lse_part,) = row_call(
        lse_kernel,
        "lse",
        [(queries, False), (keys, False), (lat_row, False), (byte_col, False)],
        [shape((rows, heads, lat_len), F32)],
        2 * unit,
    )
    lse_parts = [lse_part] + [net.shift(lse_part, step) for step in range(1, mp)]
    feed_slices = after(feed_slices, lse_part)
    b_up_all = from_three_parts(feed_slices[:, -1], b_up.shape[0])
    feed_slices = net.gather_chips(feed_slices[:, :-1], lines)
    values = dot(after(byte_norm, lse_part), value_t, NT).astype(BF16)
    values = values.reshape(rows, byte_len, lat_width)

    lat_half = shape((mp, rows, own_lat, half_width), BF16)
    parts = []
    for half in range(2):
        attended_part, lse = row_call(
            functools.partial(attend_kernel, own_lat, half * half_heads),
            "attend",
            [(queries, True), (keys, True), (values, True), (lat_row, False), (byte_col, False)]
            + [(part, False) for part in lse_parts],
            [lat_half, shape((rows, heads, lat_len), F32)],
            2 * unit,
            half,
        )
        parts.append(attended_part)
    attended = [parts[0][1], parts[1][1]]
    for step in range(2, mp + 1):
        moved = net.shift(attended[0], 1)
        if step == 2:
            moved, attended[1] = lax.optimization_barrier((moved, attended[1]))
            feed_slices = after(feed_slices, moved)
        attended[0] = add(moved, parts[0][step % mp])
        attended[1] = add(net.shift(after(attended[1], moved), 1), parts[1][step % mp])
    attended = [x.reshape(own_lines, half_width) for x in attended]

    out_w, up_t, down_w = net.both_cores(feed_slices, feed_widths)
    grad_down = cotangent.astype(BF16)
    grad_act = dot(grad_down, down_w, NT)
    whole = shape((own_lines, lat_width), BF16)
    wide = shape((own_lines, lat_width), F32)
    part = shape((own_lines, half_width), BF16)
    (
        hidden,
        mid_norm,
        activated,
        grad_pre,
        grad_hidden,
        grad_attn,
        attended,
        grad_att_a,
        grad_att_b,
        delta,
        feed_vectors,
    ) = block_call(
        feed_kernel,
        "feed",
        own_lines,
        [(latents, True), (cotangent, True), (grad_act, True)]
        + [(v[None], False) for v in (mlp_gain, b_out, b_up_all)]
        + [(out_w, False), (up_t, False), (attended[0], True), (attended[1], True)],
        [(wide, True), (whole, True), (whole, True), (whole, True), (wide, True), (whole, True)]
        + [(whole, True), (part, True), (part, True), (shape((own_lines, heads), F32), True)]
        + [(shape((4, lat_width), F32), False)],
        8 * own_lines * lat_width * lat_width,
    )

    result = hidden + dot(activated, down_w) + b_down
    delta = delta.reshape(rows, own_lat, heads).transpose(0, 2, 1)
    delta = jnp.concatenate([delta] + [net.shift(delta, step) for step in range(1, mp)], 2)
    feed_partials = [
        dot(activated, grad_down, TN).astype(BF16),
        dot(grad_pre, mid_norm, TN).astype(BF16),
        dot(attended, grad_attn, TN).astype(BF16),
    ]
    def gathered(grad, *earlier):
        grad = grad.reshape(rows, own_lat, half_width)
        return lax.all_gather(after(grad, *earlier) if earlier else grad, "mp", axis=0)

    grads_a = gathered(grad_att_a)
    grads_b = gathered(grad_att_b)
    feed_kept, feed_sent = net.split_core(feed_partials, lines)
    feed_sums = add(feed_kept, net.swap(feed_sent, 1))
    grads_a, feed_sums, result, delta = lax.optimization_barrier(
        (grads_a, feed_sums, result, delta)
    )
    feed_sums = net.scatter_chips(feed_sums, lines)

    def attend_back(half, grads):
        return row_call(
            functools.partial(attend_back_kernel, half * half_heads),
            "attend_back",
            [(mp_index[None], False), (queries, True), (keys, True), (values, True)]
            + [(lat_row, False), (byte_col, False), (lse, False), (delta, False), (grads, False)],
            [lat_half] + [shape((rows, byte_len, half_width), BF16)] * 2,
            5 * unit,
            half,
        )

    def head_partials(grads):
        grad_query, grad_key, grad_value = grads
        return [
            (dot(grad_query.reshape(-1, half_width), lat_flat, TN) * score_scale).astype(BF16),
            dot(grad_key.reshape(-1, half_width), byte_norm, TN).astype(BF16),
            dot(grad_value.reshape(-1, half_width), byte_norm, TN).astype(BF16),
        ]

    back_a, *rest_a = attend_back(0, grads_a)
    total_a = back_a[1]
    moved_a = net.shift(total_a, 1)
    partials_a = head_partials((back_a, *rest_a))
    kept_a, sent_a = net.split_core(partials_a, lines)
    sums_a = net.link_pieces(add(kept_a, net.swap(sent_a, 1)), lines)

    grads_b = after(grads_b, moved_a, sums_a[0][0])
    back_b, *rest_b = attend_back(1, grads_b)
    sums_a = net.link_step(sums_a) if sums_a[0][1] else sums_a
    total_a = add(moved_a, back_a[2 % mp])
    moved_a = net.shift(total_a, 1) if mp > 2 else total_a
    total_b = back_b[1]
    tied = lax.optimization_barrier((back_b, *rest_b, moved_a, sums_a[0][0], sums_a[1][0]))
    partials_b = head_partials(tied[:3])
    moved_a = tied[3]
    sums_a = [(piece, *state[1:]) for piece, state in zip(tied[4:], sums_a)]
    while sums_a[0][1]:
        sums_a = net.link_step(sums_a)
    if mp > 2:
        total_a = add(moved_a, back_a[3 % mp])
    for step in range(4, mp + 1):
        total_a = add(net.shift(total_a, 1), back_a[step % mp])
    moved_b = net.shift(after(total_b, moved_a), 1)
    tied = lax.optimization_barrier(
        (total_a, moved_b, sums_a[0][0], sums_a[1][0], *partials_b)
    )
    total_a, moved_b, partials_b = tied[0], tied[1], tied[4:]
    sums_a = [(piece, *state[1:]) for piece, state in zip(tied[2:4], sums_a)]
    kept_b, sent_b = net.split_core(partials_b, lines)
    total_b = add(moved_b, back_b[2 % mp])
    moved_b = net.shift(total_b, 1) if mp > 2 else total_b
    sums_b = net.link_pieces(add(kept_b, net.swap(sent_b, 1)), lines)
    if sums_b[0][1]:
        sums_b = net.link_step(sums_b)
    halves = [x.reshape(-1, half_width) for x in (rest_a[0], rest_b[0], rest_a[1], rest_b[1])]
    halves[0] = after(halves[0], sent_b)
    grad_bytes, grad_byte_gain = block_call(
        functools.partial(byte_back_kernel, 2),
        "byte_back",
        byte_len,
        [(byte_in, True), (byte_gain[None], False), (key_t, False), (value_t, False)]
        + [(half, True) for half in halves],
        [(shape(byte_in.shape, F32), True), (shape((1, byte_width), F32), False)],
        4 * rows * byte_len * lat_width * byte_width,
    )
    tied = lax.optimization_barrier((grad_bytes, moved_b, sums_b[0][0], sums_b[1][0]))
    grad_bytes, moved_b = tied[:2]
    sums_b = [(piece, *state[1:]) for piece, state in zip(tied[2:], sums_b)]
    while sums_b[0][1]:
        sums_b = net.link_step(sums_b)
    total_b = add(moved_b, back_b[3 % mp]) if mp > 2 else total_b
    for step in range(4, mp + 1):
        total_b = add(net.shift(total_b, 1), back_b[step % mp])
    grad_queries_own = [t.reshape(own_lines, half_width) for t in (total_a, total_b)]

    head_sums = jnp.concatenate(
        [jnp.concatenate([piece for piece, _, _ in sums], 1) for sums in (sums_a, sums_b)]
    )
    head_grads = net.finish_sum(head_sums, lines, head_widths)
    grad_lat_norm = score_scale * (
        dot(grad_queries_own[0], query_t[:half_width])
        + dot(grad_queries_own[1], query_t[half_width:])
    )
    grad_lat_back, grad_latent_gain = norm_back(grad_lat_norm, lat_hat, lat_inv, latent_gain)
    grad_latents = grad_hidden + grad_lat_back

    small = jnp.concatenate([grad_byte_gain[0], grad_latent_gain, feed_vectors.reshape(-1)])
    feed_grads, sums = net.finish_sum(
        after(feed_sums, sums_b[0][0]), lines, feed_widths, small
    )
    sums = [sums[:byte_width]] + list(sums[byte_width:].reshape(5, lat_width))
    own_units = b_up.shape[0]
    return (
        result.reshape(rows, own_lat, lat_width),
        grad_bytes.reshape(rows, byte_len, byte_width),
        grad_latents.reshape(rows, own_lat, lat_width),
        sums[0],
        sums[1],
        sums[2],
        head_grads[0].astype(F32).T,
        head_grads[1].astype(F32).T,
        head_grads[2].astype(F32).T,
        feed_grads[2].astype(F32),
        sums[4],
        feed_grads[1].astype(F32).T,
        lax.dynamic_slice_in_dim(sums[3], mp_index * own_units, own_units, 0),
        feed_grads[0].astype(F32),
        sums[5],
    )


def solution(mesh):
    by_row = P("dp", "mp", None)
    columns, lines = P(None, "mp"), P("mp", None)
    return jax.shard_map(
        functools.partial(shards, mesh.shape["dp"], mesh.shape["mp"]),
        mesh=mesh,
        in_specs=(
            by_row,
            by_row,
            by_row,
            P(),
            P(),
            P(),
            columns,
            columns,
            columns,
            lines,
            P(),
            columns,
            P("mp"),
            lines,
            P(),
            P("dp", None),
            P("dp", None),
            P("dp", None),
        ),
        out_specs=(
            by_row,
            by_row,
            by_row,
            P(),
            P(),
            P(),
            columns,
            columns,
            columns,
            lines,
            P(),
            columns,
            P("mp"),
            lines,
            P(),
        ),
        check_vma=False,
    )
```

```python
import functools

import jax
import jax.numpy as jnp
from jax import lax
from jax.experimental import pallas as pl
from jax.experimental.pallas import tpu as pltpu
from jax.sharding import PartitionSpec as P

HEAD_DIM = 160
EPS = 1e-05
NEG = -1e30
LANES = 128
F32 = jnp.float32
BF16 = jnp.bfloat16
NN = (((1,), (0,)), ((), ()))
NT = (((1,), (1,)), ((), ()))
TN = (((0,), (0,)), ((), ()))


def dot(a, b, dims=NN):
    return lax.dot_general(a, b, dims, preferred_element_type=F32)


def normalize(field):
    average = jnp.mean(field, -1, keepdims=True)
    centred = field - average
    inv_scale = lax.rsqrt(jnp.mean(centred * centred, -1, keepdims=True) + EPS)
    return (centred * inv_scale, inv_scale)


def norm_back(grad_out, normed, inv_scale, scale_vec):
    weighted = grad_out * scale_vec
    centred_grad = (
        weighted
        - jnp.mean(weighted, -1, keepdims=True)
        - normed * jnp.mean(weighted * normed, -1, keepdims=True)
    )
    return (inv_scale * centred_grad, jnp.sum(grad_out * normed, axis=0))


def gelu_exact(field):
    return jax.nn.gelu(field, approximate=False)


def windows(columns):
    out = []
    for head in range(columns // HEAD_DIM):
        start = head * HEAD_DIM
        base = start // LANES * LANES
        assert start + HEAD_DIM <= base + 2 * LANES
        out.append((base, start - base, start - base + HEAD_DIM))
    return out


def lines_of(ref, base):
    return ref[:, 0, :, base : base + 2 * LANES].reshape(-1, 2 * LANES)


def own_columns(shape, low, high):
    lane = lax.broadcasted_iota(jnp.int32, shape, 1)
    return (lane >= low) & (lane < high)


def byte_norm_kernel(byte_ref, gain_ref, out_ref):
    out_ref[...] = (normalize(byte_ref[...])[0] * gain_ref[...]).astype(BF16)


def byte_back_kernel(
    byte_ref,
    gain_ref,
    key_ref,
    value_ref,
    grad_key_ref,
    grad_value_ref,
    grad_ref,
    gain_grad_ref,
):
    grad = dot(grad_key_ref[...], key_ref[...]) + dot(grad_value_ref[...], value_ref[...])
    normed, inv_scale = normalize(byte_ref[...])
    grad_ref[...], gain_grad = norm_back(grad, normed, inv_scale, gain_ref[...])

    @pl.when(pl.program_id(0) == 0)
    def _():
        gain_grad_ref[...] = jnp.zeros_like(gain_grad_ref)

    gain_grad_ref[...] += gain_grad


def feed_kernel(
    latents_ref,
    cotangent_ref,
    gain_ref,
    b_out_ref,
    b_up_ref,
    b_down_ref,
    out_ref,
    up_ref,
    down_ref,
    attended_ref,
    result_ref,
    mid_norm_ref,
    activated_ref,
    grad_pre_ref,
    grad_hidden_ref,
    grad_attn_ref,
    grad_att_ref,
    delta_ref,
    sums_ref,
    hidden_ref,
):
    hidden_ref[...] = latents_ref[...] + dot(attended_ref[...], out_ref[...]) + b_out_ref[...]
    mid_hat, mid_inv = normalize(hidden_ref[...])
    mid_norm_ref[...] = (mid_hat * gain_ref[...]).astype(BF16)
    pre_act = dot(mid_norm_ref[...], up_ref[...], NT) + b_up_ref[...]
    below = 0.5 * (1.0 + lax.erf(pre_act * 0.5**0.5))
    activated_ref[...] = (pre_act * below).astype(BF16)
    slope = below + pre_act * (jnp.exp(-0.5 * pre_act * pre_act) * (2.0 * jnp.pi) ** -0.5)
    grad_act = dot(cotangent_ref[...].astype(BF16), down_ref[...], NT)
    grad_pre_ref[...] = (grad_act * slope).astype(BF16)
    sums_ref[1:2, :] = jnp.sum(grad_pre_ref[...].astype(F32), axis=0, keepdims=True)
    grad_mid = dot(grad_pre_ref[...], up_ref[...])
    mid_hat, mid_inv = normalize(hidden_ref[...])
    back, gain_grad = norm_back(grad_mid, mid_hat, mid_inv, gain_ref[...])
    sums_ref[0:1, :] = gain_grad[None]
    grad_hidden_ref[...] = cotangent_ref[...] + back
    sums_ref[2:3, :] = jnp.sum(grad_hidden_ref[...], axis=0, keepdims=True)
    sums_ref[3:4, :] = jnp.sum(cotangent_ref[...], axis=0, keepdims=True)
    grad_attn_ref[...] = grad_hidden_ref[...].astype(BF16)
    grad_att_ref[...] = dot(grad_attn_ref[...], out_ref[...], NT).astype(BF16)
    for head, (base, low, high) in enumerate(windows(attended_ref.shape[1])):
        product = attended_ref[:, base : base + 2 * LANES].astype(F32) * grad_att_ref[
            :, base : base + 2 * LANES
        ].astype(F32)
        product = jnp.where(own_columns(product.shape, low, high), product, 0.0)
        delta_ref[:, head : head + 1] = jnp.sum(product, 1, keepdims=True)
    result_ref[...] = hidden_ref[...] + dot(activated_ref[...], down_ref[...]) + b_down_ref[...]


def lse_kernel(query_ref, key_ref, lat_seg_ref, byte_seg_ref, lse_ref):
    allowed = byte_seg_ref[0] == lat_seg_ref[0]
    for head, (base, low, high) in enumerate(windows(query_ref.shape[3])):
        query = lines_of(query_ref, base)
        query = jnp.where(own_columns(query.shape, low, high), query, 0)
        key = key_ref[0, :, base : base + 2 * LANES]
        scores = jnp.where(allowed, dot(key, query, NT), NEG)
        peak = jnp.max(scores, 0, keepdims=True)
        total = jnp.sum(jnp.exp(scores - peak), 0, keepdims=True)
        lse_ref[0, head : head + 1, :] = peak + jnp.log(total)


class Tiles:
    def __init__(self, ref):
        self.ref = ref
        self.held = {}

    def add(self, base, window):
        for part in range(2):
            tile = base + part * LANES
            piece = window[:, part * LANES : (part + 1) * LANES]
            self.held[tile] = self.held[tile] + piece if tile in self.held else piece
        for tile in [t for t in self.held if t < base]:
            self.store(tile)

    def store(self, tile):
        done = self.held.pop(tile).astype(self.ref.dtype)
        if len(self.ref.shape) == 4:
            self.ref[:, 0, :, tile : tile + LANES] = done.reshape(
                self.ref.shape[0], self.ref.shape[2], LANES
            )
        else:
            self.ref[0, :, tile : tile + LANES] = done

    def finish(self):
        for tile in list(self.held):
            self.store(tile)


def attend_kernel(own_lat, query_ref, key_ref, value_ref, lat_seg_ref, byte_seg_ref, *refs):
    part_refs, (out_ref, lse_ref) = refs[:-2], refs[-2:]
    parts = [part_refs[0][0]]
    for step, ref in enumerate(part_refs[1:], 1):
        parts.append(pltpu.roll(ref[0], step * own_lat, 1))
    peak = functools.reduce(jnp.maximum, parts)
    lse_ref[0] = peak + jnp.log(sum(jnp.exp(part - peak) for part in parts))
    allowed = byte_seg_ref[0] == lat_seg_ref[0]
    tiles = Tiles(out_ref)
    for head, (base, low, high) in enumerate(windows(query_ref.shape[3])):
        query = lines_of(query_ref, base)
        mine = own_columns(query.shape, low, high)
        query = jnp.where(mine, query, 0)
        key = key_ref[0, :, base : base + 2 * LANES]
        value = value_ref[0, :, base : base + 2 * LANES]
        scores = jnp.where(allowed, dot(key, query, NT), NEG)
        probs = jnp.exp(scores - lse_ref[0, head : head + 1, :]).astype(BF16)
        tiles.add(base, jnp.where(mine, dot(probs, value, TN), 0.0))
    tiles.finish()


def attend_back_kernel(
    query_ref,
    key_ref,
    value_ref,
    lat_seg_ref,
    byte_seg_ref,
    lse_ref,
    delta_ref,
    *refs,
):
    grad_refs, (grad_query_ref, grad_key_ref, grad_value_ref) = refs[:-3], refs[-3:]
    allowed = byte_seg_ref[0] == lat_seg_ref[0]
    query_tiles, key_tiles, value_tiles = (
        Tiles(grad_query_ref),
        Tiles(grad_key_ref),
        Tiles(grad_value_ref),
    )
    for head, (base, low, high) in enumerate(windows(query_ref.shape[3])):
        query = lines_of(query_ref, base)
        mine = own_columns(query.shape, low, high)
        query = jnp.where(mine, query, 0)
        grad = jnp.concatenate([ref[0, :, base : base + 2 * LANES] for ref in grad_refs])
        grad = jnp.where(mine, grad, 0)
        key = key_ref[0, :, base : base + 2 * LANES]
        value = value_ref[0, :, base : base + 2 * LANES]
        scores = jnp.where(allowed, dot(key, query, NT), NEG)
        probs = jnp.exp(scores - lse_ref[0, head : head + 1, :])
        grad_probs = dot(value, grad, NT)
        grad_scores = (probs * (grad_probs - delta_ref[0, head : head + 1, :])).astype(BF16)
        value_tiles.add(base, dot(probs.astype(BF16), grad))
        key_tiles.add(base, dot(grad_scores, query))
        query_tiles.add(base, jnp.where(mine, dot(grad_scores, key, TN), 0.0))
    query_tiles.finish()
    key_tiles.finish()
    value_tiles.finish()


def row_call(kernel, name, args, outs, flops):
    def spec(shape):
        if len(shape) == 1:
            return pl.BlockSpec(memory_space=pltpu.SMEM)
        if len(shape) == 4:
            return pl.BlockSpec((shape[0], 1, *shape[2:]), lambda row: (0, row, 0, 0))
        return pl.BlockSpec((1, *shape[1:]), lambda row: (row, 0, 0))

    moved = sum(a.size * a.dtype.itemsize for a in args)
    return pl.pallas_call(
        kernel,
        grid=(outs[-1].shape[0],),
        in_specs=[spec(a.shape) for a in args],
        out_specs=[spec(o.shape) for o in outs],
        out_shape=outs,
        name=name,
        cost_estimate=pl.CostEstimate(flops=flops // 8, bytes_accessed=moved // 8, transcendentals=0),
        compiler_params=pltpu.CompilerParams(vmem_limit_bytes=48 * 1024 * 1024),
    )(*args)


def block_call(kernel, name, lines, args, outs, flops, scratch=()):
    def spec(shape, cut):
        block = (lines if cut else shape[0], shape[1])
        return pl.BlockSpec(block, (lambda i: (i, 0)) if cut else (lambda i: (0, 0)))

    moved = sum(a.size * a.dtype.itemsize for a, _ in args)
    return pl.pallas_call(
        kernel,
        grid=(args[0][0].shape[0] // lines,),
        in_specs=[spec(a.shape, cut) for a, cut in args],
        out_specs=[spec(o.shape, cut) for o, cut in outs],
        out_shape=[o for o, _ in outs],
        scratch_shapes=list(scratch),
        name=name,
        cost_estimate=pl.CostEstimate(flops=flops // 8, bytes_accessed=moved // 8, transcendentals=0),
        compiler_params=pltpu.CompilerParams(vmem_limit_bytes=56 * 1024 * 1024),
    )(*[a for a, _ in args])


def ring(size, step=1):
    return [(i, (i + step) % size) for i in range(size)]


def add(first, *others):
    total = first.astype(F32)
    for other in others:
        total = total + other.astype(F32)
    return total.astype(first.dtype)


def panels(widths):
    return [(m, p) for m, width in enumerate(widths) for p in range(width // (2 * LANES))]


def join_kernel(widths, core_ref, mine_ref, other_ref, *out_refs):
    chips, part = mine_ref.shape[0], mine_ref.shape[3]

    def copy(sides):
        for number, (m, p) in enumerate(panels(widths)):
            for side, ref in enumerate(sides):
                at = side * widths[m] // 2 + p * LANES
                for chip in range(chips):
                    out_refs[m][chip * part : (chip + 1) * part, at : at + LANES] = ref[
                        chip, 0, number
                    ]

    @pl.when(core_ref[0] == 0)
    def _():
        copy((mine_ref, other_ref))

    @pl.when(core_ref[0] == 1)
    def _():
        copy((other_ref, mine_ref))


def join_own_kernel(widths, where_ref, *refs):
    count = len(widths)
    own_refs, (mine_ref, other_ref), out_refs = refs[:count], refs[count : count + 2], refs[count + 2 :]
    first = pl.program_id(0) == 0

    @pl.when(first)
    def _():
        for own_ref, out_ref in zip(own_refs, out_refs):
            out_ref[...] = own_ref[...]

    @pl.when(jnp.logical_not(first))
    def _():
        join_kernel(widths, where_ref, mine_ref, other_ref, *out_refs)


def grads_kernel(widths, core_ref, *refs):
    count = len(widths)
    (kept_ref, sent_ref), work_refs = refs[2 * count : 2 * count + 2], refs[2 * count + 2 :]
    chips, blocks, _, part, _ = kept_ref.shape
    for m in range(count):
        work_refs[m][...] = dot(refs[m][...], refs[count + m][...], TN).astype(BF16)

    def copy(sides):
        for number, (m, p) in enumerate(panels(widths)):
            for side, ref in enumerate(sides):
                at = side * widths[m] // 2 + p * LANES
                for block in range(blocks):
                    for chip in range(chips):
                        start = (block * chips + chip) * part
                        ref[chip, block, number] = work_refs[m][
                            start : start + part, at : at + LANES
                        ]

    @pl.when(core_ref[0] == 0)
    def _():
        copy((kept_ref, sent_ref))

    @pl.when(core_ref[0] == 1)
    def _():
        copy((sent_ref, kept_ref))


def add_kernel(a_ref, b_ref, out_ref):
    out_ref[...] = (a_ref[...].astype(F32) + b_ref[...].astype(F32)).astype(out_ref.dtype)


def split_kernel(widths, core_ref, *refs):
    in_refs, (kept_ref, sent_ref) = refs[:-2], refs[-2:]
    chips, _, _, part, _ = kept_ref.shape

    def copy(sides):
        for number, (m, p) in enumerate(panels(widths)):
            for side, ref in enumerate(sides):
                at = side * widths[m] // 2 + p * LANES
                for chip in range(chips):
                    ref[chip, 0, number] = in_refs[m][
                        chip * part : (chip + 1) * part, at : at + LANES
                    ]

    @pl.when(core_ref[0] == 0)
    def _():
        copy((kept_ref, sent_ref))

    @pl.when(core_ref[0] == 1)
    def _():
        copy((sent_ref, kept_ref))


def packed_spec(shape):
    chips, _, count, part, lanes = shape
    return pl.BlockSpec((chips, 1, count, part, lanes), lambda z: (0, z, 0, 0, 0))


def matrix_spec(lines, width):
    return pl.BlockSpec((lines, width), lambda z: (z, 0))


def join(core, mine, other, widths):
    chips, blocks, _, part, _ = mine.shape
    lines = chips * part
    return pl.pallas_call(
        functools.partial(join_kernel, widths),
        grid=(blocks,),
        in_specs=[
            pl.BlockSpec(memory_space=pltpu.SMEM),
            packed_spec(mine.shape),
            packed_spec(mine.shape),
        ],
        out_specs=[matrix_spec(lines, width) for width in widths],
        out_shape=[jax.ShapeDtypeStruct((blocks * lines, width), mine.dtype) for width in widths],
        name="join",
        cost_estimate=pl.CostEstimate(
            flops=0, bytes_accessed=mine.size, transcendentals=0
        ),
        compiler_params=pltpu.CompilerParams(vmem_limit_bytes=48 * 1024 * 1024),
    )(core, mine, other)


def join_own(where, own, mine, other, widths, total):
    chips, blocks, count, part, _ = mine.shape
    lines = chips * part

    def packed(r, where_ref):
        return (0, jnp.maximum(r, 1) - 1, 0, 0, 0)

    return pl.pallas_call(
        functools.partial(join_own_kernel, widths),
        grid_spec=pltpu.PrefetchScalarGridSpec(
            num_scalar_prefetch=1,
            grid=(blocks + 1,),
            in_specs=[pl.BlockSpec((lines, width), lambda r, where_ref: (0, 0)) for width in widths]
            + [pl.BlockSpec((chips, 1, count, part, LANES), packed)] * 2,
            out_specs=[
                pl.BlockSpec(
                    (lines, width),
                    lambda r, where_ref: (lax.rem(where_ref[1] + (total - r), total), 0),
                )
                for width in widths
            ],
        ),
        out_shape=[jax.ShapeDtypeStruct((total * lines, width), mine.dtype) for width in widths],
        name="join_own",
        cost_estimate=pl.CostEstimate(flops=0, bytes_accessed=mine.size, transcendentals=0),
        compiler_params=pltpu.CompilerParams(vmem_limit_bytes=48 * 1024 * 1024),
    )(where, *own, mine, other)


def split(core, matrices, chips, lines):
    widths = [m.shape[1] for m in matrices]
    blocks = matrices[0].shape[0] // lines
    shape = (chips, blocks, len(panels(widths)), lines // chips, LANES)
    packed = jax.ShapeDtypeStruct(shape, BF16)
    return pl.pallas_call(
        functools.partial(split_kernel, widths),
        grid=(blocks,),
        in_specs=[pl.BlockSpec(memory_space=pltpu.SMEM)]
        + [matrix_spec(lines, width) for width in widths],
        out_specs=[packed_spec(shape)] * 2,
        out_shape=[packed] * 2,
        name="split",
        cost_estimate=pl.CostEstimate(
            flops=0, bytes_accessed=sum(m.size for m in matrices) // 2, transcendentals=0
        ),
        compiler_params=pltpu.CompilerParams(vmem_limit_bytes=48 * 1024 * 1024),
    )(core, *matrices)


def add_packed(a, b):
    return pl.pallas_call(
        add_kernel,
        grid=(a.shape[1],),
        in_specs=[packed_spec(a.shape)] * 2,
        out_specs=packed_spec(a.shape),
        out_shape=jax.ShapeDtypeStruct(a.shape, a.dtype),
        name="add_packed",
        cost_estimate=pl.CostEstimate(flops=0, bytes_accessed=a.size // 2, transcendentals=0),
    )(a, b)


def grads(core, pairs, chips, lines, columns):
    widths = [rhs.shape[1] for _, rhs in pairs]
    steps = pairs[0][0].shape[1] // columns
    blocks = columns // lines
    shape = (chips, blocks * steps, len(panels(widths)), lines // chips, LANES)
    packed = jax.ShapeDtypeStruct(shape, BF16)
    block = (chips, blocks) + shape[2:]
    return pl.pallas_call(
        functools.partial(grads_kernel, widths),
        grid=(steps,),
        in_specs=[pl.BlockSpec(memory_space=pltpu.SMEM)]
        + [pl.BlockSpec((lhs.shape[0], columns), lambda i: (0, i)) for lhs, _ in pairs]
        + [pl.BlockSpec(rhs.shape, lambda i: (0, 0)) for _, rhs in pairs],
        out_specs=[pl.BlockSpec(block, lambda i: (0, i, 0, 0, 0))] * 2,
        out_shape=[packed] * 2,
        scratch_shapes=[pltpu.VMEM((columns, width), BF16) for width in widths],
        name="grads",
        cost_estimate=pl.CostEstimate(
            flops=sum(lhs.size * rhs.shape[1] for lhs, rhs in pairs) // 4,
            bytes_accessed=sum(lhs.size + rhs.size for lhs, rhs in pairs) // 4,
            transcendentals=0,
        ),
        compiler_params=pltpu.CompilerParams(vmem_limit_bytes=56 * 1024 * 1024),
    )(core, *[lhs for lhs, _ in pairs], *[rhs for _, rhs in pairs])


def after(x, *earlier):
    return lax.optimization_barrier((x, *earlier))[0]


def three_parts(x, shape):
    parts = []
    for _ in range(3):
        part = lax.reduce_precision(x, 8, 7)
        parts.append(part.astype(BF16))
        x = x - part
    parts = jnp.concatenate(parts)
    size = shape[0] * shape[1]
    return jnp.pad(parts, (0, size - parts.size)).reshape(shape)


def from_three_parts(x, size):
    parts = x.reshape(x.shape[0], -1)[:, : 3 * size].astype(F32).reshape(-1, 3, size)
    return (parts[:, 0] + (parts[:, 1] + parts[:, 2])).reshape(-1)


def pick(x, index, axis):
    return jnp.take(x, index, axis=axis, mode="clip")


class Mesh:
    def __init__(self, dp, mp):
        self.dp, self.mp = dp, mp
        self.dp_index = lax.axis_index("dp")
        self.mp_index = lax.axis_index("mp")
        self.core = self.dp_index % 2

    def cut(self, lines):
        chips = 1
        while 2 * chips <= self.dp // 2 and lines % (32 * chips) == 0:
            chips *= 2
        return chips, [2 * k for k in (1 << b for b in range(8)) if chips <= k < self.dp // 2]

    def swap(self, x, bit):
        return lax.ppermute(x, "dp", [(i, i ^ bit) for i in range(self.dp)])

    def shift(self, x, step):
        return lax.ppermute(x, "mp", ring(self.mp, step))

    def ring_gather(self, x):
        blocks = [x]
        for _ in range(self.mp - 1):
            blocks.append(self.shift(blocks[-1], 1))
        return blocks

    def ring_scatter(self, parts):
        total = parts[1] if self.mp > 1 else parts[0]
        for step in range(2, self.mp + 1):
            total = add(self.shift(total, 1), parts[step % self.mp])
        return total

    def chip_groups(self, chips):
        return [
            [2 * (chip + chips * rest) + core for chip in range(chips)]
            for rest in range(self.dp // 2 // chips)
            for core in range(2)
        ]

    def slice_of(self, shards):
        chips, _ = self.cut(shards[0].shape[0])
        part = shards[0].shape[0] // chips
        chip = self.dp_index // 2 % chips
        return jnp.concatenate(
            [
                lax.dynamic_slice(
                    shard,
                    (chip * part, self.core * (shard.shape[1] // 2)),
                    (part, shard.shape[1] // 2),
                )
                .reshape(part, -1, LANES)
                .transpose(1, 0, 2)
                for shard in shards
            ]
        )

    def gather_chips(self, x, lines):
        chips, _ = self.cut(lines)
        return lax.all_gather(x, "dp", axis=0, axis_index_groups=self.chip_groups(chips))

    def both_cores(self, own, mine):
        where = jnp.stack([self.core, self.mp_index])
        widths = [shard.shape[1] for shard in own]
        return join_own(where, own, mine, self.swap(mine, 1), widths, self.mp)

    def split_core(self, pairs, lines):
        chips, _ = self.cut(lines)
        columns = self.mp * lines // 2
        return grads(self.core[None], pairs, chips, lines, columns)

    def scatter_chips(self, total, lines):
        chips, _ = self.cut(lines)
        return lax.psum_scatter(
            total, "dp", scatter_dimension=0, axis_index_groups=self.chip_groups(chips)
        )

    def link_pieces(self, total, lines):
        chips, _ = self.cut(lines)
        bits = [1 << b for b in range(chips.bit_length() - 1)]
        middle = (total.shape[2] + 1) // 2
        return [
            (piece.reshape((2,) * len(bits) + piece.shape[1:]), order, sorted(bits, reverse=True))
            for order, piece in ((bits, total[:, :, :middle]), (bits[::-1], total[:, :, middle:]))
        ]

    def link_step(self, pieces, *earlier):
        out = []
        for piece, order, left in pieces:
            mine = self.dp_index // (2 * order[0]) % 2
            axis = left.index(order[0])
            if earlier:
                piece = after(piece, *earlier)
            sent = lax.dynamic_index_in_dim(piece, 1 - mine, axis, False)
            kept = lax.dynamic_index_in_dim(piece, mine, axis, False)
            piece = add(kept, self.swap(sent, 2 * order[0]))
            out.append((piece, order[1:], [bit for bit in left if bit != order[0]]))
        return out

    def arrays(self, pieces):
        return [piece for piece, _, _ in pieces]

    def with_arrays(self, pieces, arrays):
        return [(array, *piece[1:]) for array, piece in zip(arrays, pieces)]

    def blocks_back(self, total, lines):
        _, rest = self.cut(lines)
        for bit in rest:
            total = add(total, self.swap(total, bit))
        return [
            lax.dynamic_index_in_dim(total, (self.mp_index + self.mp - r) % self.mp, 0, False)
            for r in range(self.mp)
        ]

    def sum_blocks(self, total, lines, small=None):
        _, rest = self.cut(lines)
        for bit in rest:
            total = add(total, self.swap(total, bit))
        blocks = [
            lax.dynamic_index_in_dim(total, (self.mp_index + step) % self.mp, 0, False)
            for step in range(self.mp)
        ]
        if small is not None:
            panel = small.astype(BF16)
            panel = jnp.pad(panel, (0, total[0, 0].size - panel.size)).reshape(1, -1, LANES)
            blocks = [jnp.concatenate([block, panel]) for block in blocks]
        return add(blocks[0], *[self.shift(blocks[step], step) for step in range(1, self.mp)])

    def finish_sum(self, total, lines, widths, small=0):
        chips, rest = self.cut(lines)
        slices = [total] + [self.swap(total, 2 * k) for k in range(1, chips)]
        if small:
            panel = add(*[piece[-1] for piece in slices])
            for bit in rest:
                panel = add(panel, self.swap(panel, bit))
            slices = [jnp.concatenate([piece[:-1], panel[None]]) for piece in slices]
        chip = self.dp_index // 2 % chips
        mine = pick(jnp.stack(slices), chip ^ jnp.arange(chips), 0)[:, None]
        other = self.swap(mine, 1)
        out = join(self.core[None], mine, other, widths)
        if not small:
            return out
        panel = mine[0, 0, -1].astype(F32) + other[0, 0, -1].astype(F32)
        return out, panel.reshape(-1)[:small]

    def turned(self, x, axis):
        blocks = x.reshape(x.shape[:axis] + (self.mp, -1) + x.shape[axis + 1 :])
        index = (self.mp_index - jnp.arange(self.mp)) % self.mp
        return pick(blocks, index, axis).reshape(x.shape)


def shards(
    dp,
    mp,
    byte_in,
    latents,
    cotangent,
    byte_gain,
    latent_gain,
    mlp_gain,
    w_query,
    w_key,
    w_value,
    w_out,
    b_out,
    w_up,
    b_up,
    w_down,
    b_down,
    byte_seg,
    byte_pad,
    latent_seg,
):
    score_scale = HEAD_DIM ** (-0.5)
    rows, byte_len, byte_width = byte_in.shape
    own_lat, lat_width = latents.shape[1:]
    lat_len = own_lat * mp
    own_lines = rows * own_lat
    heads = w_query.shape[1] * mp // HEAD_DIM
    net = Mesh(dp, mp)
    mp_index = net.mp_index
    shape = jax.ShapeDtypeStruct
    lines = w_query.shape[1]
    head_widths = [lat_width, byte_width, byte_width]
    feed_widths = [lat_width] * 3

    head_own = [w_query.T, w_key.T, w_value.T]
    feed_own = [w_out, w_up.T, w_down]
    head_slice = net.slice_of(head_own)
    head_blocks = [net.shift(head_slice, step) for step in range(1, mp)]
    latents = latents.reshape(own_lines, lat_width)
    cotangent = cotangent.reshape(own_lines, lat_width)
    byte_in = byte_in.reshape(rows * byte_len, byte_width)
    lat_hat, lat_inv = normalize(latents)
    lat_norm = (lat_hat * latent_gain).astype(BF16).reshape(rows, own_lat, lat_width)
    (byte_norm,) = block_call(
        byte_norm_kernel,
        "byte_norm",
        byte_len,
        [(byte_in, True), (byte_gain[None], False)],
        [(shape(byte_in.shape, BF16), True)],
        10 * byte_in.size,
    )
    feed_slice = net.slice_of(feed_own)
    feed_slice = jnp.concatenate([feed_slice, three_parts(b_up, feed_slice.shape[1:])[None]])
    head_blocks, byte_norm, lat_norm, feed_slice = lax.optimization_barrier(
        (head_blocks, byte_norm, lat_norm, feed_slice)
    )
    head_slices = net.gather_chips(jnp.stack(head_blocks), lines)
    lat_blocks = net.ring_gather(lat_norm)
    feed_blocks = [feed_slice, net.shift(after(feed_slice, lat_blocks[-1]), 1)]
    head_slices = after(head_slices, lat_blocks[-1])
    query_t, key_t, value_t = net.both_cores(head_own, head_slices)

    real_seg = jnp.where(byte_pad == 1, byte_seg, -1)
    real_seg = lax.dynamic_slice_in_dim(real_seg, mp_index * byte_len, byte_len, 1)
    byte_col = real_seg[:, :, None]
    lat_row = net.turned(latent_seg, 1)[:, None, :]
    unit = 2 * rows * lat_len * byte_len * heads * 2 * LANES

    key_t, feed_blocks[1] = lax.optimization_barrier((key_t, feed_blocks[1]))
    feed_blocks.append(net.shift(feed_blocks[1], 1))
    keys = dot(byte_norm, key_t, NT).astype(BF16).reshape(rows, byte_len, lat_width)
    lat_all = jnp.stack(lat_blocks)
    lat_flat = after(lat_all.reshape(rows * lat_len, lat_width), keys)
    queries = (dot(lat_flat, query_t, NT) * score_scale).astype(BF16).reshape(lat_all.shape)
    queries, feed_blocks[2] = lax.optimization_barrier((queries, feed_blocks[2]))
    for _ in range(3, mp):
        feed_blocks.append(net.shift(feed_blocks[-1], 1))
    (lse_part,) = row_call(
        lse_kernel,
        "lse",
        [queries, keys, lat_row, byte_col],
        [shape((rows, heads, lat_len), F32)],
        unit,
    )
    lse_part, feed_blocks[-1] = lax.optimization_barrier((lse_part, feed_blocks[-1]))
    lse_parts = [lse_part] + [net.shift(lse_part, step) for step in range(1, mp)]
    feed_slices = net.gather_chips(jnp.stack([block[:-1] for block in feed_blocks[1:]]), lines)
    b_up_all = from_three_parts(jnp.stack([block[-1] for block in feed_blocks]), b_up.shape[0])
    b_up_all = net.turned(b_up_all, 0)
    values = dot(after(byte_norm, lse_part), value_t, NT).astype(BF16)
    values = values.reshape(rows, byte_len, lat_width)
    lat_shape = shape(lat_all.shape, BF16)
    parts, lse = row_call(
        functools.partial(attend_kernel, own_lat),
        "attend",
        [queries, keys, values, lat_row, byte_col] + lse_parts,
        [lat_shape, shape((rows, heads, lat_len), F32)],
        2 * unit,
    )
    attended = parts[1]
    for step in range(2, mp + 1):
        moved = net.shift(attended, 1)
        if step == 2:
            feed_slices = after(feed_slices, moved)
            out_w, up_t, down_w = net.both_cores(feed_own, feed_slices)
        if step == mp - 1:
            moved, out_w = lax.optimization_barrier((moved, out_w))
        attended = add(moved, parts[step % mp])
    attended = attended.reshape(own_lines, lat_width)

    whole = shape((own_lines, lat_width), BF16)
    wide = shape((own_lines, lat_width), F32)
    (
        result,
        mid_norm,
        activated,
        grad_pre,
        grad_hidden,
        grad_attn,
        grad_att,
        delta,
        feed_vectors,
    ) = block_call(
        feed_kernel,
        "feed",
        own_lines,
        [(latents, True), (cotangent, True)]
        + [(v[None], False) for v in (mlp_gain, b_out, b_up_all, b_down)]
        + [(w, False) for w in (out_w, up_t, down_w)]
        + [(attended, True)],
        [(wide, True), (whole, True), (whole, True), (whole, True), (wide, True), (whole, True)]
        + [(whole, True), (shape((own_lines, heads), F32), True)]
        + [(shape((4, lat_width), F32), False)],
        8 * own_lines * lat_width * lat_width,
        [pltpu.VMEM((own_lines, lat_width), F32)],
    )

    grads = [grad_att.reshape(rows, own_lat, lat_width)]
    block = net.shift(grads[0], 1)
    feed_kept, feed_sent = net.split_core(
        [(activated, cotangent.astype(BF16)), (grad_pre, mid_norm), (attended, grad_attn)], lines
    )
    delta = delta.reshape(rows, own_lat, heads).transpose(0, 2, 1)
    delta = jnp.concatenate([delta] + [net.shift(delta, step) for step in range(1, mp)], 2)
    block, feed_kept, feed_sent, delta = lax.optimization_barrier(
        (block, feed_kept, feed_sent, delta)
    )
    grads.append(block)
    feed_sums = add_packed(feed_kept, net.swap(feed_sent, 1))
    if mp > 2:
        block = net.shift(grads[-1], 1)
        block, feed_sums = lax.optimization_barrier((block, feed_sums))
        grads.append(block)
    for _ in range(3, mp):
        grads.append(net.shift(grads[-1], 1))
    feed_sums = net.link_pieces(feed_sums, lines)
    if feed_sums[0][1]:
        feed_sums = net.link_step(feed_sums)

    back, grad_keys, grad_values = row_call(
        attend_back_kernel,
        "attend_back",
        [queries, keys, values, lat_row, byte_col, lse, delta] + grads,
        [lat_shape] + [shape((rows, byte_len, lat_width), BF16)] * 2,
        5 * unit,
    )
    grad_keys = grad_keys.reshape(-1, lat_width)
    grad_values = grad_values.reshape(-1, lat_width)
    total = back[1]
    moved = net.shift(total, 1)
    products = [dot(grad_values, byte_norm, TN).astype(BF16)]
    while feed_sums[0][1]:
        feed_sums = net.link_step(feed_sums)
    moved, products[0], feed_half = lax.optimization_barrier(
        (moved, products[0], net.arrays(feed_sums))
    )
    feed_parts = net.blocks_back(jnp.concatenate(feed_half, 1), lines)
    feed_total = feed_parts[1]
    total = add(moved, back[2 % mp])
    grad_keys, back_flat = lax.optimization_barrier(
        (grad_keys, back.reshape(-1, lat_width), moved)
    )[:2]
    products.insert(0, dot(grad_keys, byte_norm, TN).astype(BF16))
    products.insert(0, dot(back_flat, lat_flat, TN).astype(BF16))
    kept, sent = split(net.core[None], products, net.cut(lines)[0], lines)
    if mp > 2:
        moved, feed_moved = net.shift(total, 1), net.shift(feed_total, 1)
        moved, feed_moved, sent = lax.optimization_barrier((moved, feed_moved, sent))
        total = add(moved, back[3 % mp])
        feed_total = add(feed_moved, feed_parts[2])
    head_sums = net.link_pieces(add_packed(kept, net.swap(sent, 1)), lines)
    if head_sums[0][1]:
        head_sums = net.link_step(head_sums)
    grad_bytes, grad_byte_gain = block_call(
        byte_back_kernel,
        "byte_back",
        byte_len,
        [(byte_in, True), (byte_gain[None], False), (key_t, False), (value_t, False)]
        + [(after(grad_keys, sent), True), (grad_values, True)],
        [(shape(byte_in.shape, F32), True), (shape((1, byte_width), F32), False)],
        4 * rows * byte_len * lat_width * byte_width,
    )
    if mp > 3:
        moved, feed_moved = net.shift(total, 1), net.shift(feed_total, 1)
        grad_bytes, moved, feed_moved, done = lax.optimization_barrier(
            (grad_bytes, moved, feed_moved, net.arrays(head_sums))
        )
        head_sums = net.with_arrays(head_sums, done)
        total = add(moved, back[4 % mp])
        feed_total = add(feed_moved, feed_parts[3])
    for step in range(5, mp + 1):
        total = add(net.shift(total, 1), back[step % mp])
        feed_total = add(net.shift(feed_total, 1), feed_parts[step - 1])
    while head_sums[0][1]:
        head_sums = net.link_step(head_sums)
    feed_total = add(net.shift(feed_total, 1), feed_parts[0])
    feed_total, done = lax.optimization_barrier((feed_total, net.arrays(head_sums)))
    head_sums = net.with_arrays(head_sums, done)
    feed_grads = net.finish_sum(feed_total, lines, feed_widths)
    grad_lat_norm = score_scale * dot(total.reshape(own_lines, lat_width), query_t)
    grad_lat_back, grad_latent_gain = norm_back(grad_lat_norm, lat_hat, lat_inv, latent_gain)
    grad_latents = grad_hidden + grad_lat_back
    small = jnp.concatenate([grad_byte_gain[0], grad_latent_gain, feed_vectors.reshape(-1)])
    head_sums = jnp.concatenate(net.arrays(head_sums), 1)
    head_total = net.sum_blocks(head_sums, lines, small)
    head_grads, sums = net.finish_sum(head_total, lines, head_widths, small.size)
    sums = [sums[:byte_width]] + list(sums[byte_width:].reshape(5, lat_width))
    own_units = b_up.shape[0]
    return (
        result.reshape(rows, own_lat, lat_width),
        grad_bytes.reshape(rows, byte_len, byte_width),
        grad_latents.reshape(rows, own_lat, lat_width),
        sums[0],
        sums[1],
        sums[2],
        head_grads[0].astype(F32).T * score_scale,
        head_grads[1].astype(F32).T,
        head_grads[2].astype(F32).T,
        feed_grads[2].astype(F32),
        sums[4],
        feed_grads[1].astype(F32).T,
        lax.dynamic_slice_in_dim(sums[3], mp_index * own_units, own_units, 0),
        feed_grads[0].astype(F32),
        sums[5],
    )


def solution(mesh):
    by_row = P("dp", "mp", None)
    columns, lines = P(None, "mp"), P("mp", None)
    return jax.shard_map(
        functools.partial(shards, mesh.shape["dp"], mesh.shape["mp"]),
        mesh=mesh,
        in_specs=(
            by_row,
            by_row,
            by_row,
            P(),
            P(),
            P(),
            columns,
            columns,
            columns,
            lines,
            P(),
            columns,
            P("mp"),
            lines,
            P(),
            P("dp", None),
            P("dp", None),
            P("dp", None),
        ),
        out_specs=(
            by_row,
            by_row,
            by_row,
            P(),
            P(),
            P(),
            columns,
            columns,
            columns,
            lines,
            P(),
            columns,
            P("mp"),
            lines,
            P(),
        ),
        check_vma=False,
    )
```

```python
import functools

import jax
import jax.numpy as jnp
from jax import lax
from jax.experimental import pallas as pl
from jax.experimental.pallas import tpu as pltpu
from jax.sharding import PartitionSpec as P

HEAD_DIM = 160
EPS = 1e-05
NEG = -1e30
LANES = 128
F32 = jnp.float32
BF16 = jnp.bfloat16
NN = (((1,), (0,)), ((), ()))
NT = (((1,), (1,)), ((), ()))
TN = (((0,), (0,)), ((), ()))


def dot(a, b, dims=NN):
    return lax.dot_general(a, b, dims, preferred_element_type=F32)


def normalize(field):
    average = jnp.mean(field, -1, keepdims=True)
    centred = field - average
    inv_scale = lax.rsqrt(jnp.mean(centred * centred, -1, keepdims=True) + EPS)
    return (centred * inv_scale, inv_scale)


def norm_back(grad_out, normed, inv_scale, scale_vec):
    weighted = grad_out * scale_vec
    centred_grad = (
        weighted
        - jnp.mean(weighted, -1, keepdims=True)
        - normed * jnp.mean(weighted * normed, -1, keepdims=True)
    )
    return (inv_scale * centred_grad, jnp.sum(grad_out * normed, axis=0))


def gelu_exact(field):
    return jax.nn.gelu(field, approximate=False)


def windows(columns):
    out = []
    for head in range(columns // HEAD_DIM):
        start = head * HEAD_DIM
        base = start // LANES * LANES
        assert start + HEAD_DIM <= base + 2 * LANES
        out.append((base, start - base, start - base + HEAD_DIM))
    return out


def lines_of(ref, base):
    return ref[:, 0, :, base : base + 2 * LANES].reshape(-1, 2 * LANES)


def own_columns(shape, low, high):
    lane = lax.broadcasted_iota(jnp.int32, shape, 1)
    return (lane >= low) & (lane < high)


def byte_norm_kernel(byte_ref, gain_ref, out_ref):
    out_ref[...] = (normalize(byte_ref[...])[0] * gain_ref[...]).astype(BF16)


def byte_back_kernel(
    byte_ref,
    gain_ref,
    key_ref,
    value_ref,
    grad_key_ref,
    grad_value_ref,
    grad_ref,
    gain_grad_ref,
):
    grad = dot(grad_key_ref[...], key_ref[...]) + dot(grad_value_ref[...], value_ref[...])
    normed, inv_scale = normalize(byte_ref[...])
    grad_ref[...], gain_grad = norm_back(grad, normed, inv_scale, gain_ref[...])

    @pl.when(pl.program_id(0) == 0)
    def _():
        gain_grad_ref[...] = jnp.zeros_like(gain_grad_ref)

    gain_grad_ref[...] += gain_grad


def feed_kernel(
    latents_ref,
    cotangent_ref,
    gain_ref,
    b_out_ref,
    b_up_ref,
    b_down_ref,
    out_ref,
    up_ref,
    down_ref,
    attended_ref,
    result_ref,
    mid_norm_ref,
    activated_ref,
    grad_pre_ref,
    grad_hidden_ref,
    grad_attn_ref,
    grad_att_ref,
    sums_ref,
    hidden_ref,
):
    hidden_ref[...] = latents_ref[...] + dot(attended_ref[...], out_ref[...]) + b_out_ref[...]
    mid_hat, mid_inv = normalize(hidden_ref[...])
    mid_norm_ref[...] = (mid_hat * gain_ref[...]).astype(BF16)
    pre_act = dot(mid_norm_ref[...], up_ref[...], NT) + b_up_ref[...]
    below = 0.5 * (1.0 + lax.erf(pre_act * 0.5**0.5))
    activated_ref[...] = (pre_act * below).astype(BF16)
    slope = below + pre_act * (jnp.exp(-0.5 * pre_act * pre_act) * (2.0 * jnp.pi) ** -0.5)
    grad_act = dot(cotangent_ref[...].astype(BF16), down_ref[...], NT)
    grad_pre_ref[...] = (grad_act * slope).astype(BF16)
    sums_ref[1:2, :] = jnp.sum(grad_pre_ref[...].astype(F32), axis=0, keepdims=True)
    grad_mid = dot(grad_pre_ref[...], up_ref[...])
    mid_hat, mid_inv = normalize(hidden_ref[...])
    back, gain_grad = norm_back(grad_mid, mid_hat, mid_inv, gain_ref[...])
    sums_ref[0:1, :] = gain_grad[None]
    grad_hidden_ref[...] = cotangent_ref[...] + back
    sums_ref[2:3, :] = jnp.sum(grad_hidden_ref[...], axis=0, keepdims=True)
    sums_ref[3:4, :] = jnp.sum(cotangent_ref[...], axis=0, keepdims=True)
    grad_attn_ref[...] = grad_hidden_ref[...].astype(BF16)
    width = attended_ref.shape[1]
    grad_att_ref[:, :width] = dot(grad_attn_ref[...], out_ref[...], NT).astype(BF16)
    lane = lax.broadcasted_iota(jnp.int32, (attended_ref.shape[0], LANES), 1)
    packed = jnp.zeros(lane.shape, F32)
    heads = width // HEAD_DIM
    for head, (base, low, high) in enumerate(windows(attended_ref.shape[1])):
        product = attended_ref[:, base : base + 2 * LANES].astype(F32) * grad_att_ref[
            :, base : base + 2 * LANES
        ].astype(F32)
        product = jnp.where(own_columns(product.shape, low, high), product, 0.0)
        rest = jnp.sum(product, 1, keepdims=True)
        for part in range(3):
            rounded = rest.astype(BF16).astype(F32)
            packed = jnp.where(lane == part * heads + head, rounded, packed)
            rest = rest - rounded
    grad_att_ref[:, width:] = packed.astype(BF16)
    result_ref[...] = hidden_ref[...] + dot(activated_ref[...], down_ref[...]) + b_down_ref[...]


def lse_kernel(query_ref, key_ref, lat_seg_ref, byte_seg_ref, lse_ref):
    allowed = byte_seg_ref[0] == lat_seg_ref[0]
    for head, (base, low, high) in enumerate(windows(query_ref.shape[3])):
        query = lines_of(query_ref, base)
        query = jnp.where(own_columns(query.shape, low, high), query, 0)
        key = key_ref[0, :, base : base + 2 * LANES]
        scores = jnp.where(allowed, dot(key, query, NT), NEG)
        peak = jnp.max(scores, 0, keepdims=True)
        total = jnp.sum(jnp.exp(scores - peak), 0, keepdims=True)
        lse_ref[0, head : head + 1, :] = peak + jnp.log(total)


class Tiles:
    def __init__(self, ref):
        self.ref = ref
        self.held = {}

    def add(self, base, window):
        for part in range(2):
            tile = base + part * LANES
            piece = window[:, part * LANES : (part + 1) * LANES]
            self.held[tile] = self.held[tile] + piece if tile in self.held else piece
        for tile in [t for t in self.held if t < base]:
            self.store(tile)

    def store(self, tile):
        done = self.held.pop(tile).astype(self.ref.dtype)
        if len(self.ref.shape) == 4:
            self.ref[:, 0, :, tile : tile + LANES] = done.reshape(
                self.ref.shape[0], self.ref.shape[2], LANES
            )
        else:
            self.ref[0, :, tile : tile + LANES] = done

    def finish(self):
        for tile in list(self.held):
            self.store(tile)


def attend_kernel(own_lat, query_ref, key_ref, value_ref, lat_seg_ref, byte_seg_ref, *refs):
    part_refs, (out_ref, lse_ref) = refs[:-2], refs[-2:]
    parts = [part_refs[0][0]]
    for step, ref in enumerate(part_refs[1:], 1):
        parts.append(pltpu.roll(ref[0], step * own_lat, 1))
    peak = functools.reduce(jnp.maximum, parts)
    lse_ref[0] = peak + jnp.log(sum(jnp.exp(part - peak) for part in parts))
    allowed = byte_seg_ref[0] == lat_seg_ref[0]
    tiles = Tiles(out_ref)
    for head, (base, low, high) in enumerate(windows(query_ref.shape[3])):
        query = lines_of(query_ref, base)
        mine = own_columns(query.shape, low, high)
        query = jnp.where(mine, query, 0)
        key = key_ref[0, :, base : base + 2 * LANES]
        value = value_ref[0, :, base : base + 2 * LANES]
        scores = jnp.where(allowed, dot(key, query, NT), NEG)
        probs = jnp.exp(scores - lse_ref[0, head : head + 1, :]).astype(BF16)
        tiles.add(base, jnp.where(mine, dot(probs, value, TN), 0.0))
    tiles.finish()


def attend_back_kernel(
    query_ref,
    key_ref,
    value_ref,
    lat_seg_ref,
    byte_seg_ref,
    lse_ref,
    *refs,
):
    grad_refs, (grad_query_ref, grad_key_ref, grad_value_ref) = refs[:-3], refs[-3:]
    width = query_ref.shape[3]
    heads = width // HEAD_DIM
    delta = jnp.concatenate([ref[0, :, width:] for ref in grad_refs]).astype(F32).T
    delta = delta[:heads] + (delta[heads : 2 * heads] + delta[2 * heads : 3 * heads])
    allowed = byte_seg_ref[0] == lat_seg_ref[0]
    query_tiles, key_tiles, value_tiles = (
        Tiles(grad_query_ref),
        Tiles(grad_key_ref),
        Tiles(grad_value_ref),
    )
    for head, (base, low, high) in enumerate(windows(query_ref.shape[3])):
        query = lines_of(query_ref, base)
        mine = own_columns(query.shape, low, high)
        query = jnp.where(mine, query, 0)
        grad = jnp.concatenate([ref[0, :, base : base + 2 * LANES] for ref in grad_refs])
        grad = jnp.where(mine, grad, 0)
        key = key_ref[0, :, base : base + 2 * LANES]
        value = value_ref[0, :, base : base + 2 * LANES]
        scores = jnp.where(allowed, dot(key, query, NT), NEG)
        probs = jnp.exp(scores - lse_ref[0, head : head + 1, :])
        grad_probs = dot(value, grad, NT)
        grad_scores = (probs * (grad_probs - delta[head : head + 1, :])).astype(BF16)
        value_tiles.add(base, dot(probs.astype(BF16), grad))
        key_tiles.add(base, dot(grad_scores, query))
        query_tiles.add(base, jnp.where(mine, dot(grad_scores, key, TN), 0.0))
    query_tiles.finish()
    key_tiles.finish()
    value_tiles.finish()


def row_call(kernel, name, args, outs, flops):
    def spec(shape):
        if len(shape) == 1:
            return pl.BlockSpec(memory_space=pltpu.SMEM)
        if len(shape) == 4:
            return pl.BlockSpec((shape[0], 1, *shape[2:]), lambda row: (0, row, 0, 0))
        return pl.BlockSpec((1, *shape[1:]), lambda row: (row, 0, 0))

    moved = sum(a.size * a.dtype.itemsize for a in args)
    return pl.pallas_call(
        kernel,
        grid=(outs[-1].shape[0],),
        in_specs=[spec(a.shape) for a in args],
        out_specs=[spec(o.shape) for o in outs],
        out_shape=outs,
        name=name,
        cost_estimate=pl.CostEstimate(flops=flops // 8, bytes_accessed=moved // 8, transcendentals=0),
        compiler_params=pltpu.CompilerParams(vmem_limit_bytes=48 * 1024 * 1024),
    )(*args)


def block_call(kernel, name, lines, args, outs, flops, scratch=()):
    def spec(shape, cut):
        block = (lines if cut else shape[0], shape[1])
        return pl.BlockSpec(block, (lambda i: (i, 0)) if cut else (lambda i: (0, 0)))

    moved = sum(a.size * a.dtype.itemsize for a, _ in args)
    return pl.pallas_call(
        kernel,
        grid=(args[0][0].shape[0] // lines,),
        in_specs=[spec(a.shape, cut) for a, cut in args],
        out_specs=[spec(o.shape, cut) for o, cut in outs],
        out_shape=[o for o, _ in outs],
        scratch_shapes=list(scratch),
        name=name,
        cost_estimate=pl.CostEstimate(flops=flops // 8, bytes_accessed=moved // 8, transcendentals=0),
        compiler_params=pltpu.CompilerParams(vmem_limit_bytes=56 * 1024 * 1024),
    )(*[a for a, _ in args])


def ring(size, step=1):
    return [(i, (i + step) % size) for i in range(size)]


def add(first, *others):
    total = first.astype(F32)
    for other in others:
        total = total + other.astype(F32)
    return total.astype(first.dtype)


def panels(widths):
    return [(m, p) for m, width in enumerate(widths) for p in range(width // (2 * LANES))]


def join_kernel(widths, core_ref, mine_ref, other_ref, *out_refs):
    chips, part = mine_ref.shape[0], mine_ref.shape[3]

    def copy(sides):
        for number, (m, p) in enumerate(panels(widths)):
            for side, ref in enumerate(sides):
                at = side * widths[m] // 2 + p * LANES
                for chip in range(chips):
                    out_refs[m][chip * part : (chip + 1) * part, at : at + LANES] = ref[
                        chip, 0, number
                    ].astype(out_refs[m].dtype)

    @pl.when(core_ref[0] == 0)
    def _():
        copy((mine_ref, other_ref))

    @pl.when(core_ref[0] == 1)
    def _():
        copy((other_ref, mine_ref))


def join_own_kernel(widths, where_ref, *refs):
    count = len(widths)
    own_refs, (mine_ref, other_ref), out_refs = refs[:count], refs[count : count + 2], refs[count + 2 :]
    first = pl.program_id(0) == 0

    @pl.when(first)
    def _():
        for own_ref, out_ref in zip(own_refs, out_refs):
            out_ref[...] = own_ref[...]

    @pl.when(jnp.logical_not(first))
    def _():
        join_kernel(widths, where_ref, mine_ref, other_ref, *out_refs)


def grads_kernel(widths, core_ref, *refs):
    count = len(widths)
    (kept_ref, sent_ref), work_refs = refs[2 * count : 2 * count + 2], refs[2 * count + 2 :]
    chips, blocks, _, part, _ = kept_ref.shape
    for m in range(count):
        work_refs[m][...] = dot(refs[m][...], refs[count + m][...], TN).astype(BF16)

    def copy(sides):
        for number, (m, p) in enumerate(panels(widths)):
            for side, ref in enumerate(sides):
                at = side * widths[m] // 2 + p * LANES
                for block in range(blocks):
                    for chip in range(chips):
                        start = (block * chips + chip) * part
                        ref[chip, block, number] = work_refs[m][
                            start : start + part, at : at + LANES
                        ]

    @pl.when(core_ref[0] == 0)
    def _():
        copy((kept_ref, sent_ref))

    @pl.when(core_ref[0] == 1)
    def _():
        copy((sent_ref, kept_ref))


def add_kernel(a_ref, b_ref, *out_refs):
    first = 0
    for out_ref in out_refs:
        group = slice(first, first + out_ref.shape[2])
        total = a_ref[:, :, group].astype(F32) + b_ref[:, :, group].astype(F32)
        out_ref[...] = total.astype(out_ref.dtype)
        first += out_ref.shape[2]


def split_kernel(widths, core_ref, *refs):
    in_refs, (kept_ref, sent_ref) = refs[:-2], refs[-2:]
    chips, _, _, part, _ = kept_ref.shape

    def copy(sides):
        for number, (m, p) in enumerate(panels(widths)):
            for side, ref in enumerate(sides):
                at = side * widths[m] // 2 + p * LANES
                for chip in range(chips):
                    ref[chip, 0, number] = in_refs[m][
                        chip * part : (chip + 1) * part, at : at + LANES
                    ]

    @pl.when(core_ref[0] == 0)
    def _():
        copy((kept_ref, sent_ref))

    @pl.when(core_ref[0] == 1)
    def _():
        copy((sent_ref, kept_ref))


def packed_spec(shape):
    chips, _, count, part, lanes = shape
    return pl.BlockSpec((chips, 1, count, part, lanes), lambda z: (0, z, 0, 0, 0))


def matrix_spec(lines, width):
    return pl.BlockSpec((lines, width), lambda z: (z, 0))


def join(core, mine, other, widths, kinds):
    chips, blocks, _, part, _ = mine.shape
    lines = chips * part
    return pl.pallas_call(
        functools.partial(join_kernel, widths),
        grid=(blocks,),
        in_specs=[
            pl.BlockSpec(memory_space=pltpu.SMEM),
            packed_spec(mine.shape),
            packed_spec(mine.shape),
        ],
        out_specs=[matrix_spec(lines, width) for width in widths],
        out_shape=[
            jax.ShapeDtypeStruct((blocks * lines, width), kind)
            for width, kind in zip(widths, kinds)
        ],
        name="join",
        cost_estimate=pl.CostEstimate(
            flops=0, bytes_accessed=mine.size, transcendentals=0
        ),
        compiler_params=pltpu.CompilerParams(vmem_limit_bytes=48 * 1024 * 1024),
    )(core, mine, other)


def join_own(where, own, mine, other, widths, total):
    chips, blocks, count, part, _ = mine.shape
    lines = chips * part

    def packed(r, where_ref):
        return (0, jnp.maximum(r, 1) - 1, 0, 0, 0)

    return pl.pallas_call(
        functools.partial(join_own_kernel, widths),
        grid_spec=pltpu.PrefetchScalarGridSpec(
            num_scalar_prefetch=1,
            grid=(blocks + 1,),
            in_specs=[pl.BlockSpec((lines, width), lambda r, where_ref: (0, 0)) for width in widths]
            + [pl.BlockSpec((chips, 1, count, part, LANES), packed)] * 2,
            out_specs=[
                pl.BlockSpec(
                    (lines, width),
                    lambda r, where_ref: (lax.rem(where_ref[1] + (total - r), total), 0),
                )
                for width in widths
            ],
        ),
        out_shape=[jax.ShapeDtypeStruct((total * lines, width), mine.dtype) for width in widths],
        name="join_own",
        cost_estimate=pl.CostEstimate(flops=0, bytes_accessed=mine.size, transcendentals=0),
        compiler_params=pltpu.CompilerParams(vmem_limit_bytes=48 * 1024 * 1024),
    )(where, *own, mine, other)


def split(core, matrices, chips, lines):
    widths = [m.shape[1] for m in matrices]
    blocks = matrices[0].shape[0] // lines
    shape = (chips, blocks, len(panels(widths)), lines // chips, LANES)
    packed = jax.ShapeDtypeStruct(shape, BF16)
    return pl.pallas_call(
        functools.partial(split_kernel, widths),
        grid=(blocks,),
        in_specs=[pl.BlockSpec(memory_space=pltpu.SMEM)]
        + [matrix_spec(lines, width) for width in widths],
        out_specs=[packed_spec(shape)] * 2,
        out_shape=[packed] * 2,
        name="split",
        cost_estimate=pl.CostEstimate(
            flops=0, bytes_accessed=sum(m.size for m in matrices) // 2, transcendentals=0
        ),
        compiler_params=pltpu.CompilerParams(vmem_limit_bytes=48 * 1024 * 1024),
    )(core, *matrices)


def add_packed(a, b):
    middle = (a.shape[2] + 1) // 2
    shapes = [a.shape[:2] + (count,) + a.shape[3:] for count in (middle, a.shape[2] - middle)]
    return pl.pallas_call(
        add_kernel,
        grid=(a.shape[1],),
        in_specs=[packed_spec(a.shape)] * 2,
        out_specs=[packed_spec(shape) for shape in shapes],
        out_shape=[jax.ShapeDtypeStruct(shape, a.dtype) for shape in shapes],
        name="add_packed",
        cost_estimate=pl.CostEstimate(flops=0, bytes_accessed=a.size // 2, transcendentals=0),
    )(a, b)


def grads(core, pairs, chips, lines, columns):
    widths = [rhs.shape[1] for _, rhs in pairs]
    steps = pairs[0][0].shape[1] // columns
    blocks = columns // lines
    shape = (chips, blocks * steps, len(panels(widths)), lines // chips, LANES)
    packed = jax.ShapeDtypeStruct(shape, BF16)
    block = (chips, blocks) + shape[2:]
    return pl.pallas_call(
        functools.partial(grads_kernel, widths),
        grid=(steps,),
        in_specs=[pl.BlockSpec(memory_space=pltpu.SMEM)]
        + [pl.BlockSpec((lhs.shape[0], columns), lambda i: (0, i)) for lhs, _ in pairs]
        + [pl.BlockSpec(rhs.shape, lambda i: (0, 0)) for _, rhs in pairs],
        out_specs=[pl.BlockSpec(block, lambda i: (0, i, 0, 0, 0))] * 2,
        out_shape=[packed] * 2,
        scratch_shapes=[pltpu.VMEM((columns, width), BF16) for width in widths],
        name="grads",
        cost_estimate=pl.CostEstimate(
            flops=sum(lhs.size * rhs.shape[1] for lhs, rhs in pairs) // 4,
            bytes_accessed=sum(lhs.size + rhs.size for lhs, rhs in pairs) // 4,
            transcendentals=0,
        ),
        compiler_params=pltpu.CompilerParams(vmem_limit_bytes=56 * 1024 * 1024),
    )(core, *[lhs for lhs, _ in pairs], *[rhs for _, rhs in pairs])


def after(x, *earlier):
    return lax.optimization_barrier((x, *earlier))[0]


def three_parts(x, shape):
    parts = []
    for _ in range(3):
        part = lax.reduce_precision(x, 8, 7)
        parts.append(part.astype(BF16))
        x = x - part
    parts = jnp.concatenate(parts)
    size = shape[0] * shape[1]
    return jnp.pad(parts, (0, size - parts.size)).reshape(shape)


def from_three_parts(x, size):
    parts = x.reshape(x.shape[0], -1)[:, : 3 * size].astype(F32).reshape(-1, 3, size)
    return (parts[:, 0] + (parts[:, 1] + parts[:, 2])).reshape(-1)


def pick(x, index, axis):
    return jnp.take(x, index, axis=axis, mode="clip")


class Mesh:
    def __init__(self, dp, mp):
        self.dp, self.mp = dp, mp
        self.dp_index = lax.axis_index("dp")
        self.mp_index = lax.axis_index("mp")
        self.core = self.dp_index % 2

    def cut(self, lines):
        chips = 1
        while 2 * chips <= self.dp // 2 and lines % (32 * chips) == 0:
            chips *= 2
        return chips, [2 * k for k in (1 << b for b in range(8)) if chips <= k < self.dp // 2]

    def swap(self, x, bit):
        return lax.ppermute(x, "dp", [(i, i ^ bit) for i in range(self.dp)])

    def shift(self, x, step):
        return lax.ppermute(x, "mp", ring(self.mp, step))

    def ring_gather(self, x):
        blocks = [x]
        for _ in range(self.mp - 1):
            blocks.append(self.shift(blocks[-1], 1))
        return blocks

    def ring_scatter(self, parts):
        total = parts[1] if self.mp > 1 else parts[0]
        for step in range(2, self.mp + 1):
            total = add(self.shift(total, 1), parts[step % self.mp])
        return total

    def chip_groups(self, chips):
        return [
            [2 * (chip + chips * rest) + core for chip in range(chips)]
            for rest in range(self.dp // 2 // chips)
            for core in range(2)
        ]

    def slice_of(self, shards):
        chips, _ = self.cut(shards[0].shape[0])
        part = shards[0].shape[0] // chips
        chip = self.dp_index // 2 % chips
        return jnp.concatenate(
            [
                lax.dynamic_slice(
                    shard,
                    (chip * part, self.core * (shard.shape[1] // 2)),
                    (part, shard.shape[1] // 2),
                )
                .reshape(part, -1, LANES)
                .transpose(1, 0, 2)
                for shard in shards
            ]
        )

    def gather_chips(self, x, lines):
        chips, _ = self.cut(lines)
        return lax.all_gather(x, "dp", axis=0, axis_index_groups=self.chip_groups(chips))

    def both_cores(self, own, mine, other):
        where = jnp.stack([self.core, self.mp_index])
        widths = [shard.shape[1] for shard in own]
        return join_own(where, own, mine, other, widths, self.mp)

    def split_core(self, pairs, lines):
        chips, _ = self.cut(lines)
        columns = self.mp * lines // 2
        return grads(self.core[None], pairs, chips, lines, columns)

    def scatter_chips(self, total, lines):
        chips, _ = self.cut(lines)
        return lax.psum_scatter(
            total, "dp", scatter_dimension=0, axis_index_groups=self.chip_groups(chips)
        )

    def link_pieces(self, groups, lines):
        chips, _ = self.cut(lines)
        bits = [1 << b for b in range(chips.bit_length() - 1)]
        return [
            (piece.reshape((2,) * len(bits) + piece.shape[1:]), order, sorted(bits, reverse=True))
            for order, piece in zip((bits, bits[::-1]), groups)
        ]

    def link_step(self, pieces, *earlier):
        out = []
        for piece, order, left in pieces:
            mine = self.dp_index // (2 * order[0]) % 2
            axis = left.index(order[0])
            if earlier:
                piece = after(piece, *earlier)
            sent = lax.dynamic_index_in_dim(piece, 1 - mine, axis, False)
            kept = lax.dynamic_index_in_dim(piece, mine, axis, False)
            piece = add(kept, self.swap(sent, 2 * order[0]))
            out.append((piece, order[1:], [bit for bit in left if bit != order[0]]))
        return out

    def arrays(self, pieces):
        return [piece for piece, _, _ in pieces]

    def with_arrays(self, pieces, arrays):
        return [(array, *piece[1:]) for array, piece in zip(arrays, pieces)]

    def blocks_back(self, total, lines):
        _, rest = self.cut(lines)
        for bit in rest:
            total = add(total, self.swap(total, bit))
        return [
            lax.dynamic_index_in_dim(total, (self.mp_index + self.mp - r) % self.mp, 0, False)
            for r in range(self.mp)
        ]

    def sum_blocks(self, total, lines):
        _, rest = self.cut(lines)
        for bit in rest:
            total = add(total, self.swap(total, bit))
        blocks = [
            lax.dynamic_index_in_dim(total, (self.mp_index + step) % self.mp, 0, False)
            for step in range(self.mp)
        ]
        return add(blocks[0], *[self.shift(blocks[step], step) for step in range(1, self.mp)])

    def share(self, total, lines, small=False):
        chips, rest = self.cut(lines)
        slices = [total] + [self.swap(total, 2 * k) for k in range(1, chips)]
        if small:
            panel = add(*[piece[-1] for piece in slices])
            for bit in rest:
                panel = add(panel, self.swap(panel, bit))
            slices = [jnp.concatenate([piece[:-1], panel[None]]) for piece in slices]
        chip = self.dp_index // 2 % chips
        return pick(jnp.stack(slices), chip ^ jnp.arange(chips), 0)[:, None]

    def turned(self, x, axis):
        blocks = x.reshape(x.shape[:axis] + (self.mp, -1) + x.shape[axis + 1 :])
        index = (self.mp_index - jnp.arange(self.mp)) % self.mp
        return pick(blocks, index, axis).reshape(x.shape)


def shards(
    dp,
    mp,
    byte_in,
    latents,
    cotangent,
    byte_gain,
    latent_gain,
    mlp_gain,
    w_query,
    w_key,
    w_value,
    w_out,
    b_out,
    w_up,
    b_up,
    w_down,
    b_down,
    byte_seg,
    byte_pad,
    latent_seg,
):
    score_scale = HEAD_DIM ** (-0.5)
    rows, byte_len, byte_width = byte_in.shape
    own_lat, lat_width = latents.shape[1:]
    lat_len = own_lat * mp
    own_lines = rows * own_lat
    heads = w_query.shape[1] * mp // HEAD_DIM
    net = Mesh(dp, mp)
    mp_index = net.mp_index
    shape = jax.ShapeDtypeStruct
    lines = w_query.shape[1]
    head_widths = [lat_width, byte_width, byte_width]
    feed_widths = [lat_width] * 3

    head_own = [w_query.T, w_key.T, w_value.T]
    feed_own = [w_out, w_up.T, w_down]
    head_slice = net.slice_of(head_own)
    head_blocks = [net.shift(head_slice, step) for step in range(1, mp)]
    latents = latents.reshape(own_lines, lat_width)
    cotangent = cotangent.reshape(own_lines, lat_width)
    byte_in = byte_in.reshape(rows * byte_len, byte_width)
    lat_hat, lat_inv = normalize(latents)
    lat_norm = (lat_hat * latent_gain).astype(BF16).reshape(rows, own_lat, lat_width)
    (byte_norm,) = block_call(
        byte_norm_kernel,
        "byte_norm",
        byte_len,
        [(byte_in, True), (byte_gain[None], False)],
        [(shape(byte_in.shape, BF16), True)],
        10 * byte_in.size,
    )
    feed_slice = net.slice_of(feed_own)
    feed_slice = jnp.concatenate([feed_slice, three_parts(b_up, feed_slice.shape[1:])[None]])
    head_blocks, byte_norm, lat_norm, feed_slice = lax.optimization_barrier(
        (head_blocks, byte_norm, lat_norm, feed_slice)
    )
    head_slices = net.gather_chips(jnp.stack(head_blocks), lines)
    lat_blocks = net.ring_gather(lat_norm)
    feed_blocks = [feed_slice, net.shift(after(feed_slice, lat_blocks[-1]), 1)]
    head_slices = after(head_slices, lat_blocks[-1])
    query_t, key_t, value_t = net.both_cores(head_own, head_slices, net.swap(head_slices, 1))

    real_seg = jnp.where(byte_pad == 1, byte_seg, -1)
    real_seg = lax.dynamic_slice_in_dim(real_seg, mp_index * byte_len, byte_len, 1)
    byte_col = real_seg[:, :, None]
    lat_row = net.turned(latent_seg, 1)[:, None, :]
    unit = 2 * rows * lat_len * byte_len * heads * 2 * LANES

    key_t, feed_blocks[1] = lax.optimization_barrier((key_t, feed_blocks[1]))
    feed_blocks.append(net.shift(feed_blocks[1], 1))
    keys = dot(byte_norm, key_t, NT).astype(BF16).reshape(rows, byte_len, lat_width)
    lat_all = jnp.stack(lat_blocks)
    lat_flat = after(lat_all.reshape(rows * lat_len, lat_width), keys)
    queries = (dot(lat_flat, query_t, NT) * score_scale).astype(BF16).reshape(lat_all.shape)
    (lse_part,) = row_call(
        lse_kernel,
        "lse",
        [queries, keys, lat_row, byte_col],
        [shape((rows, heads, lat_len), F32)],
        unit,
    )
    lse_part, feed_blocks[2] = lax.optimization_barrier((lse_part, feed_blocks[2]))
    for _ in range(3, mp):
        feed_blocks.append(net.shift(feed_blocks[-1], 1))
    lse_parts = [lse_part] + [net.shift(lse_part, step) for step in range(1, mp)]
    values = dot(after(byte_norm, lse_part), value_t, NT).astype(BF16)
    values = values.reshape(rows, byte_len, lat_width)
    values, feed_blocks[-1] = lax.optimization_barrier((values, feed_blocks[-1]))
    feed_slices = net.gather_chips(jnp.stack([block[:-1] for block in feed_blocks[1:]]), lines)
    b_up_all = from_three_parts(jnp.stack([block[-1] for block in feed_blocks]), b_up.shape[0])
    b_up_all = net.turned(b_up_all, 0)
    lat_shape = shape(lat_all.shape, BF16)
    parts, lse = row_call(
        functools.partial(attend_kernel, own_lat),
        "attend",
        [queries, keys, values, lat_row, byte_col] + lse_parts,
        [lat_shape, shape((rows, heads, lat_len), F32)],
        2 * unit,
    )
    attended = parts[1]
    for step in range(2, mp + 1):
        moved = net.shift(attended, 1)
        if step == mp - 1:
            feed_slices = after(feed_slices, moved)
            out_w, up_t, down_w = net.both_cores(
                feed_own, feed_slices, net.swap(feed_slices, 1)
            )
        if step == mp:
            moved, out_w = lax.optimization_barrier((moved, out_w))
        attended = add(moved, parts[step % mp])
    attended = attended.reshape(own_lines, lat_width)

    whole = shape((own_lines, lat_width), BF16)
    wide = shape((own_lines, lat_width), F32)
    (
        result,
        mid_norm,
        activated,
        grad_pre,
        grad_hidden,
        grad_attn,
        grad_att,
        feed_vectors,
    ) = block_call(
        feed_kernel,
        "feed",
        own_lines,
        [(latents, True), (cotangent, True)]
        + [(v[None], False) for v in (mlp_gain, b_out, b_up_all, b_down)]
        + [(w, False) for w in (out_w, up_t, down_w)]
        + [(attended, True)],
        [(wide, True), (whole, True), (whole, True), (whole, True), (wide, True), (whole, True)]
        + [(shape((own_lines, lat_width + LANES), BF16), True)]
        + [(shape((4, lat_width), F32), False)],
        8 * own_lines * lat_width * lat_width,
        [pltpu.VMEM((own_lines, lat_width), F32)],
    )

    grads = [grad_att.reshape(rows, own_lat, lat_width + LANES)]
    block = net.shift(grads[0], 1)
    feed_kept, feed_sent = net.split_core(
        [(activated, cotangent.astype(BF16)), (grad_pre, mid_norm), (attended, grad_attn)], lines
    )
    block, feed_kept, feed_sent = lax.optimization_barrier((block, feed_kept, feed_sent))
    grads.append(block)
    feed_sums = add_packed(feed_kept, net.swap(feed_sent, 1))
    if mp > 2:
        block = net.shift(grads[-1], 1)
        block, *feed_sums = lax.optimization_barrier((block, *feed_sums))
        grads.append(block)
    for _ in range(3, mp):
        grads.append(net.shift(grads[-1], 1))
    feed_sums = net.link_pieces(feed_sums, lines)
    if feed_sums[0][1]:
        feed_sums = net.link_step(feed_sums)

    back, grad_keys, grad_values = row_call(
        attend_back_kernel,
        "attend_back",
        [queries, keys, values, lat_row, byte_col, lse] + grads,
        [lat_shape] + [shape((rows, byte_len, lat_width), BF16)] * 2,
        5 * unit,
    )
    grad_keys = grad_keys.reshape(-1, lat_width)
    grad_values = grad_values.reshape(-1, lat_width)
    total = back[1]
    moved = net.shift(total, 1)
    products = [dot(grad, byte_norm, TN).astype(BF16) for grad in (grad_keys, grad_values)]
    while feed_sums[0][1]:
        feed_sums = net.link_step(feed_sums)
    moved, products, feed_half = lax.optimization_barrier(
        (moved, products, net.arrays(feed_sums))
    )
    feed_parts = net.blocks_back(jnp.concatenate(feed_half, 1), lines)
    feed_total = feed_parts[1]
    total = add(moved, back[2 % mp])
    back_flat = after(back.reshape(-1, lat_width), total, feed_total)
    products.insert(0, dot(back_flat, lat_flat, TN).astype(BF16))
    kept, sent = split(net.core[None], products, net.cut(lines)[0], lines)
    head_sums = add_packed(kept, net.swap(sent, 1))
    added = head_sums[0]
    feed_moved, added = lax.optimization_barrier((net.shift(feed_total, 1), added))
    feed_total = add(feed_moved, feed_parts[2 % mp])
    total = after(total, added)
    head_sums = net.link_pieces(head_sums, lines)
    if head_sums[0][1]:
        head_sums = net.link_step(head_sums)
    grad_bytes, grad_byte_gain = block_call(
        byte_back_kernel,
        "byte_back",
        byte_len,
        [(byte_in, True), (byte_gain[None], False), (key_t, False), (value_t, False)]
        + [(after(grad_keys, added), True), (grad_values, True)],
        [(shape(byte_in.shape, F32), True), (shape((1, byte_width), F32), False)],
        4 * rows * byte_len * lat_width * byte_width,
    )
    for step in range(3, mp + 1):
        if step == 4:
            total = after(total, grad_bytes)
        total = add(net.shift(total, 1), back[step % mp])
    grad_bytes, done = lax.optimization_barrier((grad_bytes, net.arrays(head_sums)))
    head_sums = net.with_arrays(head_sums, done)
    while head_sums[0][1]:
        head_sums = net.link_step(head_sums)
    for step in range(3, mp + 1):
        if step == mp:
            feed_total = after(feed_total, *net.arrays(head_sums))
        feed_total = add(net.shift(feed_total, 1), feed_parts[step % mp])
    feed_mine = net.share(feed_total, lines)
    grad_lat_norm = score_scale * dot(total.reshape(own_lines, lat_width), query_t)
    grad_lat_back, grad_latent_gain = norm_back(grad_lat_norm, lat_hat, lat_inv, latent_gain)
    grad_latents = grad_hidden + grad_lat_back
    small = jnp.concatenate([grad_byte_gain[0], grad_latent_gain, feed_vectors.reshape(-1)])
    head_sums = jnp.concatenate(net.arrays(head_sums), 1)
    head_total = net.sum_blocks(head_sums, lines)
    panel = small.astype(BF16)
    panel = jnp.pad(panel, (0, head_total[0].size - panel.size)).reshape(1, -1, LANES)
    panel = add(panel, *[net.shift(panel, step) for step in range(1, mp)])
    head_total, panel, feed_mine = lax.optimization_barrier((head_total, panel, feed_mine))
    head_mine = net.share(jnp.concatenate([head_total, panel]), lines, True)
    feed_other, head_other = net.swap(feed_mine, 1), net.swap(head_mine, 1)
    feed_grads = join(net.core[None], feed_mine, feed_other, feed_widths, [F32, BF16, F32])
    head_grads = join(net.core[None], head_mine, head_other, head_widths, [BF16] * 3)
    sums = head_mine[0, 0, -1].astype(F32) + head_other[0, 0, -1].astype(F32)
    sums = sums.reshape(-1)[: small.size]
    sums = [sums[:byte_width]] + list(sums[byte_width:].reshape(5, lat_width))
    own_units = b_up.shape[0]
    return (
        result.reshape(rows, own_lat, lat_width),
        grad_bytes.reshape(rows, byte_len, byte_width),
        grad_latents.reshape(rows, own_lat, lat_width),
        sums[0],
        sums[1],
        sums[2],
        head_grads[0].astype(F32).T * score_scale,
        head_grads[1].astype(F32).T,
        head_grads[2].astype(F32).T,
        feed_grads[2],
        sums[4],
        feed_grads[1].astype(F32).T,
        lax.dynamic_slice_in_dim(sums[3], mp_index * own_units, own_units, 0),
        feed_grads[0],
        sums[5],
    )


def solution(mesh):
    by_row = P("dp", "mp", None)
    columns, lines = P(None, "mp"), P("mp", None)
    return jax.shard_map(
        functools.partial(shards, mesh.shape["dp"], mesh.shape["mp"]),
        mesh=mesh,
        in_specs=(
            by_row,
            by_row,
            by_row,
            P(),
            P(),
            P(),
            columns,
            columns,
            columns,
            lines,
            P(),
            columns,
            P("mp"),
            lines,
            P(),
            P("dp", None),
            P("dp", None),
            P("dp", None),
        ),
        out_specs=(
            by_row,
            by_row,
            by_row,
            P(),
            P(),
            P(),
            columns,
            columns,
            columns,
            lines,
            P(),
            columns,
            P("mp"),
            lines,
            P(),
        ),
        check_vma=False,
    )
```

```python
import functools

import jax
import jax.numpy as jnp
from jax import lax
from jax.experimental import pallas as pl
from jax.experimental.pallas import tpu as pltpu
from jax.sharding import PartitionSpec as P

HEAD_DIM = 160
EPS = 1e-05
NEG = -1e30
LANES = 128
F32 = jnp.float32
BF16 = jnp.bfloat16
NN = (((1,), (0,)), ((), ()))
NT = (((1,), (1,)), ((), ()))
TN = (((0,), (0,)), ((), ()))


def dot(a, b, dims=NN):
    return lax.dot_general(a, b, dims, preferred_element_type=F32)


def normalize(field):
    average = jnp.mean(field, -1, keepdims=True)
    centred = field - average
    inv_scale = lax.rsqrt(jnp.mean(centred * centred, -1, keepdims=True) + EPS)
    return (centred * inv_scale, inv_scale)


def norm_back(grad_out, normed, inv_scale, scale_vec):
    weighted = grad_out * scale_vec
    centred_grad = (
        weighted
        - jnp.mean(weighted, -1, keepdims=True)
        - normed * jnp.mean(weighted * normed, -1, keepdims=True)
    )
    return (inv_scale * centred_grad, jnp.sum(grad_out * normed, axis=0))


def gelu_exact(field):
    return jax.nn.gelu(field, approximate=False)


def windows(columns):
    out = []
    for head in range(columns // HEAD_DIM):
        start = head * HEAD_DIM
        base = start // LANES * LANES
        assert start + HEAD_DIM <= base + 2 * LANES
        out.append((base, start - base, start - base + HEAD_DIM))
    return out


def lines_of(ref, base):
    return ref[:, 0, :, base : base + 2 * LANES].reshape(-1, 2 * LANES)


def own_columns(shape, low, high):
    lane = lax.broadcasted_iota(jnp.int32, shape, 1)
    return (lane >= low) & (lane < high)


def byte_norm_kernel(byte_ref, gain_ref, out_ref):
    out_ref[...] = (normalize(byte_ref[...])[0] * gain_ref[...]).astype(BF16)


def byte_back_kernel(
    byte_ref,
    gain_ref,
    key_ref,
    value_ref,
    grad_key_ref,
    grad_value_ref,
    grad_ref,
    gain_grad_ref,
):
    grad = dot(grad_key_ref[...], key_ref[...]) + dot(grad_value_ref[...], value_ref[...])
    normed, inv_scale = normalize(byte_ref[...])
    grad_ref[...], gain_grad = norm_back(grad, normed, inv_scale, gain_ref[...])

    @pl.when(pl.program_id(0) == 0)
    def _():
        gain_grad_ref[...] = jnp.zeros_like(gain_grad_ref)

    gain_grad_ref[...] += gain_grad


def feed_kernel(
    latents_ref,
    cotangent_ref,
    gain_ref,
    b_out_ref,
    b_up_ref,
    b_down_ref,
    out_ref,
    up_ref,
    down_ref,
    attended_ref,
    result_ref,
    mid_norm_ref,
    activated_ref,
    grad_pre_ref,
    grad_hidden_ref,
    grad_attn_ref,
    grad_att_ref,
    sums_ref,
    hidden_ref,
):
    hidden_ref[...] = latents_ref[...] + dot(attended_ref[...], out_ref[...]) + b_out_ref[...]
    mid_hat, mid_inv = normalize(hidden_ref[...])
    mid_norm_ref[...] = (mid_hat * gain_ref[...]).astype(BF16)
    pre_act = dot(mid_norm_ref[...], up_ref[...], NT) + b_up_ref[...]
    below = 0.5 * (1.0 + lax.erf(pre_act * 0.5**0.5))
    activated_ref[...] = (pre_act * below).astype(BF16)
    slope = below + pre_act * (jnp.exp(-0.5 * pre_act * pre_act) * (2.0 * jnp.pi) ** -0.5)
    grad_act = dot(cotangent_ref[...].astype(BF16), down_ref[...], NT)
    grad_pre_ref[...] = (grad_act * slope).astype(BF16)
    sums_ref[1:2, :] = jnp.sum(grad_pre_ref[...].astype(F32), axis=0, keepdims=True)
    grad_mid = dot(grad_pre_ref[...], up_ref[...])
    mid_hat, mid_inv = normalize(hidden_ref[...])
    back, gain_grad = norm_back(grad_mid, mid_hat, mid_inv, gain_ref[...])
    sums_ref[0:1, :] = gain_grad[None]
    grad_hidden_ref[...] = cotangent_ref[...] + back
    sums_ref[2:3, :] = jnp.sum(grad_hidden_ref[...], axis=0, keepdims=True)
    sums_ref[3:4, :] = jnp.sum(cotangent_ref[...], axis=0, keepdims=True)
    grad_attn_ref[...] = grad_hidden_ref[...].astype(BF16)
    width = attended_ref.shape[1]
    grad_att_ref[:, :width] = dot(grad_attn_ref[...], out_ref[...], NT).astype(BF16)
    lane = lax.broadcasted_iota(jnp.int32, (attended_ref.shape[0], LANES), 1)
    packed = jnp.zeros(lane.shape, F32)
    heads = width // HEAD_DIM
    for head, (base, low, high) in enumerate(windows(attended_ref.shape[1])):
        product = attended_ref[:, base : base + 2 * LANES].astype(F32) * grad_att_ref[
            :, base : base + 2 * LANES
        ].astype(F32)
        product = jnp.where(own_columns(product.shape, low, high), product, 0.0)
        rest = jnp.sum(product, 1, keepdims=True)
        for part in range(3):
            rounded = rest.astype(BF16).astype(F32)
            packed = jnp.where(lane == part * heads + head, rounded, packed)
            rest = rest - rounded
    grad_att_ref[:, width:] = packed.astype(BF16)
    result_ref[...] = hidden_ref[...] + dot(activated_ref[...], down_ref[...]) + b_down_ref[...]


def lse_kernel(query_ref, key_ref, lat_seg_ref, byte_seg_ref, lse_ref):
    allowed = byte_seg_ref[0] == lat_seg_ref[0]
    for head, (base, low, high) in enumerate(windows(query_ref.shape[3])):
        query = lines_of(query_ref, base)
        query = jnp.where(own_columns(query.shape, low, high), query, 0)
        key = key_ref[0, :, base : base + 2 * LANES]
        scores = jnp.where(allowed, dot(key, query, NT), NEG)
        peak = jnp.max(scores, 0, keepdims=True)
        total = jnp.sum(jnp.exp(scores - peak), 0, keepdims=True)
        lse_ref[0, head : head + 1, :] = peak + jnp.log(total)


class Tiles:
    def __init__(self, ref):
        self.ref = ref
        self.held = {}

    def add(self, base, window):
        for part in range(2):
            tile = base + part * LANES
            piece = window[:, part * LANES : (part + 1) * LANES]
            self.held[tile] = self.held[tile] + piece if tile in self.held else piece
        for tile in [t for t in self.held if t < base]:
            self.store(tile)

    def store(self, tile):
        done = self.held.pop(tile).astype(self.ref.dtype)
        if len(self.ref.shape) == 4:
            self.ref[:, 0, :, tile : tile + LANES] = done.reshape(
                self.ref.shape[0], self.ref.shape[2], LANES
            )
        else:
            self.ref[0, :, tile : tile + LANES] = done

    def finish(self):
        for tile in list(self.held):
            self.store(tile)


def attend_kernel(own_lat, query_ref, key_ref, value_ref, lat_seg_ref, byte_seg_ref, *refs):
    part_refs, (out_ref, lse_ref) = refs[:-2], refs[-2:]
    parts = [part_refs[0][0]]
    for step, ref in enumerate(part_refs[1:], 1):
        parts.append(pltpu.roll(ref[0], step * own_lat, 1))
    peak = functools.reduce(jnp.maximum, parts)
    lse_ref[0] = peak + jnp.log(sum(jnp.exp(part - peak) for part in parts))
    allowed = byte_seg_ref[0] == lat_seg_ref[0]
    tiles = Tiles(out_ref)
    for head, (base, low, high) in enumerate(windows(query_ref.shape[3])):
        query = lines_of(query_ref, base)
        mine = own_columns(query.shape, low, high)
        query = jnp.where(mine, query, 0)
        key = key_ref[0, :, base : base + 2 * LANES]
        value = value_ref[0, :, base : base + 2 * LANES]
        scores = jnp.where(allowed, dot(key, query, NT), NEG)
        probs = jnp.exp(scores - lse_ref[0, head : head + 1, :]).astype(BF16)
        tiles.add(base, jnp.where(mine, dot(probs, value, TN), 0.0))
    tiles.finish()


def attend_back_kernel(
    query_ref,
    key_ref,
    value_ref,
    lat_seg_ref,
    byte_seg_ref,
    lse_ref,
    *refs,
):
    grad_refs, (grad_query_ref, grad_key_ref, grad_value_ref) = refs[:-3], refs[-3:]
    width = query_ref.shape[3]
    heads = width // HEAD_DIM
    delta = jnp.concatenate([ref[0, :, width:] for ref in grad_refs]).astype(F32).T
    delta = delta[:heads] + (delta[heads : 2 * heads] + delta[2 * heads : 3 * heads])
    allowed = byte_seg_ref[0] == lat_seg_ref[0]
    query_tiles, key_tiles, value_tiles = (
        Tiles(grad_query_ref),
        Tiles(grad_key_ref),
        Tiles(grad_value_ref),
    )
    for head, (base, low, high) in enumerate(windows(query_ref.shape[3])):
        query = lines_of(query_ref, base)
        mine = own_columns(query.shape, low, high)
        query = jnp.where(mine, query, 0)
        grad = jnp.concatenate([ref[0, :, base : base + 2 * LANES] for ref in grad_refs])
        grad = jnp.where(mine, grad, 0)
        key = key_ref[0, :, base : base + 2 * LANES]
        value = value_ref[0, :, base : base + 2 * LANES]
        scores = jnp.where(allowed, dot(key, query, NT), NEG)
        probs = jnp.exp(scores - lse_ref[0, head : head + 1, :])
        grad_probs = dot(value, grad, NT)
        grad_scores = (probs * (grad_probs - delta[head : head + 1, :])).astype(BF16)
        value_tiles.add(base, dot(probs.astype(BF16), grad))
        key_tiles.add(base, dot(grad_scores, query))
        query_tiles.add(base, jnp.where(mine, dot(grad_scores, key, TN), 0.0))
    query_tiles.finish()
    key_tiles.finish()
    value_tiles.finish()


def row_call(kernel, name, args, outs, flops):
    def spec(shape):
        if len(shape) == 1:
            return pl.BlockSpec(memory_space=pltpu.SMEM)
        if len(shape) == 4:
            return pl.BlockSpec((shape[0], 1, *shape[2:]), lambda row: (0, row, 0, 0))
        return pl.BlockSpec((1, *shape[1:]), lambda row: (row, 0, 0))

    moved = sum(a.size * a.dtype.itemsize for a in args)
    return pl.pallas_call(
        kernel,
        grid=(outs[-1].shape[0],),
        in_specs=[spec(a.shape) for a in args],
        out_specs=[spec(o.shape) for o in outs],
        out_shape=outs,
        name=name,
        cost_estimate=pl.CostEstimate(flops=flops // 8, bytes_accessed=moved // 8, transcendentals=0),
        compiler_params=pltpu.CompilerParams(vmem_limit_bytes=48 * 1024 * 1024),
    )(*args)


def block_call(kernel, name, lines, args, outs, flops, scratch=()):
    def spec(shape, cut):
        block = (lines if cut else shape[0], shape[1])
        return pl.BlockSpec(block, (lambda i: (i, 0)) if cut else (lambda i: (0, 0)))

    moved = sum(a.size * a.dtype.itemsize for a, _ in args)
    return pl.pallas_call(
        kernel,
        grid=(args[0][0].shape[0] // lines,),
        in_specs=[spec(a.shape, cut) for a, cut in args],
        out_specs=[spec(o.shape, cut) for o, cut in outs],
        out_shape=[o for o, _ in outs],
        scratch_shapes=list(scratch),
        name=name,
        cost_estimate=pl.CostEstimate(flops=flops // 8, bytes_accessed=moved // 8, transcendentals=0),
        compiler_params=pltpu.CompilerParams(vmem_limit_bytes=56 * 1024 * 1024),
    )(*[a for a, _ in args])


def ring(size, step=1):
    return [(i, (i + step) % size) for i in range(size)]


def add(first, *others):
    total = first.astype(F32)
    for other in others:
        total = total + other.astype(F32)
    return total.astype(first.dtype)


def panels(widths):
    return [(m, p) for m, width in enumerate(widths) for p in range(width // (2 * LANES))]


def join_kernel(widths, core_ref, mine_ref, other_ref, *out_refs):
    chips, part = mine_ref.shape[0], mine_ref.shape[3]

    def copy(sides):
        for number, (m, p) in enumerate(panels(widths)):
            for side, ref in enumerate(sides):
                at = side * widths[m] // 2 + p * LANES
                for chip in range(chips):
                    out_refs[m][chip * part : (chip + 1) * part, at : at + LANES] = ref[
                        chip, 0, number
                    ].astype(out_refs[m].dtype)

    @pl.when(core_ref[0] == 0)
    def _():
        copy((mine_ref, other_ref))

    @pl.when(core_ref[0] == 1)
    def _():
        copy((other_ref, mine_ref))


def join_own_kernel(widths, where_ref, *refs):
    count = len(widths)
    own_refs, (mine_ref, other_ref), out_refs = refs[:count], refs[count : count + 2], refs[count + 2 :]
    first = pl.program_id(0) == 0

    @pl.when(first)
    def _():
        for own_ref, out_ref in zip(own_refs, out_refs):
            out_ref[...] = own_ref[...]

    @pl.when(jnp.logical_not(first))
    def _():
        join_kernel(widths, where_ref, mine_ref, other_ref, *out_refs)


def grads_kernel(widths, core_ref, *refs):
    count = len(widths)
    (kept_ref, sent_ref), work_refs = refs[2 * count : 2 * count + 2], refs[2 * count + 2 :]
    chips, blocks, _, part, _ = kept_ref.shape
    for m in range(count):
        work_refs[m][...] = dot(refs[m][...], refs[count + m][...], TN).astype(BF16)

    def copy(sides):
        for number, (m, p) in enumerate(panels(widths)):
            for side, ref in enumerate(sides):
                at = side * widths[m] // 2 + p * LANES
                for block in range(blocks):
                    for chip in range(chips):
                        start = (block * chips + chip) * part
                        ref[chip, block, number] = work_refs[m][
                            start : start + part, at : at + LANES
                        ]

    @pl.when(core_ref[0] == 0)
    def _():
        copy((kept_ref, sent_ref))

    @pl.when(core_ref[0] == 1)
    def _():
        copy((sent_ref, kept_ref))


def add_kernel(a_ref, b_ref, *out_refs):
    first = 0
    for out_ref in out_refs:
        group = slice(first, first + out_ref.shape[2])
        total = a_ref[:, :, group].astype(F32) + b_ref[:, :, group].astype(F32)
        out_ref[...] = total.astype(out_ref.dtype)
        first += out_ref.shape[2]


def split_kernel(widths, core_ref, *refs):
    in_refs, (kept_ref, sent_ref) = refs[:-2], refs[-2:]
    chips, _, _, part, _ = kept_ref.shape

    def copy(sides):
        for number, (m, p) in enumerate(panels(widths)):
            for side, ref in enumerate(sides):
                at = side * widths[m] // 2 + p * LANES
                for chip in range(chips):
                    ref[chip, 0, number] = in_refs[m][
                        chip * part : (chip + 1) * part, at : at + LANES
                    ]

    @pl.when(core_ref[0] == 0)
    def _():
        copy((kept_ref, sent_ref))

    @pl.when(core_ref[0] == 1)
    def _():
        copy((sent_ref, kept_ref))


def packed_spec(shape):
    chips, _, count, part, lanes = shape
    return pl.BlockSpec((chips, 1, count, part, lanes), lambda z: (0, z, 0, 0, 0))


def matrix_spec(lines, width):
    return pl.BlockSpec((lines, width), lambda z: (z, 0))


def join(core, mine, other, widths, kinds):
    chips, blocks, _, part, _ = mine.shape
    lines = chips * part
    return pl.pallas_call(
        functools.partial(join_kernel, widths),
        grid=(blocks,),
        in_specs=[
            pl.BlockSpec(memory_space=pltpu.SMEM),
            packed_spec(mine.shape),
            packed_spec(mine.shape),
        ],
        out_specs=[matrix_spec(lines, width) for width in widths],
        out_shape=[
            jax.ShapeDtypeStruct((blocks * lines, width), kind)
            for width, kind in zip(widths, kinds)
        ],
        name="join",
        cost_estimate=pl.CostEstimate(
            flops=0, bytes_accessed=mine.size, transcendentals=0
        ),
        compiler_params=pltpu.CompilerParams(vmem_limit_bytes=48 * 1024 * 1024),
    )(core, mine, other)


def join_own(where, own, mine, other, widths, total):
    chips, blocks, count, part, _ = mine.shape
    lines = chips * part

    def packed(r, where_ref):
        return (0, jnp.maximum(r, 1) - 1, 0, 0, 0)

    return pl.pallas_call(
        functools.partial(join_own_kernel, widths),
        grid_spec=pltpu.PrefetchScalarGridSpec(
            num_scalar_prefetch=1,
            grid=(blocks + 1,),
            in_specs=[pl.BlockSpec((lines, width), lambda r, where_ref: (0, 0)) for width in widths]
            + [pl.BlockSpec((chips, 1, count, part, LANES), packed)] * 2,
            out_specs=[
                pl.BlockSpec(
                    (lines, width),
                    lambda r, where_ref: (lax.rem(where_ref[1] + (total - r), total), 0),
                )
                for width in widths
            ],
        ),
        out_shape=[jax.ShapeDtypeStruct((total * lines, width), mine.dtype) for width in widths],
        name="join_own",
        cost_estimate=pl.CostEstimate(flops=0, bytes_accessed=mine.size, transcendentals=0),
        compiler_params=pltpu.CompilerParams(vmem_limit_bytes=48 * 1024 * 1024),
    )(where, *own, mine, other)


def split(core, matrices, chips, lines):
    widths = [m.shape[1] for m in matrices]
    blocks = matrices[0].shape[0] // lines
    shape = (chips, blocks, len(panels(widths)), lines // chips, LANES)
    packed = jax.ShapeDtypeStruct(shape, BF16)
    return pl.pallas_call(
        functools.partial(split_kernel, widths),
        grid=(blocks,),
        in_specs=[pl.BlockSpec(memory_space=pltpu.SMEM)]
        + [matrix_spec(lines, width) for width in widths],
        out_specs=[packed_spec(shape)] * 2,
        out_shape=[packed] * 2,
        name="split",
        cost_estimate=pl.CostEstimate(
            flops=0, bytes_accessed=sum(m.size for m in matrices) // 2, transcendentals=0
        ),
        compiler_params=pltpu.CompilerParams(vmem_limit_bytes=48 * 1024 * 1024),
    )(core, *matrices)


def add_packed(a, b):
    middle = (a.shape[2] + 1) // 2
    shapes = [a.shape[:2] + (count,) + a.shape[3:] for count in (middle, a.shape[2] - middle)]
    return pl.pallas_call(
        add_kernel,
        grid=(a.shape[1],),
        in_specs=[packed_spec(a.shape)] * 2,
        out_specs=[packed_spec(shape) for shape in shapes],
        out_shape=[jax.ShapeDtypeStruct(shape, a.dtype) for shape in shapes],
        name="add_packed",
        cost_estimate=pl.CostEstimate(flops=0, bytes_accessed=a.size // 2, transcendentals=0),
    )(a, b)


def grads(core, pairs, chips, lines, columns):
    widths = [rhs.shape[1] for _, rhs in pairs]
    steps = pairs[0][0].shape[1] // columns
    blocks = columns // lines
    shape = (chips, blocks * steps, len(panels(widths)), lines // chips, LANES)
    packed = jax.ShapeDtypeStruct(shape, BF16)
    block = (chips, blocks) + shape[2:]
    return pl.pallas_call(
        functools.partial(grads_kernel, widths),
        grid=(steps,),
        in_specs=[pl.BlockSpec(memory_space=pltpu.SMEM)]
        + [pl.BlockSpec((lhs.shape[0], columns), lambda i: (0, i)) for lhs, _ in pairs]
        + [pl.BlockSpec(rhs.shape, lambda i: (0, 0)) for _, rhs in pairs],
        out_specs=[pl.BlockSpec(block, lambda i: (0, i, 0, 0, 0))] * 2,
        out_shape=[packed] * 2,
        scratch_shapes=[pltpu.VMEM((columns, width), BF16) for width in widths],
        name="grads",
        cost_estimate=pl.CostEstimate(
            flops=sum(lhs.size * rhs.shape[1] for lhs, rhs in pairs) // 4,
            bytes_accessed=sum(lhs.size + rhs.size for lhs, rhs in pairs) // 4,
            transcendentals=0,
        ),
        compiler_params=pltpu.CompilerParams(vmem_limit_bytes=56 * 1024 * 1024),
    )(core, *[lhs for lhs, _ in pairs], *[rhs for _, rhs in pairs])


def after(x, *earlier):
    return lax.optimization_barrier((x, *earlier))[0]


def three_parts(x, shape):
    parts = []
    for _ in range(3):
        part = lax.reduce_precision(x, 8, 7)
        parts.append(part.astype(BF16))
        x = x - part
    parts = jnp.concatenate(parts)
    size = shape[0] * shape[1]
    return jnp.pad(parts, (0, size - parts.size)).reshape(shape)


def from_three_parts(x, size):
    parts = x.reshape(x.shape[0], -1)[:, : 3 * size].astype(F32).reshape(-1, 3, size)
    return (parts[:, 0] + (parts[:, 1] + parts[:, 2])).reshape(-1)


def pick(x, index, axis):
    return jnp.take(x, index, axis=axis, mode="clip")


class Mesh:
    def __init__(self, dp, mp):
        self.dp, self.mp = dp, mp
        self.dp_index = lax.axis_index("dp")
        self.mp_index = lax.axis_index("mp")
        self.core = self.dp_index % 2

    def cut(self, lines):
        chips = 1
        while 2 * chips <= self.dp // 2 and lines % (32 * chips) == 0:
            chips *= 2
        return chips, [2 * k for k in (1 << b for b in range(8)) if chips <= k < self.dp // 2]

    def swap(self, x, bit):
        return lax.ppermute(x, "dp", [(i, i ^ bit) for i in range(self.dp)])

    def shift(self, x, step):
        return lax.ppermute(x, "mp", ring(self.mp, step))

    def ring_gather(self, x):
        blocks = [x]
        for _ in range(self.mp - 1):
            blocks.append(self.shift(blocks[-1], 1))
        return blocks

    def ring_scatter(self, parts):
        total = parts[1] if self.mp > 1 else parts[0]
        for step in range(2, self.mp + 1):
            total = add(self.shift(total, 1), parts[step % self.mp])
        return total

    def chip_groups(self, chips):
        return [
            [2 * (chip + chips * rest) + core for chip in range(chips)]
            for rest in range(self.dp // 2 // chips)
            for core in range(2)
        ]

    def slice_of(self, shards):
        chips, _ = self.cut(shards[0].shape[0])
        part = shards[0].shape[0] // chips
        chip = self.dp_index // 2 % chips
        return jnp.concatenate(
            [
                lax.dynamic_slice(
                    shard,
                    (chip * part, self.core * (shard.shape[1] // 2)),
                    (part, shard.shape[1] // 2),
                )
                .reshape(part, -1, LANES)
                .transpose(1, 0, 2)
                for shard in shards
            ]
        )

    def gather_chips(self, x, lines):
        chips, _ = self.cut(lines)
        return lax.all_gather(x, "dp", axis=0, axis_index_groups=self.chip_groups(chips))

    def both_cores(self, own, mine, other):
        where = jnp.stack([self.core, self.mp_index])
        widths = [shard.shape[1] for shard in own]
        return join_own(where, own, mine, other, widths, self.mp)

    def split_core(self, pairs, lines):
        chips, _ = self.cut(lines)
        columns = self.mp * lines // 2
        return grads(self.core[None], pairs, chips, lines, columns)

    def scatter_chips(self, total, lines):
        chips, _ = self.cut(lines)
        return lax.psum_scatter(
            total, "dp", scatter_dimension=0, axis_index_groups=self.chip_groups(chips)
        )

    def link_pieces(self, groups, lines):
        chips, _ = self.cut(lines)
        bits = [1 << b for b in range(chips.bit_length() - 1)]
        return [
            (piece.reshape((2,) * len(bits) + piece.shape[1:]), order, sorted(bits, reverse=True))
            for order, piece in zip((bits, bits[::-1]), groups)
        ]

    def link_step(self, pieces, *earlier):
        out = []
        for piece, order, left in pieces:
            mine = self.dp_index // (2 * order[0]) % 2
            axis = left.index(order[0])
            if earlier:
                piece = after(piece, *earlier)
            sent = lax.dynamic_index_in_dim(piece, 1 - mine, axis, False)
            kept = lax.dynamic_index_in_dim(piece, mine, axis, False)
            piece = add(kept, self.swap(sent, 2 * order[0]))
            out.append((piece, order[1:], [bit for bit in left if bit != order[0]]))
        return out

    def arrays(self, pieces):
        return [piece for piece, _, _ in pieces]

    def with_arrays(self, pieces, arrays):
        return [(array, *piece[1:]) for array, piece in zip(arrays, pieces)]

    def blocks_back(self, total, lines):
        _, rest = self.cut(lines)
        for bit in rest:
            total = add(total, self.swap(total, bit))
        return [
            lax.dynamic_index_in_dim(total, (self.mp_index + self.mp - r) % self.mp, 0, False)
            for r in range(self.mp)
        ]

    def sum_blocks(self, total, lines):
        _, rest = self.cut(lines)
        for bit in rest:
            total = add(total, self.swap(total, bit))
        blocks = [
            lax.dynamic_index_in_dim(total, (self.mp_index + step) % self.mp, 0, False)
            for step in range(self.mp)
        ]
        return add(blocks[0], *[self.shift(blocks[step], step) for step in range(1, self.mp)])

    def share(self, total, lines, small=False):
        chips, rest = self.cut(lines)
        slices = [total] + [self.swap(total, 2 * k) for k in range(1, chips)]
        if small:
            panel = add(*[piece[-1] for piece in slices])
            for bit in rest:
                panel = add(panel, self.swap(panel, bit))
            slices = [jnp.concatenate([piece[:-1], panel[None]]) for piece in slices]
        chip = self.dp_index // 2 % chips
        return pick(jnp.stack(slices), chip ^ jnp.arange(chips), 0)[:, None]

    def turned(self, x, axis):
        blocks = x.reshape(x.shape[:axis] + (self.mp, -1) + x.shape[axis + 1 :])
        index = (self.mp_index - jnp.arange(self.mp)) % self.mp
        return pick(blocks, index, axis).reshape(x.shape)


def shards(
    dp,
    mp,
    byte_in,
    latents,
    cotangent,
    byte_gain,
    latent_gain,
    mlp_gain,
    w_query,
    w_key,
    w_value,
    w_out,
    b_out,
    w_up,
    b_up,
    w_down,
    b_down,
    byte_seg,
    byte_pad,
    latent_seg,
):
    score_scale = HEAD_DIM ** (-0.5)
    rows, byte_len, byte_width = byte_in.shape
    own_lat, lat_width = latents.shape[1:]
    lat_len = own_lat * mp
    own_lines = rows * own_lat
    heads = w_query.shape[1] * mp // HEAD_DIM
    net = Mesh(dp, mp)
    mp_index = net.mp_index
    shape = jax.ShapeDtypeStruct
    lines = w_query.shape[1]
    head_widths = [lat_width, byte_width, byte_width]
    feed_widths = [lat_width] * 3

    head_own = [w_query.T, w_key.T, w_value.T]
    feed_own = [w_out, w_up.T, w_down]
    head_blocks = net.ring_gather(net.slice_of(head_own))[1:]
    latents = latents.reshape(own_lines, lat_width)
    cotangent = cotangent.reshape(own_lines, lat_width)
    byte_in = byte_in.reshape(rows * byte_len, byte_width)
    lat_hat, lat_inv = normalize(latents)
    lat_norm = (lat_hat * latent_gain).astype(BF16).reshape(rows, own_lat, lat_width)
    (byte_norm,) = block_call(
        byte_norm_kernel,
        "byte_norm",
        byte_len,
        [(byte_in, True), (byte_gain[None], False)],
        [(shape(byte_in.shape, BF16), True)],
        10 * byte_in.size,
    )
    feed_slice = net.slice_of(feed_own)
    feed_slice = jnp.concatenate([feed_slice, three_parts(b_up, feed_slice.shape[1:])[None]])
    flat = [v[None] for v in (mlp_gain, b_out, b_down)]
    head_blocks[-1], byte_norm, lat_norm, feed_slice, flat = lax.optimization_barrier(
        (head_blocks[-1], byte_norm, lat_norm, feed_slice, flat)
    )
    head_slices = net.gather_chips(jnp.stack(head_blocks), lines)
    lat_blocks = net.ring_gather(lat_norm)
    feed_blocks = [feed_slice, net.shift(after(feed_slice, lat_blocks[-1]), 1)]
    head_slices = after(head_slices, lat_blocks[-1])
    query_t, key_t, value_t = net.both_cores(head_own, head_slices, net.swap(head_slices, 1))

    real_seg = jnp.where(byte_pad == 1, byte_seg, -1)
    real_seg = lax.dynamic_slice_in_dim(real_seg, mp_index * byte_len, byte_len, 1)
    byte_col = real_seg[:, :, None]
    lat_row = net.turned(latent_seg, 1)[:, None, :]
    unit = 2 * rows * lat_len * byte_len * heads * 2 * LANES

    key_t, feed_blocks[1] = lax.optimization_barrier((key_t, feed_blocks[1]))
    feed_blocks.append(net.shift(feed_blocks[1], 1))
    keys = dot(byte_norm, key_t, NT).astype(BF16).reshape(rows, byte_len, lat_width)
    lat_all = jnp.stack(lat_blocks)
    lat_flat = after(lat_all.reshape(rows * lat_len, lat_width), keys)
    queries = (dot(lat_flat, query_t, NT) * score_scale).astype(BF16).reshape(lat_all.shape)
    (lse_part,) = row_call(
        lse_kernel,
        "lse",
        [queries, keys, lat_row, byte_col],
        [shape((rows, heads, lat_len), F32)],
        unit,
    )
    lse_part, feed_blocks[2] = lax.optimization_barrier((lse_part, feed_blocks[2]))
    for _ in range(3, mp):
        feed_blocks.append(net.shift(feed_blocks[-1], 1))
    lse_parts = [lse_part] + [net.shift(lse_part, step) for step in range(1, mp)]
    values = dot(after(byte_norm, lse_part), value_t, NT).astype(BF16)
    values = values.reshape(rows, byte_len, lat_width)
    values, feed_blocks[-1] = lax.optimization_barrier((values, feed_blocks[-1]))
    feed_slices = net.gather_chips(jnp.stack([block[:-1] for block in feed_blocks[1:]]), lines)
    b_up_all = from_three_parts(jnp.stack([block[-1] for block in feed_blocks]), b_up.shape[0])
    b_up_all = net.turned(b_up_all, 0)[None]
    lat_shape = shape(lat_all.shape, BF16)
    parts, lse = row_call(
        functools.partial(attend_kernel, own_lat),
        "attend",
        [queries, keys, values, lat_row, byte_col] + lse_parts,
        [lat_shape, shape((rows, heads, lat_len), F32)],
        2 * unit,
    )
    attended = parts[1]
    for step in range(2, mp + 1):
        moved = net.shift(attended, 1)
        if step == 2:
            moved, b_up_all = lax.optimization_barrier((moved, b_up_all))
        if step == mp - 1:
            feed_slices = after(feed_slices, moved)
            out_w, up_t, down_w = net.both_cores(
                feed_own, feed_slices, net.swap(feed_slices, 1)
            )
        if step == mp:
            moved, out_w = lax.optimization_barrier((moved, out_w))
        attended = add(moved, parts[step % mp])
    attended = attended.reshape(own_lines, lat_width)

    whole = shape((own_lines, lat_width), BF16)
    wide = shape((own_lines, lat_width), F32)
    (
        result,
        mid_norm,
        activated,
        grad_pre,
        grad_hidden,
        grad_attn,
        grad_att,
        feed_vectors,
    ) = block_call(
        feed_kernel,
        "feed",
        own_lines,
        [(latents, True), (cotangent, True)]
        + [(v, False) for v in (flat[0], flat[1], b_up_all, flat[2])]
        + [(w, False) for w in (out_w, up_t, down_w)]
        + [(attended, True)],
        [(wide, True), (whole, True), (whole, True), (whole, True), (wide, True), (whole, True)]
        + [(shape((own_lines, lat_width + LANES), BF16), True)]
        + [(shape((4, lat_width), F32), False)],
        8 * own_lines * lat_width * lat_width,
        [pltpu.VMEM((own_lines, lat_width), F32)],
    )

    grads = [grad_att.reshape(rows, own_lat, lat_width + LANES)]
    block = net.shift(grads[0], 1)
    feed_kept, feed_sent = net.split_core(
        [(activated, cotangent.astype(BF16)), (grad_pre, mid_norm), (attended, grad_attn)], lines
    )
    block, feed_kept, feed_sent = lax.optimization_barrier((block, feed_kept, feed_sent))
    grads.append(block)
    feed_sums = add_packed(feed_kept, net.swap(feed_sent, 1))
    if mp > 2:
        block = net.shift(grads[-1], 1)
        block = after(block, feed_sums[0])
        grads.append(block)
    for _ in range(3, mp):
        grads.append(net.shift(grads[-1], 1))
    feed_sums = net.link_pieces(feed_sums, lines)
    if feed_sums[0][1]:
        feed_sums = net.link_step(feed_sums)

    back, grad_keys, grad_values = row_call(
        attend_back_kernel,
        "attend_back",
        [queries, keys, values, lat_row, byte_col, lse] + grads,
        [lat_shape] + [shape((rows, byte_len, lat_width), BF16)] * 2,
        5 * unit,
    )
    grad_keys = grad_keys.reshape(-1, lat_width)
    grad_values = grad_values.reshape(-1, lat_width)
    total = back[1]
    moved = net.shift(total, 1)
    products = [dot(grad, byte_norm, TN).astype(BF16) for grad in (grad_keys, grad_values)]
    while feed_sums[0][1]:
        feed_sums = net.link_step(feed_sums)
    moved, products, feed_half = lax.optimization_barrier(
        (moved, products, net.arrays(feed_sums))
    )
    feed_parts = net.blocks_back(jnp.concatenate(feed_half, 1), lines)
    feed_total = feed_parts[1]
    total = add(moved, back[2 % mp])
    back_flat = after(back.reshape(-1, lat_width), total, feed_total)
    products.insert(0, dot(back_flat, lat_flat, TN).astype(BF16))
    kept, sent = split(net.core[None], products, net.cut(lines)[0], lines)
    head_sums = add_packed(kept, net.swap(sent, 1))
    added = head_sums[0]
    feed_moved, added = lax.optimization_barrier((net.shift(feed_total, 1), added))
    feed_total = add(feed_moved, feed_parts[2 % mp])
    total = after(total, added)
    head_sums = net.link_pieces(head_sums, lines)
    if head_sums[0][1]:
        head_sums = net.link_step(head_sums)
    grad_bytes, grad_byte_gain = block_call(
        byte_back_kernel,
        "byte_back",
        byte_len,
        [(byte_in, True), (byte_gain[None], False), (key_t, False), (value_t, False)]
        + [(after(grad_keys, added), True), (grad_values, True)],
        [(shape(byte_in.shape, F32), True), (shape((1, byte_width), F32), False)],
        4 * rows * byte_len * lat_width * byte_width,
    )
    for step in range(3, mp + 1):
        if step == 4:
            total = after(total, grad_bytes)
        total = add(net.shift(total, 1), back[step % mp])
    grad_bytes, done = lax.optimization_barrier((grad_bytes, net.arrays(head_sums)))
    head_sums = net.with_arrays(head_sums, done)
    while head_sums[0][1]:
        head_sums = net.link_step(head_sums)
    for step in range(3, mp + 1):
        if step == mp:
            feed_total = after(feed_total, *net.arrays(head_sums))
        feed_total = add(net.shift(feed_total, 1), feed_parts[step % mp])
    feed_mine = net.share(feed_total, lines)
    grad_lat_norm = score_scale * dot(total.reshape(own_lines, lat_width), query_t)
    grad_lat_back, grad_latent_gain = norm_back(grad_lat_norm, lat_hat, lat_inv, latent_gain)
    grad_latents = grad_hidden + grad_lat_back
    small = jnp.concatenate([grad_byte_gain[0], grad_latent_gain, feed_vectors.reshape(-1)])
    head_sums = jnp.concatenate(net.arrays(head_sums), 1)
    head_total = net.sum_blocks(head_sums, lines)
    panel = small.astype(BF16)
    panel = jnp.pad(panel, (0, head_total[0].size - panel.size)).reshape(1, -1, LANES)
    panel = add(panel, *[net.shift(panel, step) for step in range(1, mp)])
    head_total, panel, feed_mine = lax.optimization_barrier((head_total, panel, feed_mine))
    head_mine = net.share(jnp.concatenate([head_total, panel]), lines, True)
    feed_other, head_other = net.swap(feed_mine, 1), net.swap(head_mine, 1)
    feed_grads = join(net.core[None], feed_mine, feed_other, feed_widths, [F32, BF16, F32])
    head_grads = join(net.core[None], head_mine, head_other, head_widths, [BF16] * 3)
    sums = head_mine[0, 0, -1].astype(F32) + head_other[0, 0, -1].astype(F32)
    sums = sums.reshape(-1)[: small.size]
    sums = [sums[:byte_width]] + list(sums[byte_width:].reshape(5, lat_width))
    own_units = b_up.shape[0]
    return (
        result.reshape(rows, own_lat, lat_width),
        grad_bytes.reshape(rows, byte_len, byte_width),
        grad_latents.reshape(rows, own_lat, lat_width),
        sums[0],
        sums[1],
        sums[2],
        head_grads[0].astype(F32).T * score_scale,
        head_grads[1].astype(F32).T,
        head_grads[2].astype(F32).T,
        feed_grads[2],
        sums[4],
        feed_grads[1].astype(F32).T,
        lax.dynamic_slice_in_dim(sums[3], mp_index * own_units, own_units, 0),
        feed_grads[0],
        sums[5],
    )


def solution(mesh):
    by_row = P("dp", "mp", None)
    columns, lines = P(None, "mp"), P("mp", None)
    return jax.shard_map(
        functools.partial(shards, mesh.shape["dp"], mesh.shape["mp"]),
        mesh=mesh,
        in_specs=(
            by_row,
            by_row,
            by_row,
            P(),
            P(),
            P(),
            columns,
            columns,
            columns,
            lines,
            P(),
            columns,
            P("mp"),
            lines,
            P(),
            P("dp", None),
            P("dp", None),
            P("dp", None),
        ),
        out_specs=(
            by_row,
            by_row,
            by_row,
            P(),
            P(),
            P(),
            columns,
            columns,
            columns,
            lines,
            P(),
            columns,
            P("mp"),
            lines,
            P(),
        ),
        check_vma=False,
    )
```

```python
import functools

import jax
import jax.numpy as jnp
from jax import lax
from jax.experimental import pallas as pl
from jax.experimental.pallas import tpu as pltpu
from jax.sharding import PartitionSpec as P

HEAD_DIM = 160
EPS = 1e-05
NEG = -1e30
LANES = 128
F32 = jnp.float32
BF16 = jnp.bfloat16
NN = (((1,), (0,)), ((), ()))
NT = (((1,), (1,)), ((), ()))
TN = (((0,), (0,)), ((), ()))


def dot(a, b, dims=NN):
    return lax.dot_general(a, b, dims, preferred_element_type=F32)


def normalize(field):
    average = jnp.mean(field, -1, keepdims=True)
    centred = field - average
    inv_scale = lax.rsqrt(jnp.mean(centred * centred, -1, keepdims=True) + EPS)
    return (centred * inv_scale, inv_scale)


def norm_back(grad_out, normed, inv_scale, scale_vec):
    weighted = grad_out * scale_vec
    centred_grad = (
        weighted
        - jnp.mean(weighted, -1, keepdims=True)
        - normed * jnp.mean(weighted * normed, -1, keepdims=True)
    )
    return (inv_scale * centred_grad, jnp.sum(grad_out * normed, axis=0))


def gelu_exact(field):
    return jax.nn.gelu(field, approximate=False)


def windows(columns):
    out = []
    for head in range(columns // HEAD_DIM):
        start = head * HEAD_DIM
        base = start // LANES * LANES
        assert start + HEAD_DIM <= base + 2 * LANES
        out.append((base, start - base, start - base + HEAD_DIM))
    return out


def lines_of(ref, base):
    return ref[:, 0, :, base : base + 2 * LANES].reshape(-1, 2 * LANES)


def own_columns(shape, low, high):
    lane = lax.broadcasted_iota(jnp.int32, shape, 1)
    return (lane >= low) & (lane < high)


def byte_norm_kernel(byte_ref, gain_ref, out_ref):
    out_ref[...] = (normalize(byte_ref[...])[0] * gain_ref[...]).astype(BF16)


def byte_back_kernel(
    byte_ref,
    gain_ref,
    key_ref,
    value_ref,
    grad_key_ref,
    grad_value_ref,
    grad_ref,
    gain_grad_ref,
):
    grad = dot(grad_key_ref[...], key_ref[...]) + dot(grad_value_ref[...], value_ref[...])
    normed, inv_scale = normalize(byte_ref[...])
    grad_ref[...], gain_grad = norm_back(grad, normed, inv_scale, gain_ref[...])

    @pl.when(pl.program_id(0) == 0)
    def _():
        gain_grad_ref[...] = jnp.zeros_like(gain_grad_ref)

    gain_grad_ref[...] += gain_grad


def feed_kernel(
    latents_ref,
    cotangent_ref,
    gain_ref,
    b_out_ref,
    b_up_ref,
    b_down_ref,
    out_ref,
    up_ref,
    down_ref,
    attended_ref,
    result_ref,
    mid_norm_ref,
    activated_ref,
    grad_pre_ref,
    grad_hidden_ref,
    grad_attn_ref,
    grad_att_ref,
    sums_ref,
    hidden_ref,
):
    hidden_ref[...] = latents_ref[...] + dot(attended_ref[...], out_ref[...]) + b_out_ref[...]
    mid_hat, mid_inv = normalize(hidden_ref[...])
    mid_norm_ref[...] = (mid_hat * gain_ref[...]).astype(BF16)
    pre_act = dot(mid_norm_ref[...], up_ref[...], NT) + b_up_ref[...]
    below = 0.5 * (1.0 + lax.erf(pre_act * 0.5**0.5))
    activated_ref[...] = (pre_act * below).astype(BF16)
    slope = below + pre_act * (jnp.exp(-0.5 * pre_act * pre_act) * (2.0 * jnp.pi) ** -0.5)
    grad_act = dot(cotangent_ref[...].astype(BF16), down_ref[...], NT)
    grad_pre_ref[...] = (grad_act * slope).astype(BF16)
    sums_ref[1:2, :] = jnp.sum(grad_pre_ref[...].astype(F32), axis=0, keepdims=True)
    grad_mid = dot(grad_pre_ref[...], up_ref[...])
    mid_hat, mid_inv = normalize(hidden_ref[...])
    back, gain_grad = norm_back(grad_mid, mid_hat, mid_inv, gain_ref[...])
    sums_ref[0:1, :] = gain_grad[None]
    grad_hidden_ref[...] = cotangent_ref[...] + back
    sums_ref[2:3, :] = jnp.sum(grad_hidden_ref[...], axis=0, keepdims=True)
    sums_ref[3:4, :] = jnp.sum(cotangent_ref[...], axis=0, keepdims=True)
    grad_attn_ref[...] = grad_hidden_ref[...].astype(BF16)
    width = attended_ref.shape[1]
    grad_att_ref[:, :width] = dot(grad_attn_ref[...], out_ref[...], NT).astype(BF16)
    lane = lax.broadcasted_iota(jnp.int32, (attended_ref.shape[0], LANES), 1)
    packed = jnp.zeros(lane.shape, F32)
    heads = width // HEAD_DIM
    for head, (base, low, high) in enumerate(windows(attended_ref.shape[1])):
        product = attended_ref[:, base : base + 2 * LANES].astype(F32) * grad_att_ref[
            :, base : base + 2 * LANES
        ].astype(F32)
        product = jnp.where(own_columns(product.shape, low, high), product, 0.0)
        rest = jnp.sum(product, 1, keepdims=True)
        for part in range(3):
            rounded = rest.astype(BF16).astype(F32)
            packed = jnp.where(lane == part * heads + head, rounded, packed)
            rest = rest - rounded
    grad_att_ref[:, width:] = packed.astype(BF16)
    result_ref[...] = hidden_ref[...] + dot(activated_ref[...], down_ref[...]) + b_down_ref[...]


def lse_kernel(query_ref, key_ref, lat_seg_ref, byte_seg_ref, lse_ref):
    allowed = byte_seg_ref[0] == lat_seg_ref[0]
    for head, (base, low, high) in enumerate(windows(query_ref.shape[3])):
        query = lines_of(query_ref, base)
        query = jnp.where(own_columns(query.shape, low, high), query, 0)
        key = key_ref[0, :, base : base + 2 * LANES]
        scores = jnp.where(allowed, dot(key, query, NT), NEG)
        peak = jnp.max(scores, 0, keepdims=True)
        total = jnp.sum(jnp.exp(scores - peak), 0, keepdims=True)
        lse_ref[0, head : head + 1, :] = peak + jnp.log(total)


class Tiles:
    def __init__(self, ref):
        self.ref = ref
        self.held = {}

    def add(self, base, window):
        for part in range(2):
            tile = base + part * LANES
            piece = window[:, part * LANES : (part + 1) * LANES]
            self.held[tile] = self.held[tile] + piece if tile in self.held else piece
        for tile in [t for t in self.held if t < base]:
            self.store(tile)

    def store(self, tile):
        done = self.held.pop(tile).astype(self.ref.dtype)
        if len(self.ref.shape) == 4:
            self.ref[:, 0, :, tile : tile + LANES] = done.reshape(
                self.ref.shape[0], self.ref.shape[2], LANES
            )
        else:
            self.ref[0, :, tile : tile + LANES] = done

    def finish(self):
        for tile in list(self.held):
            self.store(tile)


def attend_kernel(own_lat, query_ref, key_ref, value_ref, lat_seg_ref, byte_seg_ref, *refs):
    part_refs, (out_ref, lse_ref) = refs[:-2], refs[-2:]
    parts = [part_refs[0][0]]
    for step, ref in enumerate(part_refs[1:], 1):
        parts.append(pltpu.roll(ref[0], step * own_lat, 1))
    peak = functools.reduce(jnp.maximum, parts)
    lse_ref[0] = peak + jnp.log(sum(jnp.exp(part - peak) for part in parts))
    allowed = byte_seg_ref[0] == lat_seg_ref[0]
    tiles = Tiles(out_ref)
    for head, (base, low, high) in enumerate(windows(query_ref.shape[3])):
        query = lines_of(query_ref, base)
        mine = own_columns(query.shape, low, high)
        query = jnp.where(mine, query, 0)
        key = key_ref[0, :, base : base + 2 * LANES]
        value = value_ref[0, :, base : base + 2 * LANES]
        scores = jnp.where(allowed, dot(key, query, NT), NEG)
        probs = jnp.exp(scores - lse_ref[0, head : head + 1, :]).astype(BF16)
        tiles.add(base, jnp.where(mine, dot(probs, value, TN), 0.0))
    tiles.finish()


def attend_back_kernel(
    query_ref,
    key_ref,
    value_ref,
    lat_seg_ref,
    byte_seg_ref,
    lse_ref,
    *refs,
):
    grad_refs, (grad_query_ref, grad_key_ref, grad_value_ref) = refs[:-3], refs[-3:]
    width = query_ref.shape[3]
    heads = width // HEAD_DIM
    delta = jnp.concatenate([ref[0, :, width:] for ref in grad_refs]).astype(F32).T
    delta = delta[:heads] + (delta[heads : 2 * heads] + delta[2 * heads : 3 * heads])
    allowed = byte_seg_ref[0] == lat_seg_ref[0]
    query_tiles, key_tiles, value_tiles = (
        Tiles(grad_query_ref),
        Tiles(grad_key_ref),
        Tiles(grad_value_ref),
    )
    for head, (base, low, high) in enumerate(windows(query_ref.shape[3])):
        query = lines_of(query_ref, base)
        mine = own_columns(query.shape, low, high)
        query = jnp.where(mine, query, 0)
        grad = jnp.concatenate([ref[0, :, base : base + 2 * LANES] for ref in grad_refs])
        grad = jnp.where(mine, grad, 0)
        key = key_ref[0, :, base : base + 2 * LANES]
        value = value_ref[0, :, base : base + 2 * LANES]
        scores = jnp.where(allowed, dot(key, query, NT), NEG)
        probs = jnp.exp(scores - lse_ref[0, head : head + 1, :])
        grad_probs = dot(value, grad, NT)
        grad_scores = (probs * (grad_probs - delta[head : head + 1, :])).astype(BF16)
        value_tiles.add(base, dot(probs.astype(BF16), grad))
        key_tiles.add(base, dot(grad_scores, query))
        query_tiles.add(base, jnp.where(mine, dot(grad_scores, key, TN), 0.0))
    query_tiles.finish()
    key_tiles.finish()
    value_tiles.finish()


def row_call(kernel, name, args, outs, flops):
    def spec(shape):
        if len(shape) == 1:
            return pl.BlockSpec(memory_space=pltpu.SMEM)
        if len(shape) == 4:
            return pl.BlockSpec((shape[0], 1, *shape[2:]), lambda row: (0, row, 0, 0))
        return pl.BlockSpec((1, *shape[1:]), lambda row: (row, 0, 0))

    moved = sum(a.size * a.dtype.itemsize for a in args)
    return pl.pallas_call(
        kernel,
        grid=(outs[-1].shape[0],),
        in_specs=[spec(a.shape) for a in args],
        out_specs=[spec(o.shape) for o in outs],
        out_shape=outs,
        name=name,
        cost_estimate=pl.CostEstimate(flops=flops, bytes_accessed=moved, transcendentals=0),
        compiler_params=pltpu.CompilerParams(vmem_limit_bytes=48 * 1024 * 1024),
    )(*args)


def block_call(kernel, name, lines, args, outs, flops, scratch=()):
    def spec(shape, cut):
        block = (lines if cut else shape[0], shape[1])
        return pl.BlockSpec(block, (lambda i: (i, 0)) if cut else (lambda i: (0, 0)))

    moved = sum(a.size * a.dtype.itemsize for a, _ in args)
    return pl.pallas_call(
        kernel,
        grid=(args[0][0].shape[0] // lines,),
        in_specs=[spec(a.shape, cut) for a, cut in args],
        out_specs=[spec(o.shape, cut) for o, cut in outs],
        out_shape=[o for o, _ in outs],
        scratch_shapes=list(scratch),
        name=name,
        cost_estimate=pl.CostEstimate(flops=flops, bytes_accessed=moved, transcendentals=0),
        compiler_params=pltpu.CompilerParams(vmem_limit_bytes=56 * 1024 * 1024),
    )(*[a for a, _ in args])


def ring(size, step=1):
    return [(i, (i + step) % size) for i in range(size)]


def add(first, *others):
    total = first.astype(F32)
    for other in others:
        total = total + other.astype(F32)
    return total.astype(first.dtype)


def panels(widths):
    return [(m, p) for m, width in enumerate(widths) for p in range(width // (2 * LANES))]


def join_kernel(widths, core_ref, mine_ref, other_ref, *out_refs):
    chips, part = mine_ref.shape[0], mine_ref.shape[3]

    def copy(sides):
        for number, (m, p) in enumerate(panels(widths)):
            for side, ref in enumerate(sides):
                at = side * widths[m] // 2 + p * LANES
                for chip in range(chips):
                    out_refs[m][chip * part : (chip + 1) * part, at : at + LANES] = ref[
                        chip, 0, number
                    ].astype(out_refs[m].dtype)

    @pl.when(core_ref[0] == 0)
    def _():
        copy((mine_ref, other_ref))

    @pl.when(core_ref[0] == 1)
    def _():
        copy((other_ref, mine_ref))


def join_own_kernel(widths, where_ref, *refs):
    count = len(widths)
    own_refs, (mine_ref, other_ref), out_refs = refs[:count], refs[count : count + 2], refs[count + 2 :]
    first = pl.program_id(0) == 0

    @pl.when(first)
    def _():
        for own_ref, out_ref in zip(own_refs, out_refs):
            out_ref[...] = own_ref[...]

    @pl.when(jnp.logical_not(first))
    def _():
        join_kernel(widths, where_ref, mine_ref, other_ref, *out_refs)


def grads_kernel(widths, core_ref, *refs):
    count = len(widths)
    (kept_ref, sent_ref), work_refs = refs[2 * count : 2 * count + 2], refs[2 * count + 2 :]
    chips, blocks, _, part, _ = kept_ref.shape
    for m in range(count):
        work_refs[m][...] = dot(refs[m][...], refs[count + m][...], TN).astype(BF16)

    def copy(sides):
        for number, (m, p) in enumerate(panels(widths)):
            for side, ref in enumerate(sides):
                at = side * widths[m] // 2 + p * LANES
                for block in range(blocks):
                    for chip in range(chips):
                        start = (block * chips + chip) * part
                        ref[chip, block, number] = work_refs[m][
                            start : start + part, at : at + LANES
                        ]

    @pl.when(core_ref[0] == 0)
    def _():
        copy((kept_ref, sent_ref))

    @pl.when(core_ref[0] == 1)
    def _():
        copy((sent_ref, kept_ref))


def add_kernel(a_ref, b_ref, *out_refs):
    first = 0
    for out_ref in out_refs:
        group = slice(first, first + out_ref.shape[2])
        total = a_ref[:, :, group].astype(F32) + b_ref[:, :, group].astype(F32)
        out_ref[...] = total.astype(out_ref.dtype)
        first += out_ref.shape[2]


def split_kernel(widths, core_ref, *refs):
    in_refs, (kept_ref, sent_ref) = refs[:-2], refs[-2:]
    chips, _, _, part, _ = kept_ref.shape

    def copy(sides):
        for number, (m, p) in enumerate(panels(widths)):
            for side, ref in enumerate(sides):
                at = side * widths[m] // 2 + p * LANES
                for chip in range(chips):
                    ref[chip, 0, number] = in_refs[m][
                        chip * part : (chip + 1) * part, at : at + LANES
                    ]

    @pl.when(core_ref[0] == 0)
    def _():
        copy((kept_ref, sent_ref))

    @pl.when(core_ref[0] == 1)
    def _():
        copy((sent_ref, kept_ref))


def packed_spec(shape):
    chips, _, count, part, lanes = shape
    return pl.BlockSpec((chips, 1, count, part, lanes), lambda z: (0, z, 0, 0, 0))


def matrix_spec(lines, width):
    return pl.BlockSpec((lines, width), lambda z: (z, 0))


def join(core, mine, other, widths, kinds):
    chips, blocks, _, part, _ = mine.shape
    lines = chips * part
    return pl.pallas_call(
        functools.partial(join_kernel, widths),
        grid=(blocks,),
        in_specs=[
            pl.BlockSpec(memory_space=pltpu.SMEM),
            packed_spec(mine.shape),
            packed_spec(mine.shape),
        ],
        out_specs=[matrix_spec(lines, width) for width in widths],
        out_shape=[
            jax.ShapeDtypeStruct((blocks * lines, width), kind)
            for width, kind in zip(widths, kinds)
        ],
        name="join",
        cost_estimate=pl.CostEstimate(
            flops=0, bytes_accessed=mine.size, transcendentals=0
        ),
        compiler_params=pltpu.CompilerParams(vmem_limit_bytes=48 * 1024 * 1024),
    )(core, mine, other)


def join_own(where, own, mine, other, widths, total):
    chips, blocks, count, part, _ = mine.shape
    lines = chips * part

    def packed(r, where_ref):
        return (0, jnp.maximum(r, 1) - 1, 0, 0, 0)

    return pl.pallas_call(
        functools.partial(join_own_kernel, widths),
        grid_spec=pltpu.PrefetchScalarGridSpec(
            num_scalar_prefetch=1,
            grid=(blocks + 1,),
            in_specs=[pl.BlockSpec((lines, width), lambda r, where_ref: (0, 0)) for width in widths]
            + [pl.BlockSpec((chips, 1, count, part, LANES), packed)] * 2,
            out_specs=[
                pl.BlockSpec(
                    (lines, width),
                    lambda r, where_ref: (lax.rem(where_ref[1] + (total - r), total), 0),
                )
                for width in widths
            ],
        ),
        out_shape=[jax.ShapeDtypeStruct((total * lines, width), mine.dtype) for width in widths],
        name="join_own",
        cost_estimate=pl.CostEstimate(flops=0, bytes_accessed=mine.size, transcendentals=0),
        compiler_params=pltpu.CompilerParams(vmem_limit_bytes=48 * 1024 * 1024),
    )(where, *own, mine, other)


def split(core, matrices, chips, lines):
    widths = [m.shape[1] for m in matrices]
    blocks = matrices[0].shape[0] // lines
    shape = (chips, blocks, len(panels(widths)), lines // chips, LANES)
    packed = jax.ShapeDtypeStruct(shape, BF16)
    return pl.pallas_call(
        functools.partial(split_kernel, widths),
        grid=(blocks,),
        in_specs=[pl.BlockSpec(memory_space=pltpu.SMEM)]
        + [matrix_spec(lines, width) for width in widths],
        out_specs=[packed_spec(shape)] * 2,
        out_shape=[packed] * 2,
        name="split",
        cost_estimate=pl.CostEstimate(
            flops=0, bytes_accessed=sum(m.size for m in matrices) // 2, transcendentals=0
        ),
        compiler_params=pltpu.CompilerParams(vmem_limit_bytes=48 * 1024 * 1024),
    )(core, *matrices)


def add_packed(a, b):
    middle = (a.shape[2] + 1) // 2
    shapes = [a.shape[:2] + (count,) + a.shape[3:] for count in (middle, a.shape[2] - middle)]
    return pl.pallas_call(
        add_kernel,
        grid=(a.shape[1],),
        in_specs=[packed_spec(a.shape)] * 2,
        out_specs=[packed_spec(shape) for shape in shapes],
        out_shape=[jax.ShapeDtypeStruct(shape, a.dtype) for shape in shapes],
        name="add_packed",
        cost_estimate=pl.CostEstimate(flops=0, bytes_accessed=a.size // 2, transcendentals=0),
    )(a, b)


def grads(core, pairs, chips, lines, columns):
    widths = [rhs.shape[1] for _, rhs in pairs]
    steps = pairs[0][0].shape[1] // columns
    blocks = columns // lines
    shape = (chips, blocks * steps, len(panels(widths)), lines // chips, LANES)
    packed = jax.ShapeDtypeStruct(shape, BF16)
    block = (chips, blocks) + shape[2:]
    return pl.pallas_call(
        functools.partial(grads_kernel, widths),
        grid=(steps,),
        in_specs=[pl.BlockSpec(memory_space=pltpu.SMEM)]
        + [pl.BlockSpec((lhs.shape[0], columns), lambda i: (0, i)) for lhs, _ in pairs]
        + [pl.BlockSpec(rhs.shape, lambda i: (0, 0)) for _, rhs in pairs],
        out_specs=[pl.BlockSpec(block, lambda i: (0, i, 0, 0, 0))] * 2,
        out_shape=[packed] * 2,
        scratch_shapes=[pltpu.VMEM((columns, width), BF16) for width in widths],
        name="grads",
        cost_estimate=pl.CostEstimate(
            flops=sum(lhs.size * rhs.shape[1] for lhs, rhs in pairs) // 4,
            bytes_accessed=sum(lhs.size + rhs.size for lhs, rhs in pairs) // 4,
            transcendentals=0,
        ),
        compiler_params=pltpu.CompilerParams(vmem_limit_bytes=56 * 1024 * 1024),
    )(core, *[lhs for lhs, _ in pairs], *[rhs for _, rhs in pairs])


def after(x, *earlier):
    return lax.optimization_barrier((x, *earlier))[0]


def three_parts(x, shape):
    parts = []
    for _ in range(3):
        part = lax.reduce_precision(x, 8, 7)
        parts.append(part.astype(BF16))
        x = x - part
    parts = jnp.concatenate(parts)
    size = shape[0] * shape[1]
    return jnp.pad(parts, (0, size - parts.size)).reshape(shape)


def from_three_parts(x, size):
    parts = x.reshape(x.shape[0], -1)[:, : 3 * size].astype(F32).reshape(-1, 3, size)
    return (parts[:, 0] + (parts[:, 1] + parts[:, 2])).reshape(-1)


def pick(x, index, axis):
    return jnp.take(x, index, axis=axis, mode="clip")


class Mesh:
    def __init__(self, dp, mp):
        self.dp, self.mp = dp, mp
        self.dp_index = lax.axis_index("dp")
        self.mp_index = lax.axis_index("mp")
        self.core = self.dp_index % 2

    def cut(self, lines):
        chips = 1
        while 2 * chips <= self.dp // 2 and lines % (32 * chips) == 0:
            chips *= 2
        return chips, [2 * k for k in (1 << b for b in range(8)) if chips <= k < self.dp // 2]

    def swap(self, x, bit):
        return lax.ppermute(x, "dp", [(i, i ^ bit) for i in range(self.dp)])

    def shift(self, x, step):
        return lax.ppermute(x, "mp", ring(self.mp, step))

    def ring_gather(self, x):
        blocks = [x]
        for _ in range(self.mp - 1):
            blocks.append(self.shift(blocks[-1], 1))
        return blocks

    def ring_scatter(self, parts):
        total = parts[1] if self.mp > 1 else parts[0]
        for step in range(2, self.mp + 1):
            total = add(self.shift(total, 1), parts[step % self.mp])
        return total

    def chip_groups(self, chips):
        return [
            [2 * (chip + chips * rest) + core for chip in range(chips)]
            for rest in range(self.dp // 2 // chips)
            for core in range(2)
        ]

    def slice_of(self, shards):
        chips, _ = self.cut(shards[0].shape[0])
        part = shards[0].shape[0] // chips
        chip = self.dp_index // 2 % chips
        return jnp.concatenate(
            [
                lax.dynamic_slice(
                    shard,
                    (chip * part, self.core * (shard.shape[1] // 2)),
                    (part, shard.shape[1] // 2),
                )
                .reshape(part, -1, LANES)
                .transpose(1, 0, 2)
                for shard in shards
            ]
        )

    def gather_chips(self, x, lines):
        chips, _ = self.cut(lines)
        return lax.all_gather(x, "dp", axis=0, axis_index_groups=self.chip_groups(chips))

    def both_cores(self, own, mine, other):
        where = jnp.stack([self.core, self.mp_index])
        widths = [shard.shape[1] for shard in own]
        return join_own(where, own, mine, other, widths, self.mp)

    def split_core(self, pairs, lines):
        chips, _ = self.cut(lines)
        columns = self.mp * lines // 2
        return grads(self.core[None], pairs, chips, lines, columns)

    def scatter_chips(self, total, lines):
        chips, _ = self.cut(lines)
        return lax.psum_scatter(
            total, "dp", scatter_dimension=0, axis_index_groups=self.chip_groups(chips)
        )

    def link_pieces(self, groups, lines):
        chips, _ = self.cut(lines)
        bits = [1 << b for b in range(chips.bit_length() - 1)]
        return [
            (piece.reshape((2,) * len(bits) + piece.shape[1:]), order, sorted(bits, reverse=True))
            for order, piece in zip((bits, bits[::-1]), groups)
        ]

    def link_step(self, pieces, *earlier):
        out = []
        for piece, order, left in pieces:
            mine = self.dp_index // (2 * order[0]) % 2
            axis = left.index(order[0])
            if earlier:
                piece = after(piece, *earlier)
            sent = lax.dynamic_index_in_dim(piece, 1 - mine, axis, False)
            kept = lax.dynamic_index_in_dim(piece, mine, axis, False)
            piece = add(kept, self.swap(sent, 2 * order[0]))
            out.append((piece, order[1:], [bit for bit in left if bit != order[0]]))
        return out

    def arrays(self, pieces):
        return [piece for piece, _, _ in pieces]

    def with_arrays(self, pieces, arrays):
        return [(array, *piece[1:]) for array, piece in zip(arrays, pieces)]

    def blocks_back(self, total, lines):
        _, rest = self.cut(lines)
        for bit in rest:
            total = add(total, self.swap(total, bit))
        return [
            lax.dynamic_index_in_dim(total, (self.mp_index + self.mp - r) % self.mp, 0, False)
            for r in range(self.mp)
        ]

    def sum_blocks(self, total, lines):
        _, rest = self.cut(lines)
        for bit in rest:
            total = add(total, self.swap(total, bit))
        blocks = [
            lax.dynamic_index_in_dim(total, (self.mp_index + step) % self.mp, 0, False)
            for step in range(self.mp)
        ]
        return add(blocks[0], *[self.shift(blocks[step], step) for step in range(1, self.mp)])

    def share(self, total, lines, small=False):
        chips, rest = self.cut(lines)
        slices = [total] + [self.swap(total, 2 * k) for k in range(1, chips)]
        if small:
            panel = add(*[piece[-1] for piece in slices])
            for bit in rest:
                panel = add(panel, self.swap(panel, bit))
            slices = [jnp.concatenate([piece[:-1], panel[None]]) for piece in slices]
        chip = self.dp_index // 2 % chips
        return pick(jnp.stack(slices), chip ^ jnp.arange(chips), 0)[:, None]

    def turned(self, x, axis):
        blocks = x.reshape(x.shape[:axis] + (self.mp, -1) + x.shape[axis + 1 :])
        index = (self.mp_index - jnp.arange(self.mp)) % self.mp
        return pick(blocks, index, axis).reshape(x.shape)


def shards(
    dp,
    mp,
    byte_in,
    latents,
    cotangent,
    byte_gain,
    latent_gain,
    mlp_gain,
    w_query,
    w_key,
    w_value,
    w_out,
    b_out,
    w_up,
    b_up,
    w_down,
    b_down,
    byte_seg,
    byte_pad,
    latent_seg,
):
    score_scale = HEAD_DIM ** (-0.5)
    rows, byte_len, byte_width = byte_in.shape
    own_lat, lat_width = latents.shape[1:]
    lat_len = own_lat * mp
    own_lines = rows * own_lat
    heads = w_query.shape[1] * mp // HEAD_DIM
    net = Mesh(dp, mp)
    mp_index = net.mp_index
    shape = jax.ShapeDtypeStruct
    lines = w_query.shape[1]
    head_widths = [lat_width, byte_width, byte_width]
    feed_widths = [lat_width] * 3

    head_own = [w_query.T, w_key.T, w_value.T]
    feed_own = [w_out, w_up.T, w_down]
    head_blocks = net.ring_gather(net.slice_of(head_own))[1:]
    latents = latents.reshape(own_lines, lat_width)
    cotangent = cotangent.reshape(own_lines, lat_width)
    byte_in = byte_in.reshape(rows * byte_len, byte_width)
    lat_hat, lat_inv = normalize(latents)
    lat_norm = (lat_hat * latent_gain).astype(BF16).reshape(rows, own_lat, lat_width)
    (byte_norm,) = block_call(
        byte_norm_kernel,
        "byte_norm",
        byte_len,
        [(byte_in, True), (byte_gain[None], False)],
        [(shape(byte_in.shape, BF16), True)],
        10 * byte_in.size,
    )
    feed_slice = net.slice_of(feed_own)
    feed_slice = jnp.concatenate([feed_slice, three_parts(b_up, feed_slice.shape[1:])[None]])
    flat = [v[None] for v in (mlp_gain, b_out, b_down)]
    head_blocks[-1], byte_norm, lat_norm, feed_slice, flat = lax.optimization_barrier(
        (head_blocks[-1], byte_norm, lat_norm, feed_slice, flat)
    )
    head_slices = net.gather_chips(jnp.stack(head_blocks), lines)
    lat_blocks = net.ring_gather(lat_norm)
    feed_blocks = [feed_slice, net.shift(after(feed_slice, lat_blocks[-1]), 1)]
    head_slices = after(head_slices, lat_blocks[-1])
    query_t, key_t, value_t = net.both_cores(head_own, head_slices, net.swap(head_slices, 1))

    real_seg = jnp.where(byte_pad == 1, byte_seg, -1)
    real_seg = lax.dynamic_slice_in_dim(real_seg, mp_index * byte_len, byte_len, 1)
    byte_col = real_seg[:, :, None]
    lat_row = net.turned(latent_seg, 1)[:, None, :]
    unit = 2 * rows * lat_len * byte_len * heads * 2 * LANES

    key_t, feed_blocks[1] = lax.optimization_barrier((key_t, feed_blocks[1]))
    feed_blocks.append(net.shift(feed_blocks[1], 1))
    keys = dot(byte_norm, key_t, NT).astype(BF16).reshape(rows, byte_len, lat_width)
    lat_all = jnp.stack(lat_blocks)
    lat_flat = after(lat_all.reshape(rows * lat_len, lat_width), keys)
    queries = (dot(lat_flat, query_t, NT) * score_scale).astype(BF16).reshape(lat_all.shape)
    (lse_part,) = row_call(
        lse_kernel,
        "lse",
        [queries, keys, lat_row, byte_col],
        [shape((rows, heads, lat_len), F32)],
        unit,
    )
    lse_part, feed_blocks[2] = lax.optimization_barrier((lse_part, feed_blocks[2]))
    for _ in range(3, mp):
        feed_blocks.append(net.shift(feed_blocks[-1], 1))
    lse_parts = [lse_part] + [net.shift(lse_part, step) for step in range(1, mp)]
    values = dot(after(byte_norm, lse_part), value_t, NT).astype(BF16)
    values = values.reshape(rows, byte_len, lat_width)
    values, feed_blocks[-1] = lax.optimization_barrier((values, feed_blocks[-1]))
    feed_slices = net.gather_chips(jnp.stack([block[:-1] for block in feed_blocks[1:]]), lines)
    b_up_all = from_three_parts(jnp.stack([block[-1] for block in feed_blocks]), b_up.shape[0])
    b_up_all = net.turned(b_up_all, 0)[None]
    lat_shape = shape(lat_all.shape, BF16)
    parts, lse = row_call(
        functools.partial(attend_kernel, own_lat),
        "attend",
        [queries, keys, values, lat_row, byte_col] + lse_parts,
        [lat_shape, shape((rows, heads, lat_len), F32)],
        2 * unit,
    )
    attended = parts[1]
    for step in range(2, mp + 1):
        moved = net.shift(attended, 1)
        if step == 2:
            moved, b_up_all = lax.optimization_barrier((moved, b_up_all))
        if step == mp - 1:
            feed_slices = after(feed_slices, moved)
            out_w, up_t, down_w = net.both_cores(
                feed_own, feed_slices, net.swap(feed_slices, 1)
            )
        if step == mp:
            moved, out_w = lax.optimization_barrier((moved, out_w))
        attended = add(moved, parts[step % mp])
    attended = attended.reshape(own_lines, lat_width)

    whole = shape((own_lines, lat_width), BF16)
    wide = shape((own_lines, lat_width), F32)
    (
        result,
        mid_norm,
        activated,
        grad_pre,
        grad_hidden,
        grad_attn,
        grad_att,
        feed_vectors,
    ) = block_call(
        feed_kernel,
        "feed",
        own_lines,
        [(latents, True), (cotangent, True)]
        + [(v, False) for v in (flat[0], flat[1], b_up_all, flat[2])]
        + [(w, False) for w in (out_w, up_t, down_w)]
        + [(attended, True)],
        [(wide, True), (whole, True), (whole, True), (whole, True), (wide, True), (whole, True)]
        + [(shape((own_lines, lat_width + LANES), BF16), True)]
        + [(shape((4, lat_width), F32), False)],
        8 * own_lines * lat_width * lat_width,
        [pltpu.VMEM((own_lines, lat_width), F32)],
    )

    grads = [grad_att.reshape(rows, own_lat, lat_width + LANES)]
    block = net.shift(grads[0], 1)
    feed_kept, feed_sent = net.split_core(
        [(activated, cotangent.astype(BF16)), (grad_pre, mid_norm), (attended, grad_attn)], lines
    )
    block, feed_kept, feed_sent = lax.optimization_barrier((block, feed_kept, feed_sent))
    grads.append(block)
    feed_sums = add_packed(feed_kept, net.swap(feed_sent, 1))
    if mp > 2:
        block = net.shift(grads[-1], 1)
        block = after(block, feed_sums[0])
        grads.append(block)
    for _ in range(3, mp):
        grads.append(net.shift(grads[-1], 1))
    feed_sums = net.link_pieces(feed_sums, lines)
    if feed_sums[0][1]:
        feed_sums = net.link_step(feed_sums)

    back, grad_keys, grad_values = row_call(
        attend_back_kernel,
        "attend_back",
        [queries, keys, values, lat_row, byte_col, lse] + grads,
        [lat_shape] + [shape((rows, byte_len, lat_width), BF16)] * 2,
        5 * unit,
    )
    grad_keys = grad_keys.reshape(-1, lat_width)
    grad_values = grad_values.reshape(-1, lat_width)
    total = back[1]
    moved = net.shift(total, 1)
    products = [dot(grad, byte_norm, TN).astype(BF16) for grad in (grad_keys, grad_values)]
    while feed_sums[0][1]:
        feed_sums = net.link_step(feed_sums)
    moved, products, feed_half = lax.optimization_barrier(
        (moved, products, net.arrays(feed_sums))
    )
    feed_parts = net.blocks_back(jnp.concatenate(feed_half, 1), lines)
    feed_total = feed_parts[1]
    total = add(moved, back[2 % mp])
    back_flat = after(back.reshape(-1, lat_width), total, feed_total)
    products.insert(0, dot(back_flat, lat_flat, TN).astype(BF16))
    kept, sent = split(net.core[None], products, net.cut(lines)[0], lines)
    head_sums = add_packed(kept, net.swap(sent, 1))
    added = head_sums[0]
    feed_moved, added = lax.optimization_barrier((net.shift(feed_total, 1), added))
    feed_total = add(feed_moved, feed_parts[2 % mp])
    total = after(total, added)
    head_sums = net.link_pieces(head_sums, lines)
    if head_sums[0][1]:
        head_sums = net.link_step(head_sums)
    grad_bytes, grad_byte_gain = block_call(
        byte_back_kernel,
        "byte_back",
        byte_len,
        [(byte_in, True), (byte_gain[None], False), (key_t, False), (value_t, False)]
        + [(after(grad_keys, added), True), (grad_values, True)],
        [(shape(byte_in.shape, F32), True), (shape((1, byte_width), F32), False)],
        4 * rows * byte_len * lat_width * byte_width,
    )
    for step in range(3, mp + 1):
        if step == 4:
            total = after(total, grad_bytes)
        total = add(net.shift(total, 1), back[step % mp])
    grad_bytes, done = lax.optimization_barrier((grad_bytes, net.arrays(head_sums)))
    head_sums = net.with_arrays(head_sums, done)
    while head_sums[0][1]:
        head_sums = net.link_step(head_sums)
    for step in range(3, mp + 1):
        if step == mp:
            feed_total = after(feed_total, *net.arrays(head_sums))
        feed_total = add(net.shift(feed_total, 1), feed_parts[step % mp])
    feed_mine = net.share(feed_total, lines)
    grad_lat_norm = score_scale * dot(total.reshape(own_lines, lat_width), query_t)
    grad_lat_back, grad_latent_gain = norm_back(grad_lat_norm, lat_hat, lat_inv, latent_gain)
    grad_latents = grad_hidden + grad_lat_back
    small = jnp.concatenate([grad_byte_gain[0], grad_latent_gain, feed_vectors.reshape(-1)])
    head_sums = jnp.concatenate(net.arrays(head_sums), 1)
    head_total = net.sum_blocks(head_sums, lines)
    panel = small.astype(BF16)
    panel = jnp.pad(panel, (0, head_total[0].size - panel.size)).reshape(1, -1, LANES)
    panel = add(panel, *[net.shift(panel, step) for step in range(1, mp)])
    head_total, panel, feed_mine = lax.optimization_barrier((head_total, panel, feed_mine))
    head_mine = net.share(jnp.concatenate([head_total, panel]), lines, True)
    feed_other, head_other = net.swap(feed_mine, 1), net.swap(head_mine, 1)
    feed_grads = join(net.core[None], feed_mine, feed_other, feed_widths, [F32, BF16, F32])
    head_grads = join(net.core[None], head_mine, head_other, head_widths, [BF16] * 3)
    sums = head_mine[0, 0, -1].astype(F32) + head_other[0, 0, -1].astype(F32)
    sums = sums.reshape(-1)[: small.size]
    sums = [sums[:byte_width]] + list(sums[byte_width:].reshape(5, lat_width))
    own_units = b_up.shape[0]
    return (
        result.reshape(rows, own_lat, lat_width),
        grad_bytes.reshape(rows, byte_len, byte_width),
        grad_latents.reshape(rows, own_lat, lat_width),
        sums[0],
        sums[1],
        sums[2],
        head_grads[0].astype(F32).T * score_scale,
        head_grads[1].astype(F32).T,
        head_grads[2].astype(F32).T,
        feed_grads[2],
        sums[4],
        feed_grads[1].astype(F32).T,
        lax.dynamic_slice_in_dim(sums[3], mp_index * own_units, own_units, 0),
        feed_grads[0],
        sums[5],
    )


def solution(mesh):
    by_row = P("dp", "mp", None)
    columns, lines = P(None, "mp"), P("mp", None)
    return jax.shard_map(
        functools.partial(shards, mesh.shape["dp"], mesh.shape["mp"]),
        mesh=mesh,
        in_specs=(
            by_row,
            by_row,
            by_row,
            P(),
            P(),
            P(),
            columns,
            columns,
            columns,
            lines,
            P(),
            columns,
            P("mp"),
            lines,
            P(),
            P("dp", None),
            P("dp", None),
            P("dp", None),
        ),
        out_specs=(
            by_row,
            by_row,
            by_row,
            P(),
            P(),
            P(),
            columns,
            columns,
            columns,
            lines,
            P(),
            columns,
            P("mp"),
            lines,
            P(),
        ),
        check_vma=False,
    )
```

```python
import functools

import jax
import jax.numpy as jnp
from jax import lax
from jax.experimental import pallas as pl
from jax.experimental.pallas import tpu as pltpu
from jax.sharding import PartitionSpec as P

HEAD_DIM = 160
EPS = 1e-05
NEG = -1e30
LANES = 128
F32 = jnp.float32
BF16 = jnp.bfloat16
NN = (((1,), (0,)), ((), ()))
NT = (((1,), (1,)), ((), ()))
TN = (((0,), (0,)), ((), ()))


def dot(a, b, dims=NN):
    return lax.dot_general(a, b, dims, preferred_element_type=F32)


def normalize(field):
    average = jnp.mean(field, -1, keepdims=True)
    centred = field - average
    inv_scale = lax.rsqrt(jnp.mean(centred * centred, -1, keepdims=True) + EPS)
    return (centred * inv_scale, inv_scale)


def norm_back(grad_out, normed, inv_scale, scale_vec):
    weighted = grad_out * scale_vec
    centred_grad = (
        weighted
        - jnp.mean(weighted, -1, keepdims=True)
        - normed * jnp.mean(weighted * normed, -1, keepdims=True)
    )
    return (inv_scale * centred_grad, jnp.sum(grad_out * normed, axis=0))


def gelu_exact(field):
    return jax.nn.gelu(field, approximate=False)


def windows(columns):
    out = []
    for head in range(columns // HEAD_DIM):
        start = head * HEAD_DIM
        base = start // LANES * LANES
        assert start + HEAD_DIM <= base + 2 * LANES
        out.append((base, start - base, start - base + HEAD_DIM))
    return out


def lines_of(ref, base):
    return ref[:, 0, :, base : base + 2 * LANES].reshape(-1, 2 * LANES)


def own_columns(shape, low, high):
    lane = lax.broadcasted_iota(jnp.int32, shape, 1)
    return (lane >= low) & (lane < high)


def byte_norm_kernel(byte_ref, gain_ref, out_ref):
    out_ref[...] = (normalize(byte_ref[...])[0] * gain_ref[...]).astype(BF16)


def byte_back_kernel(
    byte_ref,
    gain_ref,
    key_ref,
    value_ref,
    grad_key_ref,
    grad_value_ref,
    grad_ref,
    gain_grad_ref,
):
    grad = dot(grad_key_ref[...], key_ref[...]) + dot(grad_value_ref[...], value_ref[...])
    normed, inv_scale = normalize(byte_ref[...])
    grad_ref[...], gain_grad = norm_back(grad, normed, inv_scale, gain_ref[...])

    @pl.when(pl.program_id(0) == 0)
    def _():
        gain_grad_ref[...] = jnp.zeros_like(gain_grad_ref)

    gain_grad_ref[...] += gain_grad


def feed_kernel(
    latents_ref,
    cotangent_ref,
    gain_ref,
    b_out_ref,
    b_up_ref,
    b_down_ref,
    out_ref,
    up_ref,
    down_ref,
    attended_ref,
    result_ref,
    mid_norm_ref,
    activated_ref,
    grad_pre_ref,
    grad_hidden_ref,
    grad_attn_ref,
    grad_att_ref,
    sums_ref,
    hidden_ref,
):
    hidden_ref[...] = latents_ref[...] + dot(attended_ref[...], out_ref[...]) + b_out_ref[...]
    mid_hat, mid_inv = normalize(hidden_ref[...])
    mid_norm_ref[...] = (mid_hat * gain_ref[...]).astype(BF16)
    pre_act = dot(mid_norm_ref[...], up_ref[...], NT) + b_up_ref[...]
    below = 0.5 * (1.0 + lax.erf(pre_act * 0.5**0.5))
    activated_ref[...] = (pre_act * below).astype(BF16)
    slope = below + pre_act * (jnp.exp(-0.5 * pre_act * pre_act) * (2.0 * jnp.pi) ** -0.5)
    grad_act = dot(cotangent_ref[...].astype(BF16), down_ref[...], NT)
    grad_pre_ref[...] = (grad_act * slope).astype(BF16)
    sums_ref[1:2, :] = jnp.sum(grad_pre_ref[...].astype(F32), axis=0, keepdims=True)
    grad_mid = dot(grad_pre_ref[...], up_ref[...])
    mid_hat, mid_inv = normalize(hidden_ref[...])
    back, gain_grad = norm_back(grad_mid, mid_hat, mid_inv, gain_ref[...])
    sums_ref[0:1, :] = gain_grad[None]
    grad_hidden_ref[...] = cotangent_ref[...] + back
    sums_ref[2:3, :] = jnp.sum(grad_hidden_ref[...], axis=0, keepdims=True)
    sums_ref[3:4, :] = jnp.sum(cotangent_ref[...], axis=0, keepdims=True)
    grad_attn_ref[...] = grad_hidden_ref[...].astype(BF16)
    width = attended_ref.shape[1]
    grad_att_ref[:, :width] = dot(grad_attn_ref[...], out_ref[...], NT).astype(BF16)
    lane = lax.broadcasted_iota(jnp.int32, (attended_ref.shape[0], LANES), 1)
    packed = jnp.zeros(lane.shape, F32)
    heads = width // HEAD_DIM
    for head, (base, low, high) in enumerate(windows(attended_ref.shape[1])):
        product = attended_ref[:, base : base + 2 * LANES].astype(F32) * grad_att_ref[
            :, base : base + 2 * LANES
        ].astype(F32)
        product = jnp.where(own_columns(product.shape, low, high), product, 0.0)
        rest = jnp.sum(product, 1, keepdims=True)
        for part in range(3):
            rounded = rest.astype(BF16).astype(F32)
            packed = jnp.where(lane == part * heads + head, rounded, packed)
            rest = rest - rounded
    grad_att_ref[:, width:] = packed.astype(BF16)
    result_ref[...] = hidden_ref[...] + dot(activated_ref[...], down_ref[...]) + b_down_ref[...]


def lse_kernel(query_ref, key_ref, lat_seg_ref, byte_seg_ref, lse_ref):
    allowed = byte_seg_ref[0] == lat_seg_ref[0]
    for head, (base, low, high) in enumerate(windows(query_ref.shape[3])):
        query = lines_of(query_ref, base)
        query = jnp.where(own_columns(query.shape, low, high), query, 0)
        key = key_ref[0, :, base : base + 2 * LANES]
        scores = jnp.where(allowed, dot(key, query, NT), NEG)
        peak = jnp.max(scores, 0, keepdims=True)
        total = jnp.sum(jnp.exp(scores - peak), 0, keepdims=True)
        lse_ref[0, head : head + 1, :] = peak + jnp.log(total)


class Tiles:
    def __init__(self, ref):
        self.ref = ref
        self.held = {}

    def add(self, base, window):
        for part in range(2):
            tile = base + part * LANES
            piece = window[:, part * LANES : (part + 1) * LANES]
            self.held[tile] = self.held[tile] + piece if tile in self.held else piece
        for tile in [t for t in self.held if t < base]:
            self.store(tile)

    def store(self, tile):
        done = self.held.pop(tile).astype(self.ref.dtype)
        if len(self.ref.shape) == 4:
            self.ref[:, 0, :, tile : tile + LANES] = done.reshape(
                self.ref.shape[0], self.ref.shape[2], LANES
            )
        else:
            self.ref[0, :, tile : tile + LANES] = done

    def finish(self):
        for tile in list(self.held):
            self.store(tile)


def attend_kernel(own_lat, query_ref, key_ref, value_ref, lat_seg_ref, byte_seg_ref, *refs):
    part_refs, (out_ref, lse_ref) = refs[:-2], refs[-2:]
    parts = [part_refs[0][0]]
    for step, ref in enumerate(part_refs[1:], 1):
        parts.append(pltpu.roll(ref[0], step * own_lat, 1))
    peak = functools.reduce(jnp.maximum, parts)
    lse_ref[0] = peak + jnp.log(sum(jnp.exp(part - peak) for part in parts))
    allowed = byte_seg_ref[0] == lat_seg_ref[0]
    tiles = Tiles(out_ref)
    for head, (base, low, high) in enumerate(windows(query_ref.shape[3])):
        query = lines_of(query_ref, base)
        mine = own_columns(query.shape, low, high)
        query = jnp.where(mine, query, 0)
        key = key_ref[0, :, base : base + 2 * LANES]
        value = value_ref[0, :, base : base + 2 * LANES]
        scores = jnp.where(allowed, dot(key, query, NT), NEG)
        probs = jnp.exp(scores - lse_ref[0, head : head + 1, :]).astype(BF16)
        tiles.add(base, jnp.where(mine, dot(probs, value, TN), 0.0))
    tiles.finish()


def attend_back_kernel(
    query_ref,
    key_ref,
    value_ref,
    lat_seg_ref,
    byte_seg_ref,
    lse_ref,
    *refs,
):
    grad_refs, (grad_query_ref, grad_key_ref, grad_value_ref) = refs[:-3], refs[-3:]
    width = query_ref.shape[3]
    heads = width // HEAD_DIM
    delta = jnp.concatenate([ref[0, :, width:] for ref in grad_refs]).astype(F32).T
    delta = delta[:heads] + (delta[heads : 2 * heads] + delta[2 * heads : 3 * heads])
    allowed = byte_seg_ref[0] == lat_seg_ref[0]
    query_tiles, key_tiles, value_tiles = (
        Tiles(grad_query_ref),
        Tiles(grad_key_ref),
        Tiles(grad_value_ref),
    )
    for head, (base, low, high) in enumerate(windows(query_ref.shape[3])):
        query = lines_of(query_ref, base)
        mine = own_columns(query.shape, low, high)
        query = jnp.where(mine, query, 0)
        grad = jnp.concatenate([ref[0, :, base : base + 2 * LANES] for ref in grad_refs])
        grad = jnp.where(mine, grad, 0)
        key = key_ref[0, :, base : base + 2 * LANES]
        value = value_ref[0, :, base : base + 2 * LANES]
        scores = jnp.where(allowed, dot(key, query, NT), NEG)
        probs = jnp.exp(scores - lse_ref[0, head : head + 1, :])
        grad_probs = dot(value, grad, NT)
        grad_scores = (probs * (grad_probs - delta[head : head + 1, :])).astype(BF16)
        value_tiles.add(base, dot(probs.astype(BF16), grad))
        key_tiles.add(base, dot(grad_scores, query))
        query_tiles.add(base, jnp.where(mine, dot(grad_scores, key, TN), 0.0))
    query_tiles.finish()
    key_tiles.finish()
    value_tiles.finish()


def row_call(kernel, name, args, outs, flops):
    def spec(shape):
        if len(shape) == 1:
            return pl.BlockSpec(memory_space=pltpu.SMEM)
        if len(shape) == 4:
            return pl.BlockSpec((shape[0], 1, *shape[2:]), lambda row: (0, row, 0, 0))
        return pl.BlockSpec((1, *shape[1:]), lambda row: (row, 0, 0))

    moved = sum(a.size * a.dtype.itemsize for a in args)
    return pl.pallas_call(
        kernel,
        grid=(outs[-1].shape[0],),
        in_specs=[spec(a.shape) for a in args],
        out_specs=[spec(o.shape) for o in outs],
        out_shape=outs,
        name=name,
        cost_estimate=pl.CostEstimate(flops=2 * flops, bytes_accessed=2 * moved, transcendentals=0),
        compiler_params=pltpu.CompilerParams(vmem_limit_bytes=48 * 1024 * 1024),
    )(*args)


def block_call(kernel, name, lines, args, outs, flops, scratch=()):
    def spec(shape, cut):
        block = (lines if cut else shape[0], shape[1])
        return pl.BlockSpec(block, (lambda i: (i, 0)) if cut else (lambda i: (0, 0)))

    moved = sum(a.size * a.dtype.itemsize for a, _ in args)
    return pl.pallas_call(
        kernel,
        grid=(args[0][0].shape[0] // lines,),
        in_specs=[spec(a.shape, cut) for a, cut in args],
        out_specs=[spec(o.shape, cut) for o, cut in outs],
        out_shape=[o for o, _ in outs],
        scratch_shapes=list(scratch),
        name=name,
        cost_estimate=pl.CostEstimate(flops=2 * flops, bytes_accessed=2 * moved, transcendentals=0),
        compiler_params=pltpu.CompilerParams(vmem_limit_bytes=56 * 1024 * 1024),
    )(*[a for a, _ in args])


def ring(size, step=1):
    return [(i, (i + step) % size) for i in range(size)]


def add(first, *others):
    total = first.astype(F32)
    for other in others:
        total = total + other.astype(F32)
    return total.astype(first.dtype)


def panels(widths):
    return [(m, p) for m, width in enumerate(widths) for p in range(width // (2 * LANES))]


def join_kernel(widths, core_ref, mine_ref, other_ref, *out_refs):
    chips, part = mine_ref.shape[0], mine_ref.shape[3]

    def copy(sides):
        for number, (m, p) in enumerate(panels(widths)):
            for side, ref in enumerate(sides):
                at = side * widths[m] // 2 + p * LANES
                for chip in range(chips):
                    out_refs[m][chip * part : (chip + 1) * part, at : at + LANES] = ref[
                        chip, 0, number
                    ].astype(out_refs[m].dtype)

    @pl.when(core_ref[0] == 0)
    def _():
        copy((mine_ref, other_ref))

    @pl.when(core_ref[0] == 1)
    def _():
        copy((other_ref, mine_ref))


def join_own_kernel(widths, where_ref, *refs):
    count = len(widths)
    own_refs, (mine_ref, other_ref), out_refs = refs[:count], refs[count : count + 2], refs[count + 2 :]
    first = pl.program_id(0) == 0

    @pl.when(first)
    def _():
        for own_ref, out_ref in zip(own_refs, out_refs):
            out_ref[...] = own_ref[...]

    @pl.when(jnp.logical_not(first))
    def _():
        join_kernel(widths, where_ref, mine_ref, other_ref, *out_refs)


def grads_kernel(widths, core_ref, *refs):
    count = len(widths)
    (kept_ref, sent_ref), work_refs = refs[2 * count : 2 * count + 2], refs[2 * count + 2 :]
    chips, blocks, _, part, _ = kept_ref.shape
    for m in range(count):
        work_refs[m][...] = dot(refs[m][...], refs[count + m][...], TN).astype(BF16)

    def copy(sides):
        for number, (m, p) in enumerate(panels(widths)):
            for side, ref in enumerate(sides):
                at = side * widths[m] // 2 + p * LANES
                for block in range(blocks):
                    for chip in range(chips):
                        start = (block * chips + chip) * part
                        ref[chip, block, number] = work_refs[m][
                            start : start + part, at : at + LANES
                        ]

    @pl.when(core_ref[0] == 0)
    def _():
        copy((kept_ref, sent_ref))

    @pl.when(core_ref[0] == 1)
    def _():
        copy((sent_ref, kept_ref))


def add_kernel(a_ref, b_ref, *out_refs):
    first = 0
    for out_ref in out_refs:
        group = slice(first, first + out_ref.shape[2])
        total = a_ref[:, :, group].astype(F32) + b_ref[:, :, group].astype(F32)
        out_ref[...] = total.astype(out_ref.dtype)
        first += out_ref.shape[2]


def split_kernel(widths, core_ref, *refs):
    in_refs, (kept_ref, sent_ref) = refs[:-2], refs[-2:]
    chips, _, _, part, _ = kept_ref.shape

    def copy(sides):
        for number, (m, p) in enumerate(panels(widths)):
            for side, ref in enumerate(sides):
                at = side * widths[m] // 2 + p * LANES
                for chip in range(chips):
                    ref[chip, 0, number] = in_refs[m][
                        chip * part : (chip + 1) * part, at : at + LANES
                    ]

    @pl.when(core_ref[0] == 0)
    def _():
        copy((kept_ref, sent_ref))

    @pl.when(core_ref[0] == 1)
    def _():
        copy((sent_ref, kept_ref))


def packed_spec(shape):
    chips, _, count, part, lanes = shape
    return pl.BlockSpec((chips, 1, count, part, lanes), lambda z: (0, z, 0, 0, 0))


def matrix_spec(lines, width):
    return pl.BlockSpec((lines, width), lambda z: (z, 0))


def join(core, mine, other, widths, kinds):
    chips, blocks, _, part, _ = mine.shape
    lines = chips * part
    return pl.pallas_call(
        functools.partial(join_kernel, widths),
        grid=(blocks,),
        in_specs=[
            pl.BlockSpec(memory_space=pltpu.SMEM),
            packed_spec(mine.shape),
            packed_spec(mine.shape),
        ],
        out_specs=[matrix_spec(lines, width) for width in widths],
        out_shape=[
            jax.ShapeDtypeStruct((blocks * lines, width), kind)
            for width, kind in zip(widths, kinds)
        ],
        name="join",
        cost_estimate=pl.CostEstimate(
            flops=0, bytes_accessed=mine.size, transcendentals=0
        ),
        compiler_params=pltpu.CompilerParams(vmem_limit_bytes=48 * 1024 * 1024),
    )(core, mine, other)


def join_own(where, own, mine, other, widths, total):
    chips, blocks, count, part, _ = mine.shape
    lines = chips * part

    def packed(r, where_ref):
        return (0, jnp.maximum(r, 1) - 1, 0, 0, 0)

    return pl.pallas_call(
        functools.partial(join_own_kernel, widths),
        grid_spec=pltpu.PrefetchScalarGridSpec(
            num_scalar_prefetch=1,
            grid=(blocks + 1,),
            in_specs=[pl.BlockSpec((lines, width), lambda r, where_ref: (0, 0)) for width in widths]
            + [pl.BlockSpec((chips, 1, count, part, LANES), packed)] * 2,
            out_specs=[
                pl.BlockSpec(
                    (lines, width),
                    lambda r, where_ref: (lax.rem(where_ref[1] + (total - r), total), 0),
                )
                for width in widths
            ],
        ),
        out_shape=[jax.ShapeDtypeStruct((total * lines, width), mine.dtype) for width in widths],
        name="join_own",
        cost_estimate=pl.CostEstimate(flops=0, bytes_accessed=mine.size, transcendentals=0),
        compiler_params=pltpu.CompilerParams(vmem_limit_bytes=48 * 1024 * 1024),
    )(where, *own, mine, other)


def split(core, matrices, chips, lines):
    widths = [m.shape[1] for m in matrices]
    blocks = matrices[0].shape[0] // lines
    shape = (chips, blocks, len(panels(widths)), lines // chips, LANES)
    packed = jax.ShapeDtypeStruct(shape, BF16)
    return pl.pallas_call(
        functools.partial(split_kernel, widths),
        grid=(blocks,),
        in_specs=[pl.BlockSpec(memory_space=pltpu.SMEM)]
        + [matrix_spec(lines, width) for width in widths],
        out_specs=[packed_spec(shape)] * 2,
        out_shape=[packed] * 2,
        name="split",
        cost_estimate=pl.CostEstimate(
            flops=0, bytes_accessed=sum(m.size for m in matrices) // 2, transcendentals=0
        ),
        compiler_params=pltpu.CompilerParams(vmem_limit_bytes=48 * 1024 * 1024),
    )(core, *matrices)


def add_packed(a, b):
    middle = (a.shape[2] + 1) // 2
    shapes = [a.shape[:2] + (count,) + a.shape[3:] for count in (middle, a.shape[2] - middle)]
    return pl.pallas_call(
        add_kernel,
        grid=(a.shape[1],),
        in_specs=[packed_spec(a.shape)] * 2,
        out_specs=[packed_spec(shape) for shape in shapes],
        out_shape=[jax.ShapeDtypeStruct(shape, a.dtype) for shape in shapes],
        name="add_packed",
        cost_estimate=pl.CostEstimate(flops=0, bytes_accessed=a.size // 2, transcendentals=0),
    )(a, b)


def grads(core, pairs, chips, lines, columns):
    widths = [rhs.shape[1] for _, rhs in pairs]
    steps = pairs[0][0].shape[1] // columns
    blocks = columns // lines
    shape = (chips, blocks * steps, len(panels(widths)), lines // chips, LANES)
    packed = jax.ShapeDtypeStruct(shape, BF16)
    block = (chips, blocks) + shape[2:]
    return pl.pallas_call(
        functools.partial(grads_kernel, widths),
        grid=(steps,),
        in_specs=[pl.BlockSpec(memory_space=pltpu.SMEM)]
        + [pl.BlockSpec((lhs.shape[0], columns), lambda i: (0, i)) for lhs, _ in pairs]
        + [pl.BlockSpec(rhs.shape, lambda i: (0, 0)) for _, rhs in pairs],
        out_specs=[pl.BlockSpec(block, lambda i: (0, i, 0, 0, 0))] * 2,
        out_shape=[packed] * 2,
        scratch_shapes=[pltpu.VMEM((columns, width), BF16) for width in widths],
        name="grads",
        cost_estimate=pl.CostEstimate(
            flops=sum(lhs.size * rhs.shape[1] for lhs, rhs in pairs) // 4,
            bytes_accessed=sum(lhs.size + rhs.size for lhs, rhs in pairs) // 4,
            transcendentals=0,
        ),
        compiler_params=pltpu.CompilerParams(vmem_limit_bytes=56 * 1024 * 1024),
    )(core, *[lhs for lhs, _ in pairs], *[rhs for _, rhs in pairs])


def after(x, *earlier):
    return lax.optimization_barrier((x, *earlier))[0]


def three_parts(x, shape):
    parts = []
    for _ in range(3):
        part = lax.reduce_precision(x, 8, 7)
        parts.append(part.astype(BF16))
        x = x - part
    parts = jnp.concatenate(parts)
    size = shape[0] * shape[1]
    return jnp.pad(parts, (0, size - parts.size)).reshape(shape)


def from_three_parts(x, size):
    parts = x.reshape(x.shape[0], -1)[:, : 3 * size].astype(F32).reshape(-1, 3, size)
    return (parts[:, 0] + (parts[:, 1] + parts[:, 2])).reshape(-1)


def pick(x, index, axis):
    return jnp.take(x, index, axis=axis, mode="clip")


class Mesh:
    def __init__(self, dp, mp):
        self.dp, self.mp = dp, mp
        self.dp_index = lax.axis_index("dp")
        self.mp_index = lax.axis_index("mp")
        self.core = self.dp_index % 2

    def cut(self, lines):
        chips = 1
        while 2 * chips <= self.dp // 2 and lines % (32 * chips) == 0:
            chips *= 2
        return chips, [2 * k for k in (1 << b for b in range(8)) if chips <= k < self.dp // 2]

    def swap(self, x, bit):
        return lax.ppermute(x, "dp", [(i, i ^ bit) for i in range(self.dp)])

    def shift(self, x, step):
        return lax.ppermute(x, "mp", ring(self.mp, step))

    def ring_gather(self, x):
        blocks = [x]
        for _ in range(self.mp - 1):
            blocks.append(self.shift(blocks[-1], 1))
        return blocks

    def ring_scatter(self, parts):
        total = parts[1] if self.mp > 1 else parts[0]
        for step in range(2, self.mp + 1):
            total = add(self.shift(total, 1), parts[step % self.mp])
        return total

    def chip_groups(self, chips):
        return [
            [2 * (chip + chips * rest) + core for chip in range(chips)]
            for rest in range(self.dp // 2 // chips)
            for core in range(2)
        ]

    def slice_of(self, shards):
        chips, _ = self.cut(shards[0].shape[0])
        part = shards[0].shape[0] // chips
        chip = self.dp_index // 2 % chips
        return jnp.concatenate(
            [
                lax.dynamic_slice(
                    shard,
                    (chip * part, self.core * (shard.shape[1] // 2)),
                    (part, shard.shape[1] // 2),
                )
                .reshape(part, -1, LANES)
                .transpose(1, 0, 2)
                for shard in shards
            ]
        )

    def gather_chips(self, x, lines):
        chips, _ = self.cut(lines)
        return lax.all_gather(x, "dp", axis=0, axis_index_groups=self.chip_groups(chips))

    def both_cores(self, own, mine, other):
        where = jnp.stack([self.core, self.mp_index])
        widths = [shard.shape[1] for shard in own]
        return join_own(where, own, mine, other, widths, self.mp)

    def split_core(self, pairs, lines):
        chips, _ = self.cut(lines)
        columns = self.mp * lines // 2
        return grads(self.core[None], pairs, chips, lines, columns)

    def scatter_chips(self, total, lines):
        chips, _ = self.cut(lines)
        return lax.psum_scatter(
            total, "dp", scatter_dimension=0, axis_index_groups=self.chip_groups(chips)
        )

    def link_pieces(self, groups, lines):
        chips, _ = self.cut(lines)
        bits = [1 << b for b in range(chips.bit_length() - 1)]
        return [
            (piece.reshape((2,) * len(bits) + piece.shape[1:]), order, sorted(bits, reverse=True))
            for order, piece in zip((bits, bits[::-1]), groups)
        ]

    def link_step(self, pieces, *earlier):
        out = []
        for piece, order, left in pieces:
            mine = self.dp_index // (2 * order[0]) % 2
            axis = left.index(order[0])
            if earlier:
                piece = after(piece, *earlier)
            sent = lax.dynamic_index_in_dim(piece, 1 - mine, axis, False)
            kept = lax.dynamic_index_in_dim(piece, mine, axis, False)
            piece = add(kept, self.swap(sent, 2 * order[0]))
            out.append((piece, order[1:], [bit for bit in left if bit != order[0]]))
        return out

    def arrays(self, pieces):
        return [piece for piece, _, _ in pieces]

    def with_arrays(self, pieces, arrays):
        return [(array, *piece[1:]) for array, piece in zip(arrays, pieces)]

    def blocks_back(self, total, lines):
        _, rest = self.cut(lines)
        for bit in rest:
            total = add(total, self.swap(total, bit))
        return [
            lax.dynamic_index_in_dim(total, (self.mp_index + self.mp - r) % self.mp, 0, False)
            for r in range(self.mp)
        ]

    def sum_blocks(self, total, lines):
        _, rest = self.cut(lines)
        for bit in rest:
            total = add(total, self.swap(total, bit))
        blocks = [
            lax.dynamic_index_in_dim(total, (self.mp_index + step) % self.mp, 0, False)
            for step in range(self.mp)
        ]
        return add(blocks[0], *[self.shift(blocks[step], step) for step in range(1, self.mp)])

    def share(self, total, lines, small=False):
        chips, rest = self.cut(lines)
        slices = [total] + [self.swap(total, 2 * k) for k in range(1, chips)]
        if small:
            panel = add(*[piece[-1] for piece in slices])
            for bit in rest:
                panel = add(panel, self.swap(panel, bit))
            slices = [jnp.concatenate([piece[:-1], panel[None]]) for piece in slices]
        chip = self.dp_index // 2 % chips
        return pick(jnp.stack(slices), chip ^ jnp.arange(chips), 0)[:, None]

    def turned(self, x, axis):
        blocks = x.reshape(x.shape[:axis] + (self.mp, -1) + x.shape[axis + 1 :])
        index = (self.mp_index - jnp.arange(self.mp)) % self.mp
        return pick(blocks, index, axis).reshape(x.shape)


def shards(
    dp,
    mp,
    byte_in,
    latents,
    cotangent,
    byte_gain,
    latent_gain,
    mlp_gain,
    w_query,
    w_key,
    w_value,
    w_out,
    b_out,
    w_up,
    b_up,
    w_down,
    b_down,
    byte_seg,
    byte_pad,
    latent_seg,
):
    score_scale = HEAD_DIM ** (-0.5)
    rows, byte_len, byte_width = byte_in.shape
    own_lat, lat_width = latents.shape[1:]
    lat_len = own_lat * mp
    own_lines = rows * own_lat
    heads = w_query.shape[1] * mp // HEAD_DIM
    net = Mesh(dp, mp)
    mp_index = net.mp_index
    shape = jax.ShapeDtypeStruct
    lines = w_query.shape[1]
    head_widths = [lat_width, byte_width, byte_width]
    feed_widths = [lat_width] * 3

    head_own = [w_query.T, w_key.T, w_value.T]
    feed_own = [w_out, w_up.T, w_down]
    head_blocks = net.ring_gather(net.slice_of(head_own))[1:]
    latents = latents.reshape(own_lines, lat_width)
    cotangent = cotangent.reshape(own_lines, lat_width)
    byte_in = byte_in.reshape(rows * byte_len, byte_width)
    lat_hat, lat_inv = normalize(latents)
    lat_norm = (lat_hat * latent_gain).astype(BF16).reshape(rows, own_lat, lat_width)
    (byte_norm,) = block_call(
        byte_norm_kernel,
        "byte_norm",
        byte_len,
        [(byte_in, True), (byte_gain[None], False)],
        [(shape(byte_in.shape, BF16), True)],
        10 * byte_in.size,
    )
    feed_slice = net.slice_of(feed_own)
    feed_slice = jnp.concatenate([feed_slice, three_parts(b_up, feed_slice.shape[1:])[None]])
    flat = [v[None] for v in (mlp_gain, b_out, b_down)]
    head_blocks[-1], byte_norm, lat_norm, feed_slice, flat = lax.optimization_barrier(
        (head_blocks[-1], byte_norm, lat_norm, feed_slice, flat)
    )
    head_slices = net.gather_chips(jnp.stack(head_blocks), lines)
    lat_blocks = net.ring_gather(lat_norm)
    feed_blocks = [feed_slice, net.shift(after(feed_slice, lat_blocks[-1]), 1)]
    head_slices = after(head_slices, lat_blocks[-1])
    query_t, key_t, value_t = net.both_cores(head_own, head_slices, net.swap(head_slices, 1))

    real_seg = jnp.where(byte_pad == 1, byte_seg, -1)
    real_seg = lax.dynamic_slice_in_dim(real_seg, mp_index * byte_len, byte_len, 1)
    byte_col = real_seg[:, :, None]
    lat_row = net.turned(latent_seg, 1)[:, None, :]
    unit = 2 * rows * lat_len * byte_len * heads * 2 * LANES

    key_t, feed_blocks[1] = lax.optimization_barrier((key_t, feed_blocks[1]))
    feed_blocks.append(net.shift(feed_blocks[1], 1))
    keys = dot(byte_norm, key_t, NT).astype(BF16).reshape(rows, byte_len, lat_width)
    lat_all = jnp.stack(lat_blocks)
    lat_flat = after(lat_all.reshape(rows * lat_len, lat_width), keys)
    queries = (dot(lat_flat, query_t, NT) * score_scale).astype(BF16).reshape(lat_all.shape)
    (lse_part,) = row_call(
        lse_kernel,
        "lse",
        [queries, keys, lat_row, byte_col],
        [shape((rows, heads, lat_len), F32)],
        unit,
    )
    lse_part, feed_blocks[2] = lax.optimization_barrier((lse_part, feed_blocks[2]))
    for _ in range(3, mp):
        feed_blocks.append(net.shift(feed_blocks[-1], 1))
    lse_parts = [lse_part] + [net.shift(lse_part, step) for step in range(1, mp)]
    values = dot(after(byte_norm, lse_part), value_t, NT).astype(BF16)
    values = values.reshape(rows, byte_len, lat_width)
    values, feed_blocks[-1] = lax.optimization_barrier((values, feed_blocks[-1]))
    feed_slices = net.gather_chips(jnp.stack([block[:-1] for block in feed_blocks[1:]]), lines)
    b_up_all = from_three_parts(jnp.stack([block[-1] for block in feed_blocks]), b_up.shape[0])
    b_up_all = net.turned(b_up_all, 0)[None]
    lat_shape = shape(lat_all.shape, BF16)
    parts, lse = row_call(
        functools.partial(attend_kernel, own_lat),
        "attend",
        [queries, keys, values, lat_row, byte_col] + lse_parts,
        [lat_shape, shape((rows, heads, lat_len), F32)],
        2 * unit,
    )
    attended = parts[1]
    for step in range(2, mp + 1):
        moved = net.shift(attended, 1)
        if step == 2:
            moved, b_up_all = lax.optimization_barrier((moved, b_up_all))
        if step == mp - 1:
            feed_slices = after(feed_slices, moved)
            out_w, up_t, down_w = net.both_cores(
                feed_own, feed_slices, net.swap(feed_slices, 1)
            )
        if step == mp:
            moved, out_w = lax.optimization_barrier((moved, out_w))
        attended = add(moved, parts[step % mp])
    attended = attended.reshape(own_lines, lat_width)

    whole = shape((own_lines, lat_width), BF16)
    wide = shape((own_lines, lat_width), F32)
    (
        result,
        mid_norm,
        activated,
        grad_pre,
        grad_hidden,
        grad_attn,
        grad_att,
        feed_vectors,
    ) = block_call(
        feed_kernel,
        "feed",
        own_lines,
        [(latents, True), (cotangent, True)]
        + [(v, False) for v in (flat[0], flat[1], b_up_all, flat[2])]
        + [(w, False) for w in (out_w, up_t, down_w)]
        + [(attended, True)],
        [(wide, True), (whole, True), (whole, True), (whole, True), (wide, True), (whole, True)]
        + [(shape((own_lines, lat_width + LANES), BF16), True)]
        + [(shape((4, lat_width), F32), False)],
        8 * own_lines * lat_width * lat_width,
        [pltpu.VMEM((own_lines, lat_width), F32)],
    )

    grads = [grad_att.reshape(rows, own_lat, lat_width + LANES)]
    block = net.shift(grads[0], 1)
    feed_kept, feed_sent = net.split_core(
        [(activated, cotangent.astype(BF16)), (grad_pre, mid_norm), (attended, grad_attn)], lines
    )
    block, feed_kept, feed_sent = lax.optimization_barrier((block, feed_kept, feed_sent))
    grads.append(block)
    feed_sums = add_packed(feed_kept, net.swap(feed_sent, 1))
    if mp > 2:
        block = net.shift(grads[-1], 1)
        block = after(block, feed_sums[0])
        grads.append(block)
    for _ in range(3, mp):
        grads.append(net.shift(grads[-1], 1))
    feed_sums = net.link_pieces(feed_sums, lines)
    if feed_sums[0][1]:
        feed_sums = net.link_step(feed_sums)

    back, grad_keys, grad_values = row_call(
        attend_back_kernel,
        "attend_back",
        [queries, keys, values, lat_row, byte_col, lse] + grads,
        [lat_shape] + [shape((rows, byte_len, lat_width), BF16)] * 2,
        5 * unit,
    )
    grad_keys = grad_keys.reshape(-1, lat_width)
    grad_values = grad_values.reshape(-1, lat_width)
    total = back[1]
    moved = net.shift(total, 1)
    products = [dot(grad, byte_norm, TN).astype(BF16) for grad in (grad_keys, grad_values)]
    while feed_sums[0][1]:
        feed_sums = net.link_step(feed_sums)
    moved, products, feed_half = lax.optimization_barrier(
        (moved, products, net.arrays(feed_sums))
    )
    feed_parts = net.blocks_back(jnp.concatenate(feed_half, 1), lines)
    feed_total = feed_parts[1]
    total = add(moved, back[2 % mp])
    back_flat = after(back.reshape(-1, lat_width), total, feed_total)
    products.insert(0, dot(back_flat, lat_flat, TN).astype(BF16))
    kept, sent = split(net.core[None], products, net.cut(lines)[0], lines)
    head_sums = add_packed(kept, net.swap(sent, 1))
    added = head_sums[0]
    feed_moved, added = lax.optimization_barrier((net.shift(feed_total, 1), added))
    feed_total = add(feed_moved, feed_parts[2 % mp])
    total = after(total, added)
    head_sums = net.link_pieces(head_sums, lines)
    if head_sums[0][1]:
        head_sums = net.link_step(head_sums)
    grad_bytes, grad_byte_gain = block_call(
        byte_back_kernel,
        "byte_back",
        byte_len,
        [(byte_in, True), (byte_gain[None], False), (key_t, False), (value_t, False)]
        + [(after(grad_keys, added), True), (grad_values, True)],
        [(shape(byte_in.shape, F32), True), (shape((1, byte_width), F32), False)],
        4 * rows * byte_len * lat_width * byte_width,
    )
    for step in range(3, mp + 1):
        if step == 4:
            total = after(total, grad_bytes)
        total = add(net.shift(total, 1), back[step % mp])
    grad_bytes, done = lax.optimization_barrier((grad_bytes, net.arrays(head_sums)))
    head_sums = net.with_arrays(head_sums, done)
    while head_sums[0][1]:
        head_sums = net.link_step(head_sums)
    for step in range(3, mp + 1):
        if step == mp:
            feed_total = after(feed_total, *net.arrays(head_sums))
        feed_total = add(net.shift(feed_total, 1), feed_parts[step % mp])
    feed_mine = net.share(feed_total, lines)
    grad_lat_norm = score_scale * dot(total.reshape(own_lines, lat_width), query_t)
    grad_lat_back, grad_latent_gain = norm_back(grad_lat_norm, lat_hat, lat_inv, latent_gain)
    grad_latents = grad_hidden + grad_lat_back
    small = jnp.concatenate([grad_byte_gain[0], grad_latent_gain, feed_vectors.reshape(-1)])
    head_sums = jnp.concatenate(net.arrays(head_sums), 1)
    head_total = net.sum_blocks(head_sums, lines)
    panel = small.astype(BF16)
    panel = jnp.pad(panel, (0, head_total[0].size - panel.size)).reshape(1, -1, LANES)
    panel = add(panel, *[net.shift(panel, step) for step in range(1, mp)])
    head_total, panel, feed_mine = lax.optimization_barrier((head_total, panel, feed_mine))
    head_mine = net.share(jnp.concatenate([head_total, panel]), lines, True)
    feed_other, head_other = net.swap(feed_mine, 1), net.swap(head_mine, 1)
    feed_grads = join(net.core[None], feed_mine, feed_other, feed_widths, [F32, BF16, F32])
    head_grads = join(net.core[None], head_mine, head_other, head_widths, [BF16] * 3)
    sums = head_mine[0, 0, -1].astype(F32) + head_other[0, 0, -1].astype(F32)
    sums = sums.reshape(-1)[: small.size]
    sums = [sums[:byte_width]] + list(sums[byte_width:].reshape(5, lat_width))
    own_units = b_up.shape[0]
    return (
        result.reshape(rows, own_lat, lat_width),
        grad_bytes.reshape(rows, byte_len, byte_width),
        grad_latents.reshape(rows, own_lat, lat_width),
        sums[0],
        sums[1],
        sums[2],
        head_grads[0].astype(F32).T * score_scale,
        head_grads[1].astype(F32).T,
        head_grads[2].astype(F32).T,
        feed_grads[2],
        sums[4],
        feed_grads[1].astype(F32).T,
        lax.dynamic_slice_in_dim(sums[3], mp_index * own_units, own_units, 0),
        feed_grads[0],
        sums[5],
    )


def solution(mesh):
    by_row = P("dp", "mp", None)
    columns, lines = P(None, "mp"), P("mp", None)
    return jax.shard_map(
        functools.partial(shards, mesh.shape["dp"], mesh.shape["mp"]),
        mesh=mesh,
        in_specs=(
            by_row,
            by_row,
            by_row,
            P(),
            P(),
            P(),
            columns,
            columns,
            columns,
            lines,
            P(),
            columns,
            P("mp"),
            lines,
            P(),
            P("dp", None),
            P("dp", None),
            P("dp", None),
        ),
        out_specs=(
            by_row,
            by_row,
            by_row,
            P(),
            P(),
            P(),
            columns,
            columns,
            columns,
            lines,
            P(),
            columns,
            P("mp"),
            lines,
            P(),
        ),
        check_vma=False,
    )
```
